128 devices in a mesh: strip: 16 (over y_hi, x, core), mode: 8 (over z, y_lo).
Axes of the slice: x: 4, y: 4 (y_hi: 2, y_lo: 2; y = y_hi * 2 + y_lo), z: 4, core: 2. Of those that a mesh axis runs over, the one named last changes fastest.
Arguments:
- object_field: float32 [2, 4096, 384], P(None, 'strip'), may hold values from -5 to 5
- probe_modes: float32 [2, 16, 256, 256], P(None, 'mode'), may hold values from -2.5 to 2.5
- measured: float32 [16, 4, 256, 256], P('strip'), may hold values from 0.1 to 27
- positions: int32 [16, 4, 2], P('strip'), may hold values from 0 to 128, as said below
Outputs:
- object_new: float32 [2, 4096, 384], P(None, 'strip')
The draws below stay inside these ranges and needn't reach their ends.
Inputs may be any that keep to these rules, and one draw needn't show every extreme that they name: positions[s,k,0] is the first row of window k within strip s and positions[s,k,1] its first column; the windows of every strip form a two by two raster with small offsets: windows 0 and 3 start at row 128, windows 1 and 2 at row 0, window 1 at column 128, window 3 at most 16 columns left of it, windows 0 and 2 at columns 0 to 16.
All inputs are finite; a program needn't handle non-finite values.
Results may differ from the reference program's by a relative error of at most 0.0001.
Values sent between devices are 32-bit elements; how exact they have to be, the bound alone decides.
No kernel may reach another device: no remote copies, remote signals or barrier semaphores. Data moves between devices by JAX's collectives and lax.ppermute only.
A program may use at most 128 MiB of HBM per device.

```python
import jax
import jax.numpy as jnp
from jax import lax

WINDOW_SIDE = 256
MODES = 16
SR = 256
W = 384
HALO = 128
POS = 4
ITERS = 3
STRIPS = 16
ROWS = 4096


def draw_positions(key, part):
    jitter_key = jax.random.fold_in(key, 7)
    row_most = SR + HALO - WINDOW_SIDE
    col_most = W - WINDOW_SIDE
    jitter = max(WINDOW_SIDE // 16, 1)
    offsets = jax.random.randint(jitter_key, (STRIPS, 3), 0, jitter + 1, dtype=jnp.int32)
    zeros_col = jnp.zeros((STRIPS,), jnp.int32)
    rows_drawn = jnp.stack([zeros_col + row_most, zeros_col, zeros_col, zeros_col + row_most], axis=1)
    cols_drawn = jnp.stack([offsets[:, 0], zeros_col + col_most, offsets[:, 1], col_most - offsets[:, 2]], axis=1)
    cols_drawn = jnp.clip(cols_drawn, 0, col_most)
    return jnp.stack([rows_drawn, cols_drawn], axis=-1).astype(jnp.int32)


def draw_measured(key, part):
    base_key, window_key = jax.random.split(jax.random.fold_in(key, 11))
    shape_full = (STRIPS, POS, WINDOW_SIDE, WINDOW_SIDE)
    base_values = jnp.exp(jax.random.uniform(base_key, shape_full, jnp.float32, jnp.log(0.1), jnp.log(3.0)))
    spread = jnp.exp(jax.random.uniform(window_key, (STRIPS, POS, 1, 1), jnp.float32, 0.0, jnp.log(3.0)))
    strip_ramp = 1.0 + 2.0 * jnp.arange(STRIPS, dtype=jnp.float32) / max(STRIPS - 1, 1)
    return base_values * spread * strip_ramp[:, None, None, None]


def levels(rng, extent, shards, low, high):
    gain, own = 1.0, jax.random.fold_in(rng, 6)
    for dim, shards_of in shards:
        draws = jnp.exp(jax.random.uniform(jax.random.fold_in(own, dim), (shards_of,), jnp.float32, low / len(shards), high / len(shards)))
        gain = gain * jnp.repeat(draws, extent[dim] // shards_of).reshape([-1 if axis == dim else 1 for axis in range(len(extent))])
    return gain


def normal_values(key, shape, scale, bound, shards=(), kind=jnp.bfloat16):
    array = jax.random.normal(key, shape, jnp.float32) * scale
    if len(shards) > 0:
        array = levels(key, shape, shards, -0.22, 0.18) * array
    return jnp.clip(array, min=-bound, max=bound).astype(kind)


def setup_inputs(seed: int = 0) -> dict:
    splits = jax.random.split(jax.random.key(seed), 5)
    object_field = normal_values(splits[0], (2, ROWS, W), 0.7, 5.0, ((1, 16),), jnp.float32)
    probe_modes = normal_values(splits[1], (2, MODES, WINDOW_SIDE, WINDOW_SIDE), 0.18, 2.5, ((1, 8),), jnp.float32)
    measured = draw_measured(jax.random.fold_in(splits[4], 71), 0)
    positions = draw_positions(jax.random.fold_in(splits[4], 71), 0)
    return dict(object_field=object_field, probe_modes=probe_modes, measured=measured, positions=positions)


regularizer = 0.1
step_scale = 0.3
epsilon = 1e-06

def gradient_window(padded_object, complex_probe, measured_window, row_begin, column_begin):
    patch = lax.dynamic_slice(padded_object, (row_begin, column_begin), (WINDOW_SIDE, WINDOW_SIDE))
    exit_wave = complex_probe * patch[None]
    far_field = jnp.fft.fft2(exit_wave, norm='ortho')
    probe_power = lax.optimization_barrier(jnp.sum(far_field.real ** 2 + far_field.imag ** 2, axis=0))
    object_update = jnp.sqrt((measured_window + regularizer) / (probe_power + regularizer)) - 1.0
    delta = jnp.fft.ifft2(object_update[None] * far_field, norm='ortho')
    return lax.optimization_barrier(jnp.sum(jnp.conj(complex_probe) * delta, axis=0))

def reference(object_field, probe_modes, measured, positions):
    complex_probe = probe_modes[0] + 1j * probe_modes[1]
    offsets = SR * jnp.arange(STRIPS, dtype=jnp.int32)
    every_row_start = (positions[:, :, 0] + offsets[:, None]).reshape(-1).astype(jnp.int32)
    every_column_start = positions[:, :, 1].reshape(-1).astype(jnp.int32)
    measured_patterns = measured.reshape(-1, WINDOW_SIDE, WINDOW_SIDE)
    field = object_field
    for iteration in range(ITERS):
        padded_object = jnp.pad(field[0] + 1j * field[1], ((0, HALO), (0, 0)))

        def single_window(element):
            return gradient_window(padded_object, complex_probe, element[0], element[1], element[2])
        window_gradients = lax.map(single_window, (measured_patterns, every_row_start, every_column_start))

        def accumulate(counter, total):
            start = (every_row_start[counter], every_column_start[counter])
            current = lax.dynamic_slice(total, start, (WINDOW_SIDE, WINDOW_SIDE))
            return lax.dynamic_update_slice(total, current + window_gradients[counter], start)
        total = lax.fori_loop(0, every_row_start.shape[0], accumulate, jnp.zeros_like(padded_object))
        gradient = total[:ROWS]
        stacked = jnp.stack([gradient.real, gradient.imag])
        square_sum = jnp.sum(stacked * stacked)
        factor = step_scale / jnp.sqrt(square_sum / (ROWS * W) + epsilon)
        field = field + factor * stacked
    return field
```

```python
import functools

import jax
import jax.numpy as jnp
import numpy as np
from jax import lax
from jax.experimental import pallas as pl
from jax.experimental.pallas import tpu as pltpu
from jax.sharding import PartitionSpec as P

ITERS = 3
SIDE = 256
HALF = 128
WIDTH = 384
OWN_MODES = 8
REGULARIZER = 0.1
STEP_SCALE = 0.3
EPSILON = 1e-06
CELLS = 4096 * 384
AXES = ("strip", "mode")
f32, bf16 = jnp.float32, jnp.bfloat16


def place(index):
    strip, mode = divmod(index, 8)
    core, j = strip % 2, strip // 2
    z, w = divmod(mode, 2)
    i = z if j % 2 == 0 else 3 - z
    return 4 * j + i, w, core


def device_of(pair, w, core):
    j, i = divmod(pair % 32, 4)
    z = i if j % 2 == 0 else 3 - i
    return (2 * j + core) * 8 + 2 * z + w


def route_pairs(move):
    return [(d, device_of(*move(*place(d)))) for d in range(128)]


def route_grid(move):
    route = []
    for d in range(128):
        strip, mode = divmod(d, 8)
        core, x, y_hi = strip % 2, strip // 2 % 4, strip // 8
        z, y_lo = divmod(mode, 2)
        y, x, z = move(2 * y_hi + y_lo, x, z)
        y, x, z = y % 4, x % 4, z % 4
        route.append((d, (((y // 2) * 4 + x) * 2 + core) * 8 + 2 * z + y % 2))
    return route


SWAP_CORE = route_pairs(lambda p, w, c: (p, w, 1 - c))
BAND_A = route_pairs(lambda p, w, c: (p, 1 - w, c))
BAND_B = route_pairs(lambda p, w, c: (p + 2 * c - 1, w, 1 - c))
BAND_C = route_pairs(lambda p, w, c: (p + 2 * c - 1, 1 - w, 1 - c))
Z_UP = route_grid(lambda y, x, z: (y, x, z + 1))
Z_DOWN = route_grid(lambda y, x, z: (y, x, z - 1))
Y_UP = route_grid(lambda y, x, z: (y + 1, x, z))
Y_DOWN = route_grid(lambda y, x, z: (y - 1, x, z))
DOUBLING = [
    route_grid(lambda y, x, z: (y, x, z ^ 1)),
    route_grid(lambda y, x, z: (y, x ^ 1, z)),
    route_grid(lambda y, x, z: (y ^ 2, x, z)),
    route_grid(lambda y, x, z: (y, x ^ 2, z)),
    route_grid(lambda y, x, z: (y, x, z ^ 2)),
]


def ring_route():
    route = []
    for j in range(8):
        for mode in range(8):
            low, high = (2 * j + 1) * 8 + mode, (2 * ((j + 1) % 8)) * 8 + mode
            route += [(low, high), (high, low)]
    return route


RING = ring_route()


def final_routes():
    one, two = [], []
    for j in range(8):
        for w in range(2):

            def at(i, c):
                return device_of(4 * j + i, w, c)

            one += [
                (at(0, 0), at(1, 0)),
                (at(1, 0), at(2, 0)),
                (at(0, 1), at(3, 0)),
                (at(2, 1), at(1, 1)),
                (at(2, 0), at(3, 1)),
                (at(1, 1), at(0, 1)),
            ]
            two += [(at(0, 0), at(2, 0)), (at(0, 1), at(3, 0)), (at(3, 0), at(0, 1))]
    return one, two


FINAL_ONE, FINAL_TWO = final_routes()


def send(value, route):
    return lax.ppermute(value, AXES, route)


def table(parity):
    n = np.arange(HALF)
    turns = (n[:, None] * (2 * n[None, :] + parity)) % SIDE
    angle = -2.0 * np.pi * turns / SIDE
    real, imag = np.cos(angle) / 16.0, np.sin(angle) / 16.0
    return np.block([[real, imag], [-imag, real]])


def tables():
    right, left = [], []
    for parity in range(2):
        t = table(parity)
        high = t.astype(np.float32).astype(jnp.bfloat16)
        low = (t - high.astype(np.float64)).astype(np.float32).astype(jnp.bfloat16)
        right.append(np.concatenate([high, high, low], axis=0))
        left.append(np.concatenate([high, high, low], axis=1))
    turned_right = [np.concatenate([r[:256].T, r[:256].T, r[512:].T], axis=0) for r in right]
    turned_left = [np.concatenate([r[:256].T, r[:256].T, r[512:].T], axis=1) for r in right]
    forward = (np.stack(right), np.stack(turned_left))
    inverse = (np.stack(left), np.stack(turned_right))
    return forward, inverse


def shuffle_table():
    rows = np.arange(SIDE)
    take = 2 * (rows % HALF) + rows // HALF
    return (take[:, None] == np.arange(SIDE)[None, :]).astype(jnp.bfloat16)


def halves(x):
    high = x.astype(bf16)
    low = (x - high.astype(f32)).astype(bf16)
    return high, low


def times_right(x, tab):
    high, low = halves(x)
    return jnp.dot(jnp.concatenate([high, low, high], axis=1), tab, preferred_element_type=f32)


def times_left(tab, x):
    high, low = halves(x)
    return jnp.dot(tab, jnp.concatenate([high, low, high], axis=0), preferred_element_type=f32)


def forward_transform(real, imag, cols, rows):
    stage = []
    for sign in (1.0, -1.0):
        if sign > 0:
            r, i = real[:, :HALF] + real[:, HALF:], imag[:, :HALF] + imag[:, HALF:]
        else:
            r, i = real[:, :HALF] - real[:, HALF:], imag[:, :HALF] - imag[:, HALF:]
        stage.append(times_right(jnp.concatenate([r, i], axis=1), cols[0 if sign > 0 else 1]))
    even, odd = stage
    top = [even[:HALF], odd[:HALF]]
    bottom = [even[HALF:], odd[HALF:]]
    out = []
    for parity in range(2):
        if parity == 0:
            mixed = [t + b for t, b in zip(top, bottom)]
        else:
            mixed = [t - b for t, b in zip(top, bottom)]
        block = jnp.concatenate(
            [
                jnp.concatenate([m[:, :HALF] for m in mixed], axis=1),
                jnp.concatenate([m[:, HALF:] for m in mixed], axis=1),
            ],
            axis=0,
        )
        out.append(times_left(rows[parity], block))
    return out


def inverse_transform(far_even, far_odd, rows, cols):
    b0 = times_left(rows[0], far_even)
    b1 = times_left(rows[1], far_odd)
    plus, minus = b0 + b1, b0 - b1
    c = []
    for q in range(2):
        lanes = slice(q * HALF, (q + 1) * HALF)
        real = jnp.concatenate([plus[:HALF, lanes], minus[:HALF, lanes]], axis=0)
        imag = jnp.concatenate([plus[HALF:, lanes], minus[HALF:, lanes]], axis=0)
        c.append(times_right(jnp.concatenate([real, imag], axis=1), cols[q]))
    real = jnp.concatenate([c[0][:, :HALF] + c[1][:, :HALF], c[0][:, :HALF] - c[1][:, :HALF]], axis=1)
    imag = jnp.concatenate([c[0][:, HALF:] + c[1][:, HALF:], c[0][:, HALF:] - c[1][:, HALF:]], axis=1)
    return real, imag


def cut_columns(x, column):
    return pltpu.roll(x, lax.rem(WIDTH - column, WIDTH), 1)[:, :SIDE]


VMEM = pl.BlockSpec(memory_space=pltpu.VMEM)
SMEM = pl.BlockSpec(memory_space=pltpu.SMEM)
ANY = pl.BlockSpec(memory_space=pl.ANY)


def params():
    return pltpu.CompilerParams(vmem_limit_bytes=48 * 1024 * 1024)


def facts_kernel(ids_ref, own_ref, core_ref, ring_ref, out_ref):
    i, core, w, last = ids_ref[0], ids_ref[1], ids_ref[2], ids_ref[3]

    def window(i, w):
        kind = lax.rem(i, 2)
        return jnp.where(kind == 0, 1 + w, 3 * w)

    def column(i, w):
        k = window(lax.rem(i + 4, 2), w)
        block = jnp.where(i < 2, 0, 1)
        mine = jnp.where(block == core, own_ref[k, 1], core_ref[k, 1])
        return jnp.where((i < 0) | (i > 3), ring_ref[k, 1], mine)

    other = i + 2 * core - 1
    out_ref[0] = i
    out_ref[1] = core
    out_ref[2] = last
    out_ref[3] = column(i, w)
    out_ref[4] = column(i, 1 - w)
    out_ref[5] = column(other, w)
    out_ref[6] = column(other, 1 - w)
    out_ref[7] = window(i, w)
    out_ref[8] = ids_ref[4]
    for extra in range(9, 16):
        out_ref[extra] = 0


def prepare_kernel(facts_ref, field_ref, field_core_ref, below_ref, below_core_ref, mine_ref, other_ref, shuffle_ref,
                   patch_ref, measured_ref, tall):
    i, core, last, column = facts_ref[0], facts_ref[1], facts_ref[2], facts_ref[3]
    for part in range(2):
        own, partner = field_ref[part], field_core_ref[part]
        tall[part, 0:256] = jnp.where(core == 0, own, partner)
        tall[part, 256:512] = jnp.where(core == 0, partner, own)
        below = jnp.where(core == 0, below_core_ref[part], below_ref[part])
        tall[part, 512:640] = jnp.where(last == 1, jnp.zeros_like(below), below)
        rows = tall[part, pl.ds(pl.multiple_of(i * HALF, HALF), SIDE), :]
        patch_ref[part] = cut_columns(rows, column)
    block = jnp.where(i < 2, 0, 1)
    window = jnp.where(block == core, mine_ref[...], other_ref[...])
    shuffle = shuffle_ref[...]
    h0 = window.astype(bf16)
    rest = window - h0.astype(f32)
    h1 = rest.astype(bf16)
    h2 = (rest - h1.astype(f32)).astype(bf16)
    moved = []
    for piece in (h0, h1, h2):
        rows = jnp.dot(shuffle, piece, preferred_element_type=f32).astype(bf16)
        moved.append(lax.dot_general(rows, shuffle, (((1,), (1,)), ((), ())), preferred_element_type=f32))
    measured_ref[...] = moved[0] + moved[1] + moved[2]


def power_of(far):
    return far[:HALF] * far[:HALF] + far[HALF:] * far[HALF:]


def first_kernel(patch_ref, real_ref, imag_ref, cols_ref, rows_ref, *refs, first):
    if first:
        far_ref, probe_ref, power_ref = refs
    else:
        _, _, power_in_ref, far_ref, probe_ref, power_ref = refs
    pr, pi = real_ref[...], imag_ref[...]
    xr, xi = patch_ref[0], patch_ref[1]
    probe_ref[0, 0] = pr
    probe_ref[0, 1] = pi
    far = forward_transform(pr * xr - pi * xi, pr * xi + pi * xr, cols_ref, rows_ref)
    for parity in range(2):
        far_ref[0, parity] = far[parity]
        power = power_of(far[parity])
        if not first:
            power = power + power_in_ref[parity]
        power_ref[parity] = power


def first_call(index, patch, real, imag, fwd, carried):
    first = carried is None
    block = (1, 2, SIDE, SIDE)
    full = jax.ShapeDtypeStruct((OWN_MODES, 2, SIDE, SIDE), f32)
    power = jax.ShapeDtypeStruct((2, HALF, SIDE), f32)

    def whole(shape):
        return pl.BlockSpec(shape, lambda g: (0,) * len(shape))

    in_specs = [whole((2, SIDE, SIDE)), whole((SIDE, SIDE)), whole((SIDE, SIDE)), whole((2, 768, 256)), whole((2, 256, 768))]
    args = [patch, real, imag, fwd[0], fwd[1]]
    aliases = {}
    if not first:
        in_specs += [ANY, ANY, whole((2, HALF, SIDE))]
        args += list(carried)
        aliases = {5: 0, 6: 1}
    slot = pl.BlockSpec(block, lambda g: (index, 0, 0, 0))
    return pl.pallas_call(
        functools.partial(first_kernel, first=first),
        grid=(1,),
        in_specs=in_specs,
        out_specs=[slot, slot, whole((2, HALF, SIDE))],
        out_shape=[full, full, power],
        input_output_aliases=aliases,
        compiler_params=params(),
        cost_estimate=pl.CostEstimate(flops=420_000_000, bytes_accessed=3_000_000, transcendentals=0),
        name="first_far",
    )(*args)


def advance_kernel(facts_ref, mine_ref, other_ref, probe_ref, far_ref, cols_ref, rows_ref, step_ref, powers_ref, patch):
    @pl.when(pl.program_id(0) == 0)
    def _():
        core, last, column = facts_ref[1], facts_ref[2], facts_ref[3]
        for part in range(2):
            mine, other = mine_ref[part], other_ref[part]
            top = jnp.where(core == 0, mine, other)
            bottom = jnp.where(core == 0, other, mine)
            bottom = jnp.where(last == 1, jnp.zeros_like(bottom), bottom)
            patch[part, 0:HALF] = cut_columns(top, column)
            patch[part, HALF:] = cut_columns(bottom, column)
        powers_ref[...] = jnp.zeros_like(powers_ref)

    pr, pi = probe_ref[0, 0], probe_ref[0, 1]
    xr, xi = patch[0], patch[1]
    step = forward_transform(pr * xr - pi * xi, pr * xi + pi * xr, cols_ref, rows_ref)
    for parity in range(2):
        step_ref[0, parity] = step[parity]
        far = far_ref[0, parity]
        cross = far * step[parity]
        powers_ref[0, parity] += cross[:HALF] + cross[HALF:]
        powers_ref[1, parity] += power_of(step[parity])


def whole(shape):
    return pl.BlockSpec(shape, lambda g: (0,) * len(shape))


SLOT = pl.BlockSpec((1, 2, SIDE, SIDE), lambda g: (g, 0, 0, 0))


def advance_call(facts, mine, other, probe, far, fwd):
    return pl.pallas_call(
        advance_kernel,
        grid=(OWN_MODES,),
        in_specs=[SMEM, whole((2, HALF, WIDTH)), whole((2, HALF, WIDTH)), SLOT, SLOT, whole((2, 768, 256)), whole((2, 256, 768))],
        out_specs=[SLOT, whole((2, 2, HALF, SIDE))],
        out_shape=[
            jax.ShapeDtypeStruct((OWN_MODES, 2, SIDE, SIDE), f32),
            jax.ShapeDtypeStruct((2, 2, HALF, SIDE), f32),
        ],
        scratch_shapes=[pltpu.VMEM((2, SIDE, SIDE), f32)],
        compiler_params=params(),
        cost_estimate=pl.CostEstimate(flops=3_400_000_000, bytes_accessed=13_000_000, transcendentals=0),
        name="far_step",
    )(facts, mine, other, probe, far, *fwd)


def step_factor(squares):
    square_sum = jnp.sum(jnp.sum(squares, axis=0, keepdims=True), axis=1, keepdims=True)
    return STEP_SCALE / jnp.sqrt(square_sum / CELLS + EPSILON)


def gradient_kernel(*refs, first):
    if first:
        facts_ref, power_ref, other_ref, measured_ref, probe_ref, far_ref, rows_ref, cols_ref, keep_ref, give_ref, change, total = refs
    else:
        (facts_ref, squares_ref, base_ref, power_ref, other_ref, measured_ref, probe_ref, far_ref, step_ref, rows_ref, cols_ref,
         keep_ref, give_ref, far_out_ref, base_out_ref, factor_ref, change, total) = refs

    @pl.when(pl.program_id(0) == 0)
    def _():
        if not first:
            factor_ref[...] = jnp.broadcast_to(step_factor(squares_ref[...]), (8, SIDE))
        for parity in range(2):
            rows = slice(parity * HALF, (parity + 1) * HALF)
            if first:
                power = power_ref[parity] + other_ref[parity]
            else:
                factor = factor_ref[0:1]
                cross = power_ref[0, parity] + other_ref[0, parity]
                square = power_ref[1, parity] + other_ref[1, parity]
                power = jnp.maximum(base_ref[parity] + factor * (2.0 * cross + factor * square), 0.0)
                base_out_ref[parity] = power
            ratio = (measured_ref[rows] + REGULARIZER) / (power + REGULARIZER)
            change[parity] = jnp.sqrt(ratio) - 1.0
        total[...] = jnp.zeros_like(total)

    shifted = []
    for parity in range(2):
        far = far_ref[0, parity]
        if not first:
            far = far + factor_ref[0:1] * step_ref[0, parity]
            far_out_ref[0, parity] = far
        c = change[parity]
        shifted.append(jnp.concatenate([far[:HALF] * c, far[HALF:] * c], axis=0))
    dr, di = inverse_transform(shifted[0], shifted[1], rows_ref, cols_ref)
    pr, pi = probe_ref[0, 0], probe_ref[0, 1]
    total[0] += pr * dr + pi * di
    total[1] += pr * di - pi * dr

    @pl.when(pl.program_id(0) == OWN_MODES - 1)
    def _():
        core = facts_ref[1]
        keep_ref[...] = total[:, pl.ds(pl.multiple_of(core * HALF, HALF), HALF), :]
        give_ref[...] = total[:, pl.ds(pl.multiple_of((1 - core) * HALF, HALF), HALF), :]


def gradient_call(facts, squares, base, power, other, measured, probe, far, step, inv):
    first = squares is None
    half = jax.ShapeDtypeStruct((2, HALF, SIDE), f32)
    half_spec = whole((2, HALF, SIDE))
    tabs = [whole((2, 256, 768)), whole((2, 768, 256))]
    if first:
        args = [facts, power, other, measured, probe, far, *inv]
        in_specs = [SMEM, half_spec, half_spec, whole((SIDE, SIDE)), SLOT, SLOT, *tabs]
        out_shape, out_specs = [half, half], [half_spec, half_spec]
    else:
        args = [facts, squares, base, power, other, measured, probe, far, step, *inv]
        two = whole((2, 2, HALF, SIDE))
        in_specs = [SMEM, whole((8, 128)), half_spec, two, two, whole((SIDE, SIDE)), SLOT, SLOT, SLOT, *tabs]
        out_shape = [half, half, jax.ShapeDtypeStruct((OWN_MODES, 2, SIDE, SIDE), f32), half, jax.ShapeDtypeStruct((8, SIDE), f32)]
        out_specs = [half_spec, half_spec, SLOT, half_spec, whole((8, SIDE))]
    return pl.pallas_call(
        functools.partial(gradient_kernel, first=first),
        grid=(OWN_MODES,),
        in_specs=in_specs,
        out_specs=out_specs,
        out_shape=out_shape,
        scratch_shapes=[pltpu.VMEM((2, HALF, SIDE), f32), pltpu.VMEM((2, SIDE, SIDE), f32)],
        compiler_params=params(),
        cost_estimate=pl.CostEstimate(flops=3_400_000_000, bytes_accessed=17_000_000, transcendentals=65536),
        name="window_gradient",
    )(*args)


def merge_kernel(facts_ref, own_ref, a_ref, b_ref, c_ref, band_ref, square_ref):
    core, last = facts_ref[1], facts_ref[2]

    def wide(x, column):
        x = jnp.concatenate([x, jnp.zeros((HALF, WIDTH - SIDE), f32)], axis=1)
        return pltpu.roll(x, column, 1)

    is_first = facts_ref[8]
    drop_own = (last == 1) & (core == 1)
    drop_other = (is_first == 1) & (core == 0)
    squares = jnp.zeros((8, 128), f32)
    for part in range(2):
        own = wide(own_ref[part], facts_ref[3]) + wide(a_ref[part], facts_ref[4])
        other = wide(b_ref[part], facts_ref[5]) + wide(c_ref[part], facts_ref[6])
        own = jnp.where(drop_own, jnp.zeros_like(own), own)
        other = jnp.where(drop_other, jnp.zeros_like(other), other)
        band = own + other
        band_ref[part] = band
        sq = (band * band).reshape(HALF // 8, 8, WIDTH).sum(axis=0)
        squares = squares + sq[:, 0:128] + sq[:, 128:256] + sq[:, 256:384]
    square_ref[...] = squares


def merge_call(facts, own, a, b, c):
    return pl.pallas_call(
        merge_kernel,
        in_specs=[SMEM, VMEM, VMEM, VMEM, VMEM],
        out_specs=[VMEM, VMEM],
        out_shape=[jax.ShapeDtypeStruct((2, HALF, WIDTH), f32), jax.ShapeDtypeStruct((8, 128), f32)],
        compiler_params=params(),
        cost_estimate=pl.CostEstimate(flops=1_000_000, bytes_accessed=2_000_000, transcendentals=0),
        name="band_sum",
    )(facts, own, a, b, c)


def body(object_field, probe_modes, measured, positions):
    strip, mode = lax.axis_index("strip"), lax.axis_index("mode")
    core, j = strip % 2, strip // 2
    z, w = mode // 2, mode % 2
    i = jnp.where(j % 2 == 0, z, 3 - z)
    pair = 4 * j + i
    last = (pair == 31).astype(jnp.int32)
    initial = (pair == 0).astype(jnp.int32)
    fwd, inv = tables()
    fwd = [jnp.asarray(t) for t in fwd]
    inv = [jnp.asarray(t) for t in inv]
    shuffle = jnp.asarray(shuffle_table())

    own = lax.dynamic_index_in_dim(probe_modes, core, 1, keepdims=False)
    re0, im0 = own[0], own[1]
    up = send(own, Z_UP)
    down = send(own, Z_DOWN)
    side = (send(re0, Y_UP), send(im0, Y_DOWN))
    far_away = (send(up[0], Z_UP), send(down[1], Z_DOWN))
    up_side = send(up, Y_UP)
    down_side = send(down, Y_DOWN)
    far_side = (send(far_away[0], Y_UP), send(far_away[1], Y_DOWN))
    modes = [(re0, im0), (up[0], up[1]), (down[0], down[1]), side, far_away, (up_side[0], up_side[1]),
             (down_side[0], down_side[1]), far_side]

    places = positions[0]
    ids = jnp.stack([i, core, w, last, initial]).astype(jnp.int32)
    facts = pl.pallas_call(
        facts_kernel,
        in_specs=[SMEM] * 4,
        out_specs=SMEM,
        out_shape=jax.ShapeDtypeStruct((16,), jnp.int32),
        name="facts",
    )(ids, places, send(places, SWAP_CORE), send(places, RING))
    window = jnp.where(i % 2 == 0, 1 + w, 3 * w)
    mine = lax.dynamic_index_in_dim(measured[0], window, 0, keepdims=False)
    below = send(object_field[:, :HALF], RING)
    patch, pattern = pl.pallas_call(
        prepare_kernel,
        in_specs=[SMEM] + [VMEM] * 7,
        out_specs=[VMEM] * 2,
        out_shape=[
            jax.ShapeDtypeStruct((2, SIDE, SIDE), f32),
            jax.ShapeDtypeStruct((SIDE, SIDE), f32),
        ],
        scratch_shapes=[pltpu.VMEM((2, 640, WIDTH), f32)],
        compiler_params=params(),
        name="prepare",
    )(facts, object_field, send(object_field, SWAP_CORE), below, send(below, SWAP_CORE), mine, send(mine, SWAP_CORE), shuffle)

    carried = None
    for index, (real, imag) in enumerate(modes):
        carried = first_call(index, patch, real, imag, fwd, carried)
    far, probe, power = carried
    base = squares = step = None
    bands, factors = [], []
    for iteration in range(ITERS):
        other = send(power, SWAP_CORE)
        if iteration == 0:
            keep, give = gradient_call(facts, None, None, power, other, pattern, probe, far, None, inv)
            base = power + other
        else:
            keep, give, far, base, factor = gradient_call(
                facts, squares, base, power, other, pattern, probe, far, step, inv
            )
            factors.append(factor[0, 0])
        if iteration + 1 == ITERS:
            earlier = [f * b for f, b in zip(factors, bands)]
            early = distribute(sum(earlier[1:], earlier[0]), i, core)
        half = keep + send(give, SWAP_CORE)
        band, squares = merge_call(facts, half, send(half, BAND_A), send(half, BAND_B), send(half, BAND_C))
        partner = send(band, SWAP_CORE)
        pair_bands = jnp.concatenate([jnp.where(core == 0, band, partner), jnp.where(core == 0, partner, band)], axis=1)
        bands.append(pair_bands)
        if iteration + 1 < ITERS:
            step, power = advance_call(facts, band, partner, probe, far, fwd)
        else:
            late = distribute(pair_bands, i, core)
        for route in DOUBLING:
            squares = squares + send(squares, route)
    return object_field + early + step_factor(squares) * late


def distribute(pair_bands, i, core):
    upper, lower = pair_bands[:, :HALF], pair_bands[:, HALF:]
    first_out = jnp.where((core == 1) & ((i == 1) | (i == 2)), lower, upper)
    second_out = jnp.where((i == 0) & (core == 1), lower, upper)
    got_one = send(first_out, FINAL_ONE)
    got_two = send(second_out, FINAL_TWO)
    has_both = i == 2 * core
    swapped = (i == 2) & (core == 0)
    near = (i == 1) & (core == 0)
    near_low = (i == 1) & (core == 1)
    near_up = (i == 3) & (core == 1)
    upper_new = jnp.where(has_both, upper, jnp.where(swapped, got_two, jnp.where(near_low, lower, got_one)))
    lower_new = jnp.where(
        has_both,
        lower,
        jnp.where(swapped | near_low, got_one, jnp.where(near | near_up, upper, got_two)),
    )
    return jnp.concatenate([upper_new, lower_new], axis=1)


def solution(mesh):
    return jax.shard_map(
        body,
        mesh=mesh,
        in_specs=(
            P(None, "strip", None),
            P(None, "mode", None, None),
            P("strip", None, None, None),
            P("strip", None, None),
        ),
        out_specs=P(None, "strip", None),
        check_vma=False,
    )
```

```python
import functools

import jax
import jax.numpy as jnp
import numpy as np
from jax import lax
from jax.experimental import pallas as pl
from jax.experimental.pallas import tpu as pltpu
from jax.sharding import PartitionSpec as P

ITERS = 3
SIDE = 256
HALF = 128
WIDTH = 384
OWN_MODES = 8
REGULARIZER = 0.1
STEP_SCALE = 0.3
EPSILON = 1e-06
CELLS = 4096 * 384
AXES = ("strip", "mode")
f32, bf16 = jnp.float32, jnp.bfloat16


def place(index):
    strip, mode = divmod(index, 8)
    core, j = strip % 2, strip // 2
    z, w = divmod(mode, 2)
    i = z if j % 2 == 0 else 3 - z
    return 4 * j + i, w, core


def device_of(pair, w, core):
    j, i = divmod(pair % 32, 4)
    z = i if j % 2 == 0 else 3 - i
    return (2 * j + core) * 8 + 2 * z + w


def route_pairs(move):
    return [(d, device_of(*move(*place(d)))) for d in range(128)]


def route_grid(move):
    route = []
    for d in range(128):
        strip, mode = divmod(d, 8)
        core, x, y_hi = strip % 2, strip // 2 % 4, strip // 8
        z, y_lo = divmod(mode, 2)
        y, x, z = move(2 * y_hi + y_lo, x, z)
        y, x, z = y % 4, x % 4, z % 4
        route.append((d, (((y // 2) * 4 + x) * 2 + core) * 8 + 2 * z + y % 2))
    return route


SWAP_CORE = route_pairs(lambda p, w, c: (p, w, 1 - c))
BAND_A = route_pairs(lambda p, w, c: (p, 1 - w, c))
BAND_B = route_pairs(lambda p, w, c: (p + 2 * c - 1, w, 1 - c))
BAND_C = route_pairs(lambda p, w, c: (p + 2 * c - 1, 1 - w, 1 - c))
Z_UP = route_grid(lambda y, x, z: (y, x, z + 1))
Z_DOWN = route_grid(lambda y, x, z: (y, x, z - 1))
Y_UP = route_grid(lambda y, x, z: (y + 1, x, z))
Y_DOWN = route_grid(lambda y, x, z: (y - 1, x, z))
DOUBLING = [
    route_grid(lambda y, x, z: (y, x, z ^ 1)),
    route_grid(lambda y, x, z: (y, x ^ 1, z)),
    route_grid(lambda y, x, z: (y ^ 2, x, z)),
    route_grid(lambda y, x, z: (y, x ^ 2, z)),
    route_grid(lambda y, x, z: (y, x, z ^ 2)),
]

LAST_DOUBLING = [DOUBLING[k] for k in (1, 2, 3, 0, 4)]


def ring_route():
    route = []
    for j in range(8):
        for mode in range(8):
            low, high = (2 * j + 1) * 8 + mode, (2 * ((j + 1) % 8)) * 8 + mode
            route += [(low, high), (high, low)]
    return route


RING = ring_route()


def final_routes():
    one, two = [], []
    for j in range(8):
        for w in range(2):

            def at(i, c):
                return device_of(4 * j + i, w, c)

            one += [
                (at(0, 0), at(1, 0)),
                (at(1, 0), at(2, 0)),
                (at(0, 1), at(3, 0)),
                (at(2, 1), at(1, 1)),
                (at(2, 0), at(3, 1)),
                (at(1, 1), at(0, 1)),
            ]
            two += [(at(0, 0), at(2, 0)), (at(0, 1), at(3, 0)), (at(3, 0), at(0, 1))]
    return one, two


FINAL_ONE, FINAL_TWO = final_routes()


def send(value, route):
    return lax.ppermute(value, AXES, route)


def table(parity):
    n = np.arange(HALF)
    turns = (n[:, None] * (2 * n[None, :] + parity)) % SIDE
    angle = -2.0 * np.pi * turns / SIDE
    real, imag = np.cos(angle) / 16.0, np.sin(angle) / 16.0
    return np.block([[real, imag], [-imag, real]])


def tables():
    right, left = [], []
    for parity in range(2):
        t = table(parity)
        high = t.astype(np.float32).astype(jnp.bfloat16)
        low = (t - high.astype(np.float64)).astype(np.float32).astype(jnp.bfloat16)
        right.append(np.concatenate([high, high, low], axis=0))
        left.append(np.concatenate([high, high, low], axis=1))
    turned_right = [np.concatenate([r[:256].T, r[:256].T, r[512:].T], axis=0) for r in right]
    turned_left = [np.concatenate([r[:256].T, r[:256].T, r[512:].T], axis=1) for r in right]
    forward = (np.stack(right), np.stack(turned_left))
    inverse = (np.stack(left), np.stack(turned_right))
    return forward, inverse


def shuffle_table():
    rows = np.arange(SIDE)
    take = 2 * (rows % HALF) + rows // HALF
    return (take[:, None] == np.arange(SIDE)[None, :]).astype(jnp.bfloat16)


def halves(x):
    high = x.astype(bf16)
    low = (x - high.astype(f32)).astype(bf16)
    return high, low


def times_right(x, tab):
    high, low = halves(x)
    return jnp.dot(jnp.concatenate([high, low, high], axis=1), tab, preferred_element_type=f32)


def times_left(tab, x):
    high, low = halves(x)
    return jnp.dot(tab, jnp.concatenate([high, low, high], axis=0), preferred_element_type=f32)


def forward_transform(real, imag, cols, rows):
    stage = []
    for sign in (1.0, -1.0):
        if sign > 0:
            r, i = real[:, :HALF] + real[:, HALF:], imag[:, :HALF] + imag[:, HALF:]
        else:
            r, i = real[:, :HALF] - real[:, HALF:], imag[:, :HALF] - imag[:, HALF:]
        stage.append(times_right(jnp.concatenate([r, i], axis=1), cols[0 if sign > 0 else 1]))
    even, odd = stage
    top = [even[:HALF], odd[:HALF]]
    bottom = [even[HALF:], odd[HALF:]]
    out = []
    for parity in range(2):
        if parity == 0:
            mixed = [t + b for t, b in zip(top, bottom)]
        else:
            mixed = [t - b for t, b in zip(top, bottom)]
        block = jnp.concatenate(
            [
                jnp.concatenate([m[:, :HALF] for m in mixed], axis=1),
                jnp.concatenate([m[:, HALF:] for m in mixed], axis=1),
            ],
            axis=0,
        )
        out.append(times_left(rows[parity], block))
    return out


def inverse_transform(far_even, far_odd, rows, cols):
    b0 = times_left(rows[0], far_even)
    b1 = times_left(rows[1], far_odd)
    plus, minus = b0 + b1, b0 - b1
    c = []
    for q in range(2):
        lanes = slice(q * HALF, (q + 1) * HALF)
        real = jnp.concatenate([plus[:HALF, lanes], minus[:HALF, lanes]], axis=0)
        imag = jnp.concatenate([plus[HALF:, lanes], minus[HALF:, lanes]], axis=0)
        c.append(times_right(jnp.concatenate([real, imag], axis=1), cols[q]))
    real = jnp.concatenate([c[0][:, :HALF] + c[1][:, :HALF], c[0][:, :HALF] - c[1][:, :HALF]], axis=1)
    imag = jnp.concatenate([c[0][:, HALF:] + c[1][:, HALF:], c[0][:, HALF:] - c[1][:, HALF:]], axis=1)
    return real, imag


def cut_columns(x, column):
    return pltpu.roll(x, lax.rem(WIDTH - column, WIDTH), 1)[:, :SIDE]


VMEM = pl.BlockSpec(memory_space=pltpu.VMEM)
SMEM = pl.BlockSpec(memory_space=pltpu.SMEM)
ANY = pl.BlockSpec(memory_space=pl.ANY)
HBM = pl.BlockSpec(memory_space=pltpu.HBM)


def params():
    return pltpu.CompilerParams(vmem_limit_bytes=12 * 1024 * 1024)


def copy_all(pairs, sems):
    copies = [pltpu.make_async_copy(source, target, sems.at[k]) for k, (source, target) in enumerate(pairs)]
    for copy in copies:
        copy.start()
    return copies


def write_columns(places_ref, out_ref, row):
    for k in range(4):
        column = places_ref[k, 1].astype(f32)
        out_ref[0, row + k : row + k + 1] = jnp.full((1, WIDTH), column, f32)
        out_ref[1, row + k : row + k + 1] = jnp.full((1, WIDTH), column, f32)
    out_ref[:, row + 4 : row + 8] = jnp.zeros((2, 4, WIDTH), f32)


def ring_pack_kernel(field_ref, places_ref, *refs):
    out_ref, sems = refs[-2:]
    copies = copy_all([(field_ref.at[:, pl.ds(0, HALF)], out_ref.at[:, pl.ds(0, HALF)])], sems)
    write_columns(places_ref, out_ref, HALF)
    for copy in copies:
        copy.wait()


def core_pack_kernel(field_ref, places_ref, ring_ref, *refs):
    out_ref, sems = refs[-2:]
    copies = copy_all(
        [(field_ref, out_ref.at[:, pl.ds(0, SIDE)]), (ring_ref, out_ref.at[:, pl.ds(SIDE, HALF + 8)])], sems
    )
    write_columns(places_ref, out_ref, SIDE + HALF + 8)
    for copy in copies:
        copy.wait()


def pack_call(kernel, rows, field, places, others, name):
    return pl.pallas_call(
        kernel,
        in_specs=[HBM, SMEM] + [ANY] * len(others),
        out_specs=VMEM,
        out_shape=jax.ShapeDtypeStruct((2, rows, WIDTH), f32),
        scratch_shapes=[pltpu.SemaphoreType.DMA((2,))],
        compiler_params=params(),
        name=name,
    )(field, places, *others)


def prepare_kernel(ids_ref, places_ref, ring_ref, mine_pack_ref, pack_ref, mine_ref, other_ref, shuffle_ref,
                   patch_ref, measured_ref, facts_ref, tall):
    i, core, w, last = ids_ref[0], ids_ref[1], ids_ref[2], ids_ref[3]

    def listed(ref, row):
        return [jnp.max(ref[0, row + k : row + k + 1, 0:128]).astype(jnp.int32) for k in range(4)]

    partner_columns = listed(pack_ref, SIDE + HALF + 8)
    ring_columns = listed(ring_ref, HALF)

    def pick(values, k):
        return jnp.where(k == 0, values[0], jnp.where(k == 1, values[1], jnp.where(k == 2, values[2], values[3])))

    def column(i, w):
        k = jnp.where(lax.rem(i + 4, 2) == 0, 1 + w, 3 * w)
        block = jnp.where(i < 2, 0, 1)
        near = jnp.where(block == core, places_ref[k, 1], pick(partner_columns, k))
        return jnp.where((i < 0) | (i > 3), pick(ring_columns, k), near)

    other = i + 2 * core - 1
    own_column = column(i, w)
    facts_ref[0] = i
    facts_ref[1] = core
    facts_ref[2] = last
    facts_ref[3] = own_column
    facts_ref[4] = column(i, 1 - w)
    facts_ref[5] = column(other, w)
    facts_ref[6] = column(other, 1 - w)
    facts_ref[7] = 0
    facts_ref[8] = ids_ref[4]
    for part in range(2):
        own, partner = mine_pack_ref[part, 0:SIDE], pack_ref[part, 0:SIDE]
        tall[part, 0:256] = jnp.where(core == 0, own, partner)
        tall[part, 256:512] = jnp.where(core == 0, partner, own)
        below = jnp.where(core == 0, pack_ref[part, SIDE : SIDE + HALF], ring_ref[part, 0:HALF])
        tall[part, 512:640] = jnp.where(last == 1, jnp.zeros_like(below), below)
        rows = tall[part, pl.ds(pl.multiple_of(i * HALF, HALF), SIDE), :]
        patch_ref[part] = cut_columns(rows, own_column)
    block = jnp.where(i < 2, 0, 1)
    window = jnp.where(block == core, mine_ref[...], other_ref[...])
    shuffle = shuffle_ref[...]
    h0 = window.astype(bf16)
    rest = window - h0.astype(f32)
    h1 = rest.astype(bf16)
    h2 = (rest - h1.astype(f32)).astype(bf16)
    moved = []
    for piece in (h0, h1, h2):
        rows = jnp.dot(shuffle, piece, preferred_element_type=f32).astype(bf16)
        moved.append(lax.dot_general(rows, shuffle, (((1,), (1,)), ((), ())), preferred_element_type=f32))
    measured_ref[...] = moved[0] + moved[1] + moved[2]


def power_of(far):
    return far[:HALF] * far[:HALF] + far[HALF:] * far[HALF:]


def first_kernel(patch_ref, cols_ref, rows_ref, *refs, begin, end):
    far_ref, probe_ref, power_ref, sems = refs[-4:]
    if begin == 0:
        copies = copy_all([(refs[m], probe_ref.at[m]) for m in range(end)], sems)
    else:
        copies = copy_all([(refs[k], probe_ref.at[begin, k]) for k in range(2)], sems)
        power_ref[...] = refs[4][...]
    xr, xi = patch_ref[0], patch_ref[1]
    for m in range(begin, end):
        if begin == 0:
            copies[m].wait()
        else:
            copies[0].wait()
            copies[1].wait()
        pr, pi = probe_ref[m, 0], probe_ref[m, 1]
        far = forward_transform(pr * xr - pi * xi, pr * xi + pi * xr, cols_ref, rows_ref)
        for parity in range(2):
            far_ref[m, parity] = far[parity]
            power = power_of(far[parity])
            power_ref[parity] = power if m == 0 else power_ref[parity] + power


FULL = jax.ShapeDtypeStruct((OWN_MODES, 2, SIDE, SIDE), f32)


def first_call(begin, end, patch, fwd, arrays, carried):
    args = [patch, *fwd, *arrays]
    in_specs = [VMEM] * 3 + [ANY] * len(arrays)
    aliases = {}
    if carried:
        aliases = {len(args) + k: k for k in range(2)}
        args += carried
        in_specs += [VMEM] * 3
    return pl.pallas_call(
        functools.partial(first_kernel, begin=begin, end=end),
        in_specs=in_specs,
        out_specs=[VMEM] * 3,
        out_shape=[FULL, FULL, jax.ShapeDtypeStruct((2, HALF, SIDE), f32)],
        input_output_aliases=aliases,
        scratch_shapes=[pltpu.SemaphoreType.DMA((8,))],
        compiler_params=params(),
        cost_estimate=pl.CostEstimate(flops=800_000_000 * (end - begin), bytes_accessed=3_000_000, transcendentals=0),
        name="first_far",
    )(*args)


def advance_kernel(*refs, begin, end, first):
    if first:
        facts_ref, mine_ref, other_ref, probe_ref, far_ref, cols_ref, rows_ref, _, patch, step_ref, powers_ref, token_ref = refs
        core, last, column = facts_ref[1], facts_ref[2], facts_ref[3]
        for part in range(2):
            mine, other = mine_ref[part], other_ref[part]
            top = jnp.where(core == 0, mine, other)
            bottom = jnp.where(core == 0, other, mine)
            bottom = jnp.where(last == 1, jnp.zeros_like(bottom), bottom)
            patch[part, 0:HALF] = cut_columns(top, column)
            patch[part, HALF:] = cut_columns(bottom, column)
        powers_ref[...] = jnp.zeros_like(powers_ref)
    else:
        patch, probe_ref, far_ref, cols_ref, rows_ref, _, _, powers_in_ref, step_ref, powers_ref, token_ref = refs
        powers_ref[...] = powers_in_ref[...]
    token_ref[...] = jnp.zeros_like(token_ref)

    for m in range(begin, end):
        pr, pi = probe_ref[m, 0], probe_ref[m, 1]
        xr, xi = patch[0], patch[1]
        step = forward_transform(pr * xr - pi * xi, pr * xi + pi * xr, cols_ref, rows_ref)
        for parity in range(2):
            step_ref[m, parity] = step[parity]
            far = far_ref[m, parity]
            cross = far * step[parity]
            powers_ref[0, parity] += cross[:HALF] + cross[HALF:]
            powers_ref[1, parity] += power_of(step[parity])


UNROLL = 2
SMALL = jax.ShapeDtypeStruct((8, 128), f32)


def advance_call(begin, end, facts, mine, other, probe, far, fwd, after, carried):
    powers = jax.ShapeDtypeStruct((2, 2, HALF, SIDE), f32)
    first = carried is None
    aliases = {}
    if first:
        args = [facts, mine, other, probe, far, *fwd, after]
        in_specs = [SMEM] + [VMEM] * 6 + [ANY]
        out_shape = [jax.ShapeDtypeStruct((2, SIDE, SIDE), f32), FULL, powers, SMALL]
    else:
        args = [carried[0], probe, far, *fwd, after, carried[1], carried[2]]
        in_specs = [VMEM] * 5 + [ANY] + [VMEM] * 2
        out_shape = [FULL, powers, SMALL]
        aliases = {6: 0, 7: 1}
    out = pl.pallas_call(
        functools.partial(advance_kernel, begin=begin, end=end, first=first),
        in_specs=in_specs,
        out_specs=[VMEM] * len(out_shape),
        out_shape=out_shape,
        input_output_aliases=aliases,
        compiler_params=params(),
        cost_estimate=pl.CostEstimate(flops=800_000_000 * (end - begin), bytes_accessed=3_000_000, transcendentals=0),
        name="far_step",
    )(*args)
    return out if first else [carried[0], *out]


def step_factor(squares):
    square_sum = jnp.sum(jnp.sum(squares, axis=0, keepdims=True), axis=1, keepdims=True)
    return STEP_SCALE / jnp.sqrt(square_sum / (2 * CELLS) + EPSILON)


def gradient_kernel(*refs, first):
    if first:
        facts_ref, power_ref, other_ref, measured_ref, probe_ref, far_ref, rows_ref, cols_ref, keep_ref, give_ref, change, total = refs
    else:
        (facts_ref, squares_ref, base_ref, power_ref, other_ref, measured_ref, probe_ref, far_ref, step_ref, rows_ref, cols_ref,
         keep_ref, give_ref, far_out_ref, base_out_ref, factor_ref, change, total) = refs
        factor_ref[...] = jnp.broadcast_to(step_factor(squares_ref[...]), (8, SIDE))
        factor = factor_ref[0:1]
    for parity in range(2):
        rows = slice(parity * HALF, (parity + 1) * HALF)
        if first:
            power = power_ref[parity] + other_ref[parity]
        else:
            cross = power_ref[0, parity] + other_ref[0, parity]
            square = power_ref[1, parity] + other_ref[1, parity]
            power = jnp.maximum(base_ref[parity] + factor * (2.0 * cross + factor * square), 0.0)
            base_out_ref[parity] = power
        ratio = (measured_ref[rows] + REGULARIZER) / (power + REGULARIZER)
        change[parity] = jnp.sqrt(ratio) - 1.0
    total[...] = jnp.zeros_like(total)

    def one(m, carry):
        shifted = []
        for parity in range(2):
            far = far_ref[m, parity]
            if not first:
                far = far + factor_ref[0:1] * step_ref[m, parity]
                far_out_ref[m, parity] = far
            c = change[parity]
            shifted.append(jnp.concatenate([far[:HALF] * c, far[HALF:] * c], axis=0))
        dr, di = inverse_transform(shifted[0], shifted[1], rows_ref, cols_ref)
        pr, pi = probe_ref[m, 0], probe_ref[m, 1]
        total[0] += pr * dr + pi * di
        total[1] += pr * di - pi * dr
        return carry

    lax.fori_loop(0, OWN_MODES, one, 0, unroll=UNROLL)
    core = facts_ref[1]
    keep_ref[...] = total[:, pl.ds(pl.multiple_of(core * HALF, HALF), HALF), :]
    give_ref[...] = total[:, pl.ds(pl.multiple_of((1 - core) * HALF, HALF), HALF), :]


def gradient_call(facts, squares, base, power, other, measured, probe, far, step, inv):
    first = squares is None
    half = jax.ShapeDtypeStruct((2, HALF, SIDE), f32)
    aliases = {}
    if first:
        args = [facts, power, other, measured, probe, far, *inv]
        out_shape = [half, half]
    else:
        args = [facts, squares, base, power, other, measured, probe, far, step, *inv]
        out_shape = [half, half, FULL, half, jax.ShapeDtypeStruct((8, SIDE), f32)]
        aliases = {7: 2, 2: 3}
    return pl.pallas_call(
        functools.partial(gradient_kernel, first=first),
        in_specs=[SMEM] + [VMEM] * (len(args) - 1),
        out_specs=[VMEM] * len(out_shape),
        out_shape=out_shape,
        input_output_aliases=aliases,
        scratch_shapes=[pltpu.VMEM((2, HALF, SIDE), f32), pltpu.VMEM((2, SIDE, SIDE), f32)],
        compiler_params=params(),
        cost_estimate=pl.CostEstimate(flops=3_400_000_000, bytes_accessed=17_000_000, transcendentals=65536),
        name="window_gradient",
    )(*args)


def merge_kernel(facts_ref, own_ref, a_ref, b_ref, c_ref, *refs, earlier):
    band_ref, square_ref = refs[-2:]
    core, last, initial = facts_ref[1], facts_ref[2], facts_ref[8]

    def wide(x, column):
        x = jnp.concatenate([x, jnp.zeros((HALF, WIDTH - SIDE), f32)], axis=1)
        return pltpu.roll(x, column, 1)

    drop_own = (last == 1) & (core == 1)
    drop_other = (initial == 1) & (core == 0)
    squares = jnp.zeros((8, 128), f32)
    for part in range(2):
        own = wide(own_ref[part], facts_ref[3]) + wide(a_ref[part], facts_ref[4])
        other = wide(b_ref[part], facts_ref[5]) + wide(c_ref[part], facts_ref[6])
        own = jnp.where(drop_own, jnp.zeros_like(own), own)
        other = jnp.where(drop_other, jnp.zeros_like(other), other)
        band = own + other
        band_ref[part] = band
        sq = (band * band).reshape(HALF // 8, 8, WIDTH).sum(axis=0)
        squares = squares + sq[:, 0:128] + sq[:, 128:256] + sq[:, 256:384]
        if earlier:
            factors, bands = refs[:earlier], refs[earlier : 2 * earlier]
            band_ref[2 + part] = sum(f[0:1, 0:1] * g[part] for f, g in zip(factors, bands))
    square_ref[...] = squares


def merge_call(facts, own, a, b, c, factors, bands):
    args = [facts, own, a, b, c, *factors, *bands]
    parts = 4 if factors else 2
    return pl.pallas_call(
        functools.partial(merge_kernel, earlier=len(factors)),
        in_specs=[SMEM] + [VMEM] * (len(args) - 1),
        out_specs=[VMEM, VMEM],
        out_shape=[jax.ShapeDtypeStruct((parts, HALF, WIDTH), f32), SMALL],
        compiler_params=params(),
        cost_estimate=pl.CostEstimate(flops=1_000_000, bytes_accessed=2_000_000, transcendentals=0),
        name="band_sum",
    )(*args)


UPPER = ((0, 2, 3, 3), (2, 0, 1, 2))
LOWER = ((1, 0, 2, 2), (3, 2, 0, 1))


def finish_kernel(facts_ref, squares_ref, field_ref, own_ref, partner_ref, one_ref, two_ref, out_ref):
    i, core = facts_ref[0], facts_ref[1]
    factor = step_factor(squares_ref[...])
    for rows, sources in ((slice(0, HALF), UPPER), (slice(HALF, SIDE), LOWER)):
        for source, ref in enumerate((own_ref, partner_ref, one_ref, two_ref)):
            chosen = [(core == c) & (i == k) for c in range(2) for k in range(4) if sources[c][k] == source]
            here = chosen[0]
            for more in chosen[1:]:
                here = here | more

            @pl.when(here)
            def _():
                for part in range(2):
                    moved = ref[2 + part] + factor * ref[part]
                    out_ref[part, rows] = field_ref[part, rows] + moved


def finish_call(*args):
    return pl.pallas_call(
        finish_kernel,
        in_specs=[SMEM] + [VMEM] * 6,
        out_specs=VMEM,
        out_shape=jax.ShapeDtypeStruct((2, SIDE, WIDTH), f32),
        compiler_params=params(),
        name="finish",
    )(*args)


def take_kernel(ids_ref, probe_ref, measured_ref, own_ref, mine_ref, sems):
    core, window = ids_ref[1], ids_ref[5]
    copies = copy_all(
        [
            (probe_ref.at[0, core], own_ref.at[0]),
            (probe_ref.at[1, core], own_ref.at[1]),
            (measured_ref.at[0, window], mine_ref),
        ],
        sems,
    )
    for copy in copies:
        copy.wait()


def take_call(ids, probe_modes, measured):
    return pl.pallas_call(
        take_kernel,
        in_specs=[SMEM, HBM, HBM],
        out_specs=[VMEM] * 2,
        out_shape=[jax.ShapeDtypeStruct((2, SIDE, SIDE), f32), jax.ShapeDtypeStruct((SIDE, SIDE), f32)],
        scratch_shapes=[pltpu.SemaphoreType.DMA((3,))],
        compiler_params=params(),
        name="take",
    )(ids, probe_modes, measured)


def split_kernel(both_ref, real_ref, imag_ref, sems):
    for copy in copy_all([(both_ref.at[0], real_ref), (both_ref.at[1], imag_ref)], sems):
        copy.wait()


def split_call(both):
    plane = jax.ShapeDtypeStruct((SIDE, SIDE), f32)
    return pl.pallas_call(
        split_kernel,
        in_specs=[ANY],
        out_specs=[VMEM] * 2,
        out_shape=[plane] * 2,
        scratch_shapes=[pltpu.SemaphoreType.DMA((2,))],
        compiler_params=params(),
        name="split",
    )(both)


def body(object_field, probe_modes, measured, positions):
    strip, mode = lax.axis_index("strip"), lax.axis_index("mode")
    core, j = strip % 2, strip // 2
    z, w = mode // 2, mode % 2
    i = jnp.where(j % 2 == 0, z, 3 - z)
    pair = 4 * j + i
    last = (pair == 31).astype(jnp.int32)
    initial = (pair == 0).astype(jnp.int32)
    fwd, inv = tables()
    fwd = [jnp.asarray(t) for t in fwd]
    inv = [jnp.asarray(t) for t in inv]
    shuffle = jnp.asarray(shuffle_table())

    window = jnp.where(i % 2 == 0, 1 + w, 3 * w)
    ids = jnp.stack([i, core, w, last, initial, window, core, core]).astype(jnp.int32)

    own, mine = take_call(ids, probe_modes, measured)
    up, down, side = send(own, Z_UP), send(own, Z_DOWN), send(own, Y_UP)
    opposite, up_side, down_side = send(up, Z_UP), send(up, Y_UP), send(down, Y_DOWN)
    real, imag = split_call(opposite)
    opposite_side = send(real, Y_UP), send(imag, Y_DOWN)

    places = positions[0]
    ring = send(pack_call(ring_pack_kernel, HALF + 8, object_field, places, [own], "ring_pack"), RING)
    pack = pack_call(core_pack_kernel, SIDE + HALF + 16, object_field, places, [ring, up, down, side], "core_pack")
    patch, pattern, facts = pl.pallas_call(
        prepare_kernel,
        in_specs=[SMEM] * 2 + [VMEM] * 6,
        out_specs=[VMEM] * 2 + [SMEM],
        out_shape=[
            jax.ShapeDtypeStruct((2, SIDE, SIDE), f32),
            jax.ShapeDtypeStruct((SIDE, SIDE), f32),
            jax.ShapeDtypeStruct((9,), jnp.int32),
        ],
        scratch_shapes=[pltpu.VMEM((2, 640, WIDTH), f32)],
        compiler_params=params(),
        name="prepare",
    )(ids, places, ring, pack, send(pack, SWAP_CORE), mine, send(mine, SWAP_CORE), shuffle)

    carried = first_call(0, 7, patch, fwd, [own, up, down, side, up_side, down_side, opposite], [])
    far, probe, power = first_call(7, 8, patch, fwd, opposite_side, carried)
    base = squares = step = None
    bands, factors = [], []
    for iteration in range(ITERS):
        other = send(power, SWAP_CORE)
        if iteration == 0:
            keep, give = gradient_call(facts, None, None, power, other, pattern, probe, far, None, inv)
            base = power + other
        else:
            keep, give, far, base, factor = gradient_call(
                facts, squares, base, power, other, pattern, probe, far, step, inv
            )
            factors.append(factor)
        final = iteration + 1 == ITERS
        half = keep + send(give, SWAP_CORE)
        band, squares = merge_call(
            facts,
            half,
            send(half, BAND_A),
            send(half, BAND_B),
            send(half, BAND_C),
            factors if final else [],
            bands if final else [],
        )
        bands.append(band)
        partner = send(band, SWAP_CORE)
        squares = squares + send(squares, SWAP_CORE)
        if final:
            got_one = send(band, FINAL_ONE)
            got_two = send(jnp.where(core == 1, partner, band), FINAL_TWO)
        carried = None
        for stage, route in enumerate(DOUBLING if not final else LAST_DOUBLING):
            arrived = send(squares, route)
            if not final and stage in PIECES:
                begin, end = PIECES[stage]
                carried = advance_call(begin, end, facts, band, partner, probe, far, fwd, squares, carried)
                arrived = arrived + carried[3]
            squares = squares + arrived
        if not final:
            _, step, power, _ = carried
    return finish_call(facts, squares, object_field, band, partner, got_one, got_two)


PIECES = {1: (0, 3), 2: (3, 5), 3: (5, 8)}


def solution(mesh):
    return jax.shard_map(
        body,
        mesh=mesh,
        in_specs=(
            P(None, "strip", None),
            P(None, "mode", None, None),
            P("strip", None, None, None),
            P("strip", None, None),
        ),
        out_specs=P(None, "strip", None),
        check_vma=False,
    )
```

```python
import functools

import jax
import jax.numpy as jnp
import numpy as np
from jax import lax
from jax.experimental import pallas as pl
from jax.experimental.pallas import tpu as pltpu
from jax.sharding import PartitionSpec as P

ITERS = 3
SIDE = 256
HALF = 128
WIDTH = 384
OWN_MODES = 8
REGULARIZER = 0.1
STEP_SCALE = 0.3
EPSILON = 1e-06
CELLS = 4096 * 384
AXES = ("strip", "mode")
f32, bf16 = jnp.float32, jnp.bfloat16


def place(index):
    strip, mode = divmod(index, 8)
    core, j = strip % 2, strip // 2
    z, w = divmod(mode, 2)
    i = z if j % 2 == 0 else 3 - z
    return 4 * j + i, w, core


def device_of(pair, w, core):
    j, i = divmod(pair % 32, 4)
    z = i if j % 2 == 0 else 3 - i
    return (2 * j + core) * 8 + 2 * z + w


def route_pairs(move):
    return [(d, device_of(*move(*place(d)))) for d in range(128)]


def route_grid(move):
    route = []
    for d in range(128):
        strip, mode = divmod(d, 8)
        core, x, y_hi = strip % 2, strip // 2 % 4, strip // 8
        z, y_lo = divmod(mode, 2)
        y, x, z = move(2 * y_hi + y_lo, x, z)
        y, x, z = y % 4, x % 4, z % 4
        route.append((d, (((y // 2) * 4 + x) * 2 + core) * 8 + 2 * z + y % 2))
    return route


SWAP_CORE = route_pairs(lambda p, w, c: (p, w, 1 - c))
BAND_A = route_pairs(lambda p, w, c: (p, 1 - w, c))
BAND_B = route_pairs(lambda p, w, c: (p + 2 * c - 1, w, 1 - c))
BAND_C = route_pairs(lambda p, w, c: (p + 2 * c - 1, 1 - w, 1 - c))
Z_UP = route_grid(lambda y, x, z: (y, x, z + 1))
Z_DOWN = route_grid(lambda y, x, z: (y, x, z - 1))
Y_UP = route_grid(lambda y, x, z: (y + 1, x, z))
Y_DOWN = route_grid(lambda y, x, z: (y - 1, x, z))
DOUBLING = [
    route_grid(lambda y, x, z: (y, x, z ^ 1)),
    route_grid(lambda y, x, z: (y, x ^ 1, z)),
    route_grid(lambda y, x, z: (y ^ 2, x, z)),
    route_grid(lambda y, x, z: (y, x ^ 2, z)),
    route_grid(lambda y, x, z: (y, x, z ^ 2)),
]

LAST_DOUBLING = [DOUBLING[k] for k in (1, 2, 3, 0, 4)]


def ring_route():
    route = []
    for j in range(8):
        for mode in range(8):
            low, high = (2 * j + 1) * 8 + mode, (2 * ((j + 1) % 8)) * 8 + mode
            route += [(low, high), (high, low)]
    return route


RING = ring_route()


def final_routes():
    one, two = [], []
    for j in range(8):
        for w in range(2):

            def at(i, c):
                return device_of(4 * j + i, w, c)

            one += [
                (at(0, 0), at(1, 0)),
                (at(1, 0), at(2, 0)),
                (at(0, 1), at(3, 0)),
                (at(2, 1), at(1, 1)),
                (at(2, 0), at(3, 1)),
                (at(1, 1), at(0, 1)),
            ]
            two += [(at(0, 0), at(2, 0)), (at(0, 1), at(3, 0)), (at(3, 0), at(0, 1))]
    return one, two


FINAL_ONE, FINAL_TWO = final_routes()


def send(value, route):
    return lax.ppermute(value, AXES, route)


def table(parity):
    n = np.arange(HALF)
    turns = (n[:, None] * (2 * n[None, :] + parity)) % SIDE
    angle = -2.0 * np.pi * turns / SIDE
    real, imag = np.cos(angle) / 16.0, np.sin(angle) / 16.0
    return np.block([[real, imag], [-imag, real]])


def tables():
    right, left = [], []
    for parity in range(2):
        t = table(parity)
        high = t.astype(np.float32).astype(jnp.bfloat16)
        low = (t - high.astype(np.float64)).astype(np.float32).astype(jnp.bfloat16)
        right.append(np.concatenate([high, high, low], axis=0))
        left.append(np.concatenate([high, high, low], axis=1))
    turned_right = [np.concatenate([r[:256].T, r[:256].T, r[512:].T], axis=0) for r in right]
    turned_left = [np.concatenate([r[:256].T, r[:256].T, r[512:].T], axis=1) for r in right]
    forward = (np.stack(right), np.stack(turned_left))
    inverse = (np.stack(left), np.stack(turned_right))
    return forward, inverse


def shuffle_table():
    rows = np.arange(SIDE)
    take = 2 * (rows % HALF) + rows // HALF
    return (take[:, None] == np.arange(SIDE)[None, :]).astype(jnp.bfloat16)


def halves(x):
    high = x.astype(bf16)
    low = (x - high.astype(f32)).astype(bf16)
    return high, low


def times_right(x, tab):
    high, low = halves(x)
    return jnp.dot(jnp.concatenate([high, low, high], axis=1), tab, preferred_element_type=f32)


def times_left(tab, x):
    high, low = halves(x)
    return jnp.dot(tab, jnp.concatenate([high, low, high], axis=0), preferred_element_type=f32)


def forward_transform(real, imag, cols, rows):
    stage = []
    for sign in (1.0, -1.0):
        if sign > 0:
            r, i = real[:, :HALF] + real[:, HALF:], imag[:, :HALF] + imag[:, HALF:]
        else:
            r, i = real[:, :HALF] - real[:, HALF:], imag[:, :HALF] - imag[:, HALF:]
        stage.append(times_right(jnp.concatenate([r, i], axis=1), cols[0 if sign > 0 else 1]))
    even, odd = stage
    top = [even[:HALF], odd[:HALF]]
    bottom = [even[HALF:], odd[HALF:]]
    out = []
    for parity in range(2):
        if parity == 0:
            mixed = [t + b for t, b in zip(top, bottom)]
        else:
            mixed = [t - b for t, b in zip(top, bottom)]
        block = jnp.concatenate(
            [
                jnp.concatenate([m[:, :HALF] for m in mixed], axis=1),
                jnp.concatenate([m[:, HALF:] for m in mixed], axis=1),
            ],
            axis=0,
        )
        out.append(times_left(rows[parity], block))
    return out


def inverse_transform(far_even, far_odd, rows, cols):
    b0 = times_left(rows[0], far_even)
    b1 = times_left(rows[1], far_odd)
    plus, minus = b0 + b1, b0 - b1
    c = []
    for q in range(2):
        lanes = slice(q * HALF, (q + 1) * HALF)
        real = jnp.concatenate([plus[:HALF, lanes], minus[:HALF, lanes]], axis=0)
        imag = jnp.concatenate([plus[HALF:, lanes], minus[HALF:, lanes]], axis=0)
        c.append(times_right(jnp.concatenate([real, imag], axis=1), cols[q]))
    real = jnp.concatenate([c[0][:, :HALF] + c[1][:, :HALF], c[0][:, :HALF] - c[1][:, :HALF]], axis=1)
    imag = jnp.concatenate([c[0][:, HALF:] + c[1][:, HALF:], c[0][:, HALF:] - c[1][:, HALF:]], axis=1)
    return real, imag


def cut_columns(x, column):
    return pltpu.roll(x, lax.rem(WIDTH - column, WIDTH), 1)[:, :SIDE]


VMEM = pl.BlockSpec(memory_space=pltpu.VMEM)
SMEM = pl.BlockSpec(memory_space=pltpu.SMEM)
ANY = pl.BlockSpec(memory_space=pl.ANY)
HBM = pl.BlockSpec(memory_space=pltpu.HBM)


def params(mebibytes=12):
    return pltpu.CompilerParams(vmem_limit_bytes=mebibytes * 1024 * 1024)


def copy_all(pairs, sems):
    copies = [pltpu.make_async_copy(source, target, sems.at[k]) for k, (source, target) in enumerate(pairs)]
    for copy in copies:
        copy.start()
    return copies


def write_columns(places_ref, out_ref, row):
    for k in range(4):
        column = places_ref[k, 1].astype(f32)
        out_ref[0, row + k : row + k + 1] = jnp.full((1, WIDTH), column, f32)
        out_ref[1, row + k : row + k + 1] = jnp.full((1, WIDTH), column, f32)
    out_ref[:, row + 4 : row + 8] = jnp.zeros((2, 4, WIDTH), f32)


def ring_pack_kernel(field_ref, places_ref, *refs):
    out_ref, sems = refs[-2:]
    copies = copy_all([(field_ref.at[:, pl.ds(0, HALF)], out_ref.at[:, pl.ds(0, HALF)])], sems)
    write_columns(places_ref, out_ref, HALF)
    for copy in copies:
        copy.wait()


def core_pack_kernel(field_ref, places_ref, ring_ref, *refs):
    out_ref, sems = refs[-2:]
    copies = copy_all(
        [(field_ref, out_ref.at[:, pl.ds(0, SIDE)]), (ring_ref, out_ref.at[:, pl.ds(SIDE, HALF + 8)])], sems
    )
    write_columns(places_ref, out_ref, SIDE + HALF + 8)
    for copy in copies:
        copy.wait()


def pack_call(kernel, rows, field, places, others, name):
    return pl.pallas_call(
        kernel,
        in_specs=[HBM, SMEM] + [ANY] * len(others),
        out_specs=VMEM,
        out_shape=jax.ShapeDtypeStruct((2, rows, WIDTH), f32),
        scratch_shapes=[pltpu.SemaphoreType.DMA((2,))],
        compiler_params=params(),
        name=name,
    )(field, places, *others)


def prepare_kernel(ids_ref, places_ref, ring_ref, mine_pack_ref, pack_ref, mine_ref, other_ref, shuffle_ref,
                   patch_ref, measured_ref, facts_ref, tall):
    i, core, w, last = ids_ref[0], ids_ref[1], ids_ref[2], ids_ref[3]

    def listed(ref, row):
        return [jnp.max(ref[0, row + k : row + k + 1, 0:128]).astype(jnp.int32) for k in range(4)]

    partner_columns = listed(pack_ref, SIDE + HALF + 8)
    ring_columns = listed(ring_ref, HALF)

    def pick(values, k):
        return jnp.where(k == 0, values[0], jnp.where(k == 1, values[1], jnp.where(k == 2, values[2], values[3])))

    def column(i, w):
        k = jnp.where(lax.rem(i + 4, 2) == 0, 1 + w, 3 * w)
        block = jnp.where(i < 2, 0, 1)
        near = jnp.where(block == core, places_ref[k, 1], pick(partner_columns, k))
        return jnp.where((i < 0) | (i > 3), pick(ring_columns, k), near)

    other = i + 2 * core - 1
    own_column = column(i, w)
    facts_ref[0] = i
    facts_ref[1] = core
    facts_ref[2] = last
    facts_ref[3] = own_column
    facts_ref[4] = column(i, 1 - w)
    facts_ref[5] = column(other, w)
    facts_ref[6] = column(other, 1 - w)
    facts_ref[7] = 0
    facts_ref[8] = ids_ref[4]
    for part in range(2):
        own, partner = mine_pack_ref[part, 0:SIDE], pack_ref[part, 0:SIDE]
        tall[part, 0:256] = jnp.where(core == 0, own, partner)
        tall[part, 256:512] = jnp.where(core == 0, partner, own)
        below = jnp.where(core == 0, pack_ref[part, SIDE : SIDE + HALF], ring_ref[part, 0:HALF])
        tall[part, 512:640] = jnp.where(last == 1, jnp.zeros_like(below), below)
        rows = tall[part, pl.ds(pl.multiple_of(i * HALF, HALF), SIDE), :]
        patch_ref[part] = cut_columns(rows, own_column)
    block = jnp.where(i < 2, 0, 1)
    window = jnp.where(block == core, mine_ref[...], other_ref[...])
    shuffle = shuffle_ref[...]
    h0 = window.astype(bf16)
    rest = window - h0.astype(f32)
    h1 = rest.astype(bf16)
    h2 = (rest - h1.astype(f32)).astype(bf16)
    moved = []
    for piece in (h0, h1, h2):
        rows = jnp.dot(shuffle, piece, preferred_element_type=f32).astype(bf16)
        moved.append(lax.dot_general(rows, shuffle, (((1,), (1,)), ((), ())), preferred_element_type=f32))
    measured_ref[...] = moved[0] + moved[1] + moved[2]


def power_of(far):
    return far[:HALF] * far[:HALF] + far[HALF:] * far[HALF:]


def first_kernel(patch_ref, cols_ref, rows_ref, *refs, begin, end):
    far_ref, probe_ref, power_ref, sems = refs[-4:]
    if begin == 0:
        copies = copy_all([(refs[m], probe_ref.at[m]) for m in range(end)], sems)
    else:
        copies = copy_all([(refs[k], probe_ref.at[begin, k]) for k in range(2)], sems)
        power_ref[...] = refs[4][...]
    xr, xi = patch_ref[0], patch_ref[1]
    for m in range(begin, end):
        if begin == 0:
            copies[m].wait()
        else:
            copies[0].wait()
            copies[1].wait()
        pr, pi = probe_ref[m, 0], probe_ref[m, 1]
        far = forward_transform(pr * xr - pi * xi, pr * xi + pi * xr, cols_ref, rows_ref)
        for parity in range(2):
            far_ref[m, parity] = far[parity]
            power = power_of(far[parity])
            power_ref[parity] = power if m == 0 else power_ref[parity] + power


FULL = jax.ShapeDtypeStruct((OWN_MODES, 2, SIDE, SIDE), f32)


def first_call(begin, end, patch, fwd, arrays, carried):
    args = [patch, *fwd, *arrays]
    in_specs = [VMEM] * 3 + [ANY] * len(arrays)
    aliases = {}
    if carried:
        aliases = {len(args) + k: k for k in range(2)}
        args += carried
        in_specs += [VMEM] * 3
    return pl.pallas_call(
        functools.partial(first_kernel, begin=begin, end=end),
        in_specs=in_specs,
        out_specs=[VMEM] * 3,
        out_shape=[FULL, FULL, jax.ShapeDtypeStruct((2, HALF, SIDE), f32)],
        input_output_aliases=aliases,
        scratch_shapes=[pltpu.SemaphoreType.DMA((8,))],
        compiler_params=params(),
        cost_estimate=pl.CostEstimate(flops=800_000_000 * (end - begin), bytes_accessed=3_000_000, transcendentals=0),
        name="first_far",
    )(*args)


def advance_kernel(*refs, begin, end, first):
    if first:
        facts_ref, mine_ref, other_ref, probe_ref, far_ref, cols_ref, rows_ref, _, patch, step_ref, powers_ref, token_ref = refs
        core, last, column = facts_ref[1], facts_ref[2], facts_ref[3]
        for part in range(2):
            mine, other = mine_ref[part], other_ref[part]
            top = jnp.where(core == 0, mine, other)
            bottom = jnp.where(core == 0, other, mine)
            bottom = jnp.where(last == 1, jnp.zeros_like(bottom), bottom)
            patch[part, 0:HALF] = cut_columns(top, column)
            patch[part, HALF:] = cut_columns(bottom, column)
        powers_ref[...] = jnp.zeros_like(powers_ref)
    else:
        patch, probe_ref, far_ref, cols_ref, rows_ref, _, _, powers_in_ref, step_ref, powers_ref, token_ref = refs
        powers_ref[...] = powers_in_ref[...]
    token_ref[...] = jnp.zeros_like(token_ref)

    for m in range(begin, end):
        pr, pi = probe_ref[m, 0], probe_ref[m, 1]
        xr, xi = patch[0], patch[1]
        step = forward_transform(pr * xr - pi * xi, pr * xi + pi * xr, cols_ref, rows_ref)
        for parity in range(2):
            step_ref[m, parity] = step[parity]
            far = far_ref[m, parity]
            cross = far * step[parity]
            powers_ref[0, parity] += cross[:HALF] + cross[HALF:]
            powers_ref[1, parity] += power_of(step[parity])


UNROLL = 8
SMALL = jax.ShapeDtypeStruct((8, 128), f32)


def advance_call(begin, end, facts, mine, other, probe, far, fwd, after, carried):
    powers = jax.ShapeDtypeStruct((2, 2, HALF, SIDE), f32)
    first = carried is None
    aliases = {}
    if first:
        args = [facts, mine, other, probe, far, *fwd, after]
        in_specs = [SMEM] + [VMEM] * 6 + [ANY]
        out_shape = [jax.ShapeDtypeStruct((2, SIDE, SIDE), f32), FULL, powers, SMALL]
    else:
        args = [carried[0], probe, far, *fwd, after, carried[1], carried[2]]
        in_specs = [VMEM] * 5 + [ANY] + [VMEM] * 2
        out_shape = [FULL, powers, SMALL]
        aliases = {6: 0, 7: 1}
    out = pl.pallas_call(
        functools.partial(advance_kernel, begin=begin, end=end, first=first),
        in_specs=in_specs,
        out_specs=[VMEM] * len(out_shape),
        out_shape=out_shape,
        input_output_aliases=aliases,
        compiler_params=params(),
        cost_estimate=pl.CostEstimate(flops=800_000_000 * (end - begin), bytes_accessed=3_000_000, transcendentals=0),
        name="far_step",
    )(*args)
    return out if first else [carried[0], *out]


def step_factor(squares, times=1):
    square_sum = jnp.sum(jnp.sum(squares, axis=0, keepdims=True), axis=1, keepdims=True)
    return STEP_SCALE / jnp.sqrt(square_sum / (times * CELLS) + EPSILON)


def gradient_kernel(*refs, first):
    if first:
        facts_ref, power_ref, other_ref, measured_ref, probe_ref, far_ref, rows_ref, cols_ref, keep_ref, give_ref, change, total = refs
    else:
        (facts_ref, squares_ref, base_ref, power_ref, other_ref, measured_ref, probe_ref, far_ref, step_ref, rows_ref, cols_ref,
         keep_ref, give_ref, far_out_ref, base_out_ref, factor_ref, change, total) = refs
        factor_ref[...] = jnp.broadcast_to(step_factor(squares_ref[...]), (8, SIDE))
        factor = factor_ref[0:1]
    for parity in range(2):
        rows = slice(parity * HALF, (parity + 1) * HALF)
        if first:
            power = power_ref[parity] + other_ref[parity]
        else:
            cross = power_ref[0, parity] + other_ref[0, parity]
            square = power_ref[1, parity] + other_ref[1, parity]
            power = jnp.maximum(base_ref[parity] + factor * (2.0 * cross + factor * square), 0.0)
            base_out_ref[parity] = power
        ratio = (measured_ref[rows] + REGULARIZER) / (power + REGULARIZER)
        change[parity] = jnp.sqrt(ratio) - 1.0
    total[...] = jnp.zeros_like(total)

    def one(m, carry):
        shifted = []
        for parity in range(2):
            far = far_ref[m, parity]
            if not first:
                far = far + factor_ref[0:1] * step_ref[m, parity]
                far_out_ref[m, parity] = far
            c = change[parity]
            shifted.append(jnp.concatenate([far[:HALF] * c, far[HALF:] * c], axis=0))
        dr, di = inverse_transform(shifted[0], shifted[1], rows_ref, cols_ref)
        pr, pi = probe_ref[m, 0], probe_ref[m, 1]
        total[0] += pr * dr + pi * di
        total[1] += pr * di - pi * dr
        return carry

    lax.fori_loop(0, OWN_MODES, one, 0, unroll=UNROLL)
    core = facts_ref[1]
    keep_ref[...] = total[:, pl.ds(pl.multiple_of(core * HALF, HALF), HALF), :]
    give_ref[...] = total[:, pl.ds(pl.multiple_of((1 - core) * HALF, HALF), HALF), :]


def gradient_call(facts, squares, base, power, other, measured, probe, far, step, inv):
    first = squares is None
    half = jax.ShapeDtypeStruct((2, HALF, SIDE), f32)
    aliases = {}
    if first:
        args = [facts, power, other, measured, probe, far, *inv]
        out_shape = [half, half]
    else:
        args = [facts, squares, base, power, other, measured, probe, far, step, *inv]
        out_shape = [half, half, FULL, half]
        aliases = {7: 2, 2: 3}
    return pl.pallas_call(
        functools.partial(gradient_kernel, first=first),
        in_specs=[SMEM] + [VMEM] * (len(args) - 1),
        out_specs=[VMEM] * len(out_shape),
        out_shape=out_shape,
        input_output_aliases=aliases,
        scratch_shapes=[pltpu.VMEM((8, SIDE), f32)] * (not first)
        + [pltpu.VMEM((2, HALF, SIDE), f32), pltpu.VMEM((2, SIDE, SIDE), f32)],
        compiler_params=params(),
        cost_estimate=pl.CostEstimate(flops=3_400_000_000, bytes_accessed=17_000_000, transcendentals=65536),
        name="window_gradient",
    )(*args)


def merge_kernel(facts_ref, own_ref, a_ref, b_ref, c_ref, *refs, earlier):
    band_ref, square_ref = refs[-2:]
    core, last, initial = facts_ref[1], facts_ref[2], facts_ref[8]

    def wide(x, column):
        x = jnp.concatenate([x, jnp.zeros((HALF, WIDTH - SIDE), f32)], axis=1)
        return pltpu.roll(x, column, 1)

    drop_own = (last == 1) & (core == 1)
    drop_other = (initial == 1) & (core == 0)
    squares = jnp.zeros((8, 128), f32)
    for part in range(2):
        own = wide(own_ref[part], facts_ref[3]) + wide(a_ref[part], facts_ref[4])
        other = wide(b_ref[part], facts_ref[5]) + wide(c_ref[part], facts_ref[6])
        own = jnp.where(drop_own, jnp.zeros_like(own), own)
        other = jnp.where(drop_other, jnp.zeros_like(other), other)
        band = own + other
        band_ref[part] = band
        sq = (band * band).reshape(HALF // 8, 8, WIDTH).sum(axis=0)
        squares = squares + sq[:, 0:128] + sq[:, 128:256] + sq[:, 256:384]
        if earlier:
            totals, bands = refs[0], refs[1 : 1 + earlier]
            factors = [step_factor(totals[8 * k : 8 * k + 8], 2) for k in range(earlier)]
            band_ref[2 + part] = sum(f * g[part] for f, g in zip(factors, bands))
    square_ref[...] = squares


def merge_call(facts, own, a, b, c, totals, bands):
    args = [facts, own, a, b, c, *totals, *bands]
    parts = 4 if bands else 2
    return pl.pallas_call(
        functools.partial(merge_kernel, earlier=len(bands)),
        in_specs=[SMEM] + [VMEM] * (len(args) - 1),
        out_specs=[VMEM, VMEM],
        out_shape=[jax.ShapeDtypeStruct((parts, HALF, WIDTH), f32), SMALL],
        compiler_params=params(),
        cost_estimate=pl.CostEstimate(flops=1_000_000, bytes_accessed=2_000_000, transcendentals=0),
        name="band_sum",
    )(*args)


def choose_kernel(facts_ref, own_ref, partner_ref, _, out_ref):
    core = facts_ref[1]

    @pl.when(core == 0)
    def _():
        out_ref[...] = own_ref[...]

    @pl.when(core == 1)
    def _():
        out_ref[...] = partner_ref[...]


def choose_call(facts, own, partner, after):
    return pl.pallas_call(
        choose_kernel,
        in_specs=[SMEM, VMEM, VMEM, ANY],
        out_specs=VMEM,
        out_shape=jax.ShapeDtypeStruct((4, HALF, WIDTH), f32),
        compiler_params=params(),
        name="choose",
    )(facts, own, partner, after)


UPPER = ((0, 2, 3, 3), (2, 0, 1, 2))
LOWER = ((1, 0, 2, 2), (3, 2, 0, 1))


def finish_kernel(facts_ref, squares_ref, field_ref, own_ref, partner_ref, one_ref, two_ref, out_ref):
    i, core = facts_ref[0], facts_ref[1]
    factor = step_factor(squares_ref[...], 2)
    for rows, sources in ((slice(0, HALF), UPPER), (slice(HALF, SIDE), LOWER)):
        for source, ref in enumerate((own_ref, partner_ref, one_ref, two_ref)):
            chosen = [(core == c) & (i == k) for c in range(2) for k in range(4) if sources[c][k] == source]
            here = chosen[0]
            for more in chosen[1:]:
                here = here | more

            @pl.when(here)
            def _():
                for part in range(2):
                    moved = ref[2 + part] + factor * ref[part]
                    out_ref[part, rows] = field_ref[part, rows] + moved


def finish_call(*args):
    return pl.pallas_call(
        finish_kernel,
        in_specs=[SMEM] + [VMEM] * 6,
        out_specs=VMEM,
        out_shape=jax.ShapeDtypeStruct((2, SIDE, WIDTH), f32),
        compiler_params=params(),
        name="finish",
    )(*args)


def take_kernel(ids_ref, probe_ref, measured_ref, own_ref, mine_ref, sems):
    core, window = ids_ref[1], ids_ref[5]
    copies = copy_all(
        [
            (probe_ref.at[0, core], own_ref.at[0]),
            (probe_ref.at[1, core], own_ref.at[1]),
            (measured_ref.at[0, window], mine_ref),
        ],
        sems,
    )
    for copy in copies:
        copy.wait()


def take_call(ids, probe_modes, measured):
    return pl.pallas_call(
        take_kernel,
        in_specs=[SMEM, HBM, HBM],
        out_specs=[VMEM] * 2,
        out_shape=[jax.ShapeDtypeStruct((2, SIDE, SIDE), f32), jax.ShapeDtypeStruct((SIDE, SIDE), f32)],
        scratch_shapes=[pltpu.SemaphoreType.DMA((3,))],
        compiler_params=params(),
        name="take",
    )(ids, probe_modes, measured)


def split_kernel(both_ref, real_ref, imag_ref, sems):
    for copy in copy_all([(both_ref.at[0], real_ref), (both_ref.at[1], imag_ref)], sems):
        copy.wait()


def split_call(both):
    plane = jax.ShapeDtypeStruct((SIDE, SIDE), f32)
    return pl.pallas_call(
        split_kernel,
        in_specs=[ANY],
        out_specs=[VMEM] * 2,
        out_shape=[plane] * 2,
        scratch_shapes=[pltpu.SemaphoreType.DMA((2,))],
        compiler_params=params(),
        name="split",
    )(both)


def body(object_field, probe_modes, measured, positions):
    strip, mode = lax.axis_index("strip"), lax.axis_index("mode")
    core, j = strip % 2, strip // 2
    z, w = mode // 2, mode % 2
    i = jnp.where(j % 2 == 0, z, 3 - z)
    pair = 4 * j + i
    last = (pair == 31).astype(jnp.int32)
    initial = (pair == 0).astype(jnp.int32)
    fwd, inv = tables()
    fwd = [jnp.asarray(t) for t in fwd]
    inv = [jnp.asarray(t) for t in inv]
    shuffle = jnp.asarray(shuffle_table())

    window = jnp.where(i % 2 == 0, 1 + w, 3 * w)
    ids = jnp.stack([i, core, w, last, initial, window, core, core]).astype(jnp.int32)

    own, mine = take_call(ids, probe_modes, measured)
    up, down, side = send(own, Z_UP), send(own, Z_DOWN), send(own, Y_UP)
    opposite, up_side, down_side = send(up, Z_UP), send(up, Y_UP), send(down, Y_DOWN)
    real, imag = split_call(opposite)
    opposite_side = send(real, Y_UP), send(imag, Y_DOWN)

    places = positions[0]
    ring = send(pack_call(ring_pack_kernel, HALF + 8, object_field, places, [own], "ring_pack"), RING)
    pack = pack_call(core_pack_kernel, SIDE + HALF + 16, object_field, places, [ring, up, down, side], "core_pack")
    patch, pattern, facts = pl.pallas_call(
        prepare_kernel,
        in_specs=[SMEM] * 2 + [VMEM] * 6,
        out_specs=[VMEM] * 2 + [SMEM],
        out_shape=[
            jax.ShapeDtypeStruct((2, SIDE, SIDE), f32),
            jax.ShapeDtypeStruct((SIDE, SIDE), f32),
            jax.ShapeDtypeStruct((9,), jnp.int32),
        ],
        scratch_shapes=[pltpu.VMEM((2, 640, WIDTH), f32)],
        compiler_params=params(),
        name="prepare",
    )(ids, places, ring, pack, send(pack, SWAP_CORE), mine, send(mine, SWAP_CORE), shuffle)

    carried = first_call(0, 7, patch, fwd, [own, up, down, side, up_side, down_side, opposite], [])
    far, probe, power = first_call(7, 8, patch, fwd, opposite_side, carried)
    base = squares = step = None
    bands, totals = [], []
    for iteration in range(ITERS):
        other = send(power, SWAP_CORE)
        if iteration == 0:
            keep, give = gradient_call(facts, None, None, power, other, pattern, probe, far, None, inv)
            base = power + other
        else:
            keep, give, far, base = gradient_call(
                facts, squares, base, power, other, pattern, probe, far, step, inv
            )
            totals.append(squares)
        final = iteration + 1 == ITERS
        if final:
            stacked = jnp.concatenate(totals, axis=0)
            stacked = stacked + send(stacked, SWAP_CORE)
        half = keep + send(give, SWAP_CORE)
        band, squares = merge_call(
            facts,
            half,
            send(half, BAND_A),
            send(half, BAND_B),
            send(half, BAND_C),
            [stacked] if final else [],
            bands if final else [],
        )
        bands.append(band)
        partner = send(band, SWAP_CORE)
        if final:
            squares = squares + send(squares, SWAP_CORE)
            got_one = send(band, FINAL_ONE)
        carried = None
        for stage, route in enumerate(DOUBLING if not final else LAST_DOUBLING):
            arrived = send(squares, route)
            if not final and stage in PIECES:
                begin, end = PIECES[stage]
                carried = advance_call(begin, end, facts, band, partner, probe, far, fwd, squares, carried)
                arrived = arrived + carried[3]
            squares = squares + arrived
            if final and stage == 0:
                got_two = send(choose_call(facts, band, partner, squares), FINAL_TWO)
        if not final:
            _, step, power, _ = carried
    return finish_call(facts, squares, object_field, band, partner, got_one, got_two)


PIECES = {1: (0, 5), 2: (5, 7), 3: (7, 8)}


def solution(mesh):
    return jax.shard_map(
        body,
        mesh=mesh,
        in_specs=(
            P(None, "strip", None),
            P(None, "mode", None, None),
            P("strip", None, None, None),
            P("strip", None, None),
        ),
        out_specs=P(None, "strip", None),
        check_vma=False,
    )
```

```python
import functools

import jax
import jax.numpy as jnp
import numpy as np
from jax import lax
from jax.experimental import pallas as pl
from jax.experimental.pallas import tpu as pltpu
from jax.sharding import PartitionSpec as P

ITERS = 3
SIDE = 256
HALF = 128
WIDTH = 384
OWN_MODES = 8
REGULARIZER = 0.1
STEP_SCALE = 0.3
EPSILON = 1e-06
CELLS = 4096 * 384
AXES = ("strip", "mode")
f32, bf16 = jnp.float32, jnp.bfloat16


def place(index):
    strip, mode = divmod(index, 8)
    core, j = strip % 2, strip // 2
    z, w = divmod(mode, 2)
    i = z if j % 2 == 0 else 3 - z
    return 4 * j + i, w, core


def device_of(pair, w, core):
    j, i = divmod(pair % 32, 4)
    z = i if j % 2 == 0 else 3 - i
    return (2 * j + core) * 8 + 2 * z + w


def route_pairs(move):
    return [(d, device_of(*move(*place(d)))) for d in range(128)]


def route_grid(move):
    route = []
    for d in range(128):
        strip, mode = divmod(d, 8)
        core, x, y_hi = strip % 2, strip // 2 % 4, strip // 8
        z, y_lo = divmod(mode, 2)
        y, x, z = move(2 * y_hi + y_lo, x, z)
        y, x, z = y % 4, x % 4, z % 4
        route.append((d, (((y // 2) * 4 + x) * 2 + core) * 8 + 2 * z + y % 2))
    return route


SWAP_CORE = route_pairs(lambda p, w, c: (p, w, 1 - c))
BAND_A = route_pairs(lambda p, w, c: (p, 1 - w, c))
BAND_B = route_pairs(lambda p, w, c: (p + 2 * c - 1, w, 1 - c))
BAND_C = route_pairs(lambda p, w, c: (p + 2 * c - 1, 1 - w, 1 - c))
Z_UP = route_grid(lambda y, x, z: (y, x, z + 1))
Z_DOWN = route_grid(lambda y, x, z: (y, x, z - 1))
Y_UP = route_grid(lambda y, x, z: (y + 1, x, z))
Y_DOWN = route_grid(lambda y, x, z: (y - 1, x, z))
DOUBLING = [
    route_grid(lambda y, x, z: (y, x, z ^ 1)),
    route_grid(lambda y, x, z: (y, x ^ 1, z)),
    route_grid(lambda y, x, z: (y ^ 2, x, z)),
    route_grid(lambda y, x, z: (y, x ^ 2, z)),
    route_grid(lambda y, x, z: (y, x, z ^ 2)),
]

LAST_DOUBLING = [DOUBLING[k] for k in (1, 2, 3, 0, 4)]


def ring_route():
    route = []
    for j in range(8):
        for mode in range(8):
            low, high = (2 * j + 1) * 8 + mode, (2 * ((j + 1) % 8)) * 8 + mode
            route += [(low, high), (high, low)]
    return route


RING = ring_route()


def final_routes():
    one, two = [], []
    for j in range(8):
        for w in range(2):

            def at(i, c):
                return device_of(4 * j + i, w, c)

            one += [
                (at(0, 0), at(1, 0)),
                (at(1, 0), at(2, 0)),
                (at(0, 1), at(3, 0)),
                (at(2, 1), at(1, 1)),
                (at(2, 0), at(3, 1)),
                (at(1, 1), at(0, 1)),
            ]
            two += [(at(0, 0), at(2, 0)), (at(0, 1), at(3, 0)), (at(3, 0), at(0, 1))]
    return one, two


FINAL_ONE, FINAL_TWO = final_routes()


def send(value, route):
    return lax.ppermute(value, AXES, route)


def table(parity):
    n = np.arange(HALF)
    turns = (n[:, None] * (2 * n[None, :] + parity)) % SIDE
    angle = -2.0 * np.pi * turns / SIDE
    real, imag = np.cos(angle) / 16.0, np.sin(angle) / 16.0
    return np.block([[real, imag], [-imag, real]])


def tables():
    right, left = [], []
    for parity in range(2):
        t = table(parity)
        high = t.astype(np.float32).astype(jnp.bfloat16)
        low = (t - high.astype(np.float64)).astype(np.float32).astype(jnp.bfloat16)
        right.append(np.concatenate([high, high, low], axis=0))
        left.append(np.concatenate([high, high, low], axis=1))
    turned_right = [np.concatenate([r[:256].T, r[:256].T, r[512:].T], axis=0) for r in right]
    turned_left = [np.concatenate([r[:256].T, r[:256].T, r[512:].T], axis=1) for r in right]
    forward = (np.stack(right), np.stack(turned_left))
    inverse = (np.stack(left), np.stack(turned_right))
    return forward, inverse


def shuffle_table():
    rows = np.arange(SIDE)
    take = 2 * (rows % HALF) + rows // HALF
    return (take[:, None] == np.arange(SIDE)[None, :]).astype(jnp.bfloat16)


def halves(x):
    high = x.astype(bf16)
    low = (x - high.astype(f32)).astype(bf16)
    return high, low


def times_right(x, tab):
    high, low = halves(x)
    return jnp.dot(jnp.concatenate([high, low, high], axis=1), tab, preferred_element_type=f32)


def times_left(tab, x):
    high, low = halves(x)
    return jnp.dot(tab, jnp.concatenate([high, low, high], axis=0), preferred_element_type=f32)


def forward_transform(real, imag, cols, rows):
    stage = []
    for sign in (1.0, -1.0):
        if sign > 0:
            r, i = real[:, :HALF] + real[:, HALF:], imag[:, :HALF] + imag[:, HALF:]
        else:
            r, i = real[:, :HALF] - real[:, HALF:], imag[:, :HALF] - imag[:, HALF:]
        stage.append(times_right(jnp.concatenate([r, i], axis=1), cols[0 if sign > 0 else 1]))
    even, odd = stage
    top = [even[:HALF], odd[:HALF]]
    bottom = [even[HALF:], odd[HALF:]]
    out = []
    for parity in range(2):
        if parity == 0:
            mixed = [t + b for t, b in zip(top, bottom)]
        else:
            mixed = [t - b for t, b in zip(top, bottom)]
        block = jnp.concatenate(
            [
                jnp.concatenate([m[:, :HALF] for m in mixed], axis=1),
                jnp.concatenate([m[:, HALF:] for m in mixed], axis=1),
            ],
            axis=0,
        )
        out.append(times_left(rows[parity], block))
    return out


def inverse_transform(far_even, far_odd, rows, cols):
    b0 = times_left(rows[0], far_even)
    b1 = times_left(rows[1], far_odd)
    plus, minus = b0 + b1, b0 - b1
    c = []
    for q in range(2):
        lanes = slice(q * HALF, (q + 1) * HALF)
        real = jnp.concatenate([plus[:HALF, lanes], minus[:HALF, lanes]], axis=0)
        imag = jnp.concatenate([plus[HALF:, lanes], minus[HALF:, lanes]], axis=0)
        c.append(times_right(jnp.concatenate([real, imag], axis=1), cols[q]))
    real = jnp.concatenate([c[0][:, :HALF] + c[1][:, :HALF], c[0][:, :HALF] - c[1][:, :HALF]], axis=1)
    imag = jnp.concatenate([c[0][:, HALF:] + c[1][:, HALF:], c[0][:, HALF:] - c[1][:, HALF:]], axis=1)
    return real, imag


def cut_columns(x, column):
    return pltpu.roll(x, lax.rem(WIDTH - column, WIDTH), 1)[:, :SIDE]


VMEM = pl.BlockSpec(memory_space=pltpu.VMEM)
SMEM = pl.BlockSpec(memory_space=pltpu.SMEM)
ANY = pl.BlockSpec(memory_space=pl.ANY)
HBM = pl.BlockSpec(memory_space=pltpu.HBM)


def params(mebibytes=12):
    return pltpu.CompilerParams(vmem_limit_bytes=mebibytes * 1024 * 1024)


def copy_all(pairs, sems):
    copies = [pltpu.make_async_copy(source, target, sems.at[k]) for k, (source, target) in enumerate(pairs)]
    for copy in copies:
        copy.start()
    return copies


def write_columns(places_ref, out_ref, row):
    for k in range(4):
        column = places_ref[k, 1].astype(f32)
        out_ref[0, row + k : row + k + 1] = jnp.full((1, WIDTH), column, f32)
        out_ref[1, row + k : row + k + 1] = jnp.full((1, WIDTH), column, f32)
    out_ref[:, row + 4 : row + 8] = jnp.zeros((2, 4, WIDTH), f32)


def ring_pack_kernel(field_ref, places_ref, *refs):
    out_ref, sems = refs[-2:]
    copies = copy_all([(field_ref.at[:, pl.ds(0, HALF)], out_ref.at[:, pl.ds(0, HALF)])], sems)
    write_columns(places_ref, out_ref, HALF)
    for copy in copies:
        copy.wait()


def core_pack_kernel(field_ref, places_ref, ring_ref, *refs):
    out_ref, sems = refs[-2:]
    copies = copy_all(
        [(field_ref, out_ref.at[:, pl.ds(0, SIDE)]), (ring_ref, out_ref.at[:, pl.ds(SIDE, HALF + 8)])], sems
    )
    write_columns(places_ref, out_ref, SIDE + HALF + 8)
    for copy in copies:
        copy.wait()


def pack_call(kernel, rows, field, places, others, name):
    return pl.pallas_call(
        kernel,
        in_specs=[HBM, SMEM] + [ANY] * len(others),
        out_specs=VMEM,
        out_shape=jax.ShapeDtypeStruct((2, rows, WIDTH), f32),
        scratch_shapes=[pltpu.SemaphoreType.DMA((2,))],
        compiler_params=params(),
        name=name,
    )(field, places, *others)


def prepare_kernel(ids_ref, places_ref, ring_ref, mine_pack_ref, pack_ref, mine_ref, other_ref, shuffle_ref,
                   patch_ref, measured_ref, facts_ref, tall):
    i, core, w, last = ids_ref[0], ids_ref[1], ids_ref[2], ids_ref[3]

    def listed(ref, row):
        return [jnp.max(ref[0, row + k : row + k + 1, 0:128]).astype(jnp.int32) for k in range(4)]

    partner_columns = listed(pack_ref, SIDE + HALF + 8)
    ring_columns = listed(ring_ref, HALF)

    def pick(values, k):
        return jnp.where(k == 0, values[0], jnp.where(k == 1, values[1], jnp.where(k == 2, values[2], values[3])))

    def column(i, w):
        k = jnp.where(lax.rem(i + 4, 2) == 0, 1 + w, 3 * w)
        block = jnp.where(i < 2, 0, 1)
        near = jnp.where(block == core, places_ref[k, 1], pick(partner_columns, k))
        return jnp.where((i < 0) | (i > 3), pick(ring_columns, k), near)

    other = i + 2 * core - 1
    own_column = column(i, w)
    facts_ref[0] = i
    facts_ref[1] = core
    facts_ref[2] = last
    facts_ref[3] = own_column
    facts_ref[4] = column(i, 1 - w)
    facts_ref[5] = column(other, w)
    facts_ref[6] = column(other, 1 - w)
    facts_ref[7] = 0
    facts_ref[8] = ids_ref[4]
    for part in range(2):
        own, partner = mine_pack_ref[part, 0:SIDE], pack_ref[part, 0:SIDE]
        tall[part, 0:256] = jnp.where(core == 0, own, partner)
        tall[part, 256:512] = jnp.where(core == 0, partner, own)
        below = jnp.where(core == 0, pack_ref[part, SIDE : SIDE + HALF], ring_ref[part, 0:HALF])
        tall[part, 512:640] = jnp.where(last == 1, jnp.zeros_like(below), below)
        rows = tall[part, pl.ds(pl.multiple_of(i * HALF, HALF), SIDE), :]
        patch_ref[part] = cut_columns(rows, own_column)
    block = jnp.where(i < 2, 0, 1)
    window = jnp.where(block == core, mine_ref[...], other_ref[...])
    shuffle = shuffle_ref[...]
    h0 = window.astype(bf16)
    rest = window - h0.astype(f32)
    h1 = rest.astype(bf16)
    h2 = (rest - h1.astype(f32)).astype(bf16)
    moved = []
    for piece in (h0, h1, h2):
        rows = jnp.dot(shuffle, piece, preferred_element_type=f32).astype(bf16)
        moved.append(lax.dot_general(rows, shuffle, (((1,), (1,)), ((), ())), preferred_element_type=f32))
    measured_ref[...] = moved[0] + moved[1] + moved[2]


def power_of(far):
    return far[:HALF] * far[:HALF] + far[HALF:] * far[HALF:]


def first_kernel(patch_ref, cols_ref, rows_ref, *refs, begin, end, planes):
    far_ref, probe_ref, power_ref, sems = refs[-4:]
    pairs, waits = [], []
    for m in range(begin, end):
        if m - begin < planes // 2:
            k = 2 * (m - begin)
            waits.append((len(pairs), len(pairs) + 1))
            pairs += [(refs[k], probe_ref.at[m, 0]), (refs[k + 1], probe_ref.at[m, 1])]
        else:
            waits.append((len(pairs),))
            pairs.append((refs[planes + m - begin - planes // 2], probe_ref.at[m]))
    copies = copy_all(pairs, sems)
    if begin > 0:
        power_ref[...] = refs[planes // 2 + end - begin + 2][...]
    xr, xi = patch_ref[0], patch_ref[1]
    for m in range(begin, end):
        for k in waits[m - begin]:
            copies[k].wait()
        pr, pi = probe_ref[m, 0], probe_ref[m, 1]
        far = forward_transform(pr * xr - pi * xi, pr * xi + pi * xr, cols_ref, rows_ref)
        for parity in range(2):
            far_ref[m, parity] = far[parity]
            power = power_of(far[parity])
            power_ref[parity] = power if m == 0 else power_ref[parity] + power


FULL = jax.ShapeDtypeStruct((OWN_MODES, 2, SIDE, SIDE), f32)


def first_call(begin, end, planes, patch, fwd, arrays, carried):
    args = [patch, *fwd, *arrays]
    in_specs = [VMEM] * 3 + [ANY] * len(arrays)
    aliases = {}
    if carried:
        aliases = {len(args) + k: k for k in range(2)}
        args += carried
        in_specs += [VMEM] * 3
    return pl.pallas_call(
        functools.partial(first_kernel, begin=begin, end=end, planes=planes),
        in_specs=in_specs,
        out_specs=[VMEM] * 3,
        out_shape=[FULL, FULL, jax.ShapeDtypeStruct((2, HALF, SIDE), f32)],
        input_output_aliases=aliases,
        scratch_shapes=[pltpu.SemaphoreType.DMA((8,))],
        compiler_params=params(),
        cost_estimate=pl.CostEstimate(flops=800_000_000 * (end - begin), bytes_accessed=3_000_000, transcendentals=0),
        name="first_far",
    )(*args)


def advance_kernel(*refs, begin, end, first):
    if first:
        facts_ref, mine_ref, other_ref, probe_ref, far_ref, cols_ref, rows_ref, _, patch, step_ref, powers_ref, token_ref = refs
        core, last, column = facts_ref[1], facts_ref[2], facts_ref[3]
        for part in range(2):
            mine, other = mine_ref[part], other_ref[part]
            top = jnp.where(core == 0, mine, other)
            bottom = jnp.where(core == 0, other, mine)
            bottom = jnp.where(last == 1, jnp.zeros_like(bottom), bottom)
            patch[part, 0:HALF] = cut_columns(top, column)
            patch[part, HALF:] = cut_columns(bottom, column)
        powers_ref[...] = jnp.zeros_like(powers_ref)
    else:
        patch, probe_ref, far_ref, cols_ref, rows_ref, _, _, powers_in_ref, step_ref, powers_ref, token_ref = refs
        powers_ref[...] = powers_in_ref[...]
    token_ref[...] = jnp.zeros_like(token_ref)

    for m in range(begin, end):
        pr, pi = probe_ref[m, 0], probe_ref[m, 1]
        xr, xi = patch[0], patch[1]
        step = forward_transform(pr * xr - pi * xi, pr * xi + pi * xr, cols_ref, rows_ref)
        for parity in range(2):
            step_ref[m, parity] = step[parity]
            far = far_ref[m, parity]
            cross = far * step[parity]
            powers_ref[0, parity] += cross[:HALF] + cross[HALF:]
            powers_ref[1, parity] += power_of(step[parity])


UNROLL = 8
SMALL = jax.ShapeDtypeStruct((8, 128), f32)


def advance_call(begin, end, facts, mine, other, probe, far, fwd, after, carried):
    powers = jax.ShapeDtypeStruct((2, 2, HALF, SIDE), f32)
    first = carried is None
    aliases = {}
    if first:
        args = [facts, mine, other, probe, far, *fwd, after]
        in_specs = [SMEM] + [VMEM] * 6 + [ANY]
        out_shape = [jax.ShapeDtypeStruct((2, SIDE, SIDE), f32), FULL, powers, SMALL]
    else:
        args = [carried[0], probe, far, *fwd, after, carried[1], carried[2]]
        in_specs = [VMEM] * 5 + [ANY] + [VMEM] * 2
        out_shape = [FULL, powers, SMALL]
        aliases = {6: 0, 7: 1}
    out = pl.pallas_call(
        functools.partial(advance_kernel, begin=begin, end=end, first=first),
        in_specs=in_specs,
        out_specs=[VMEM] * len(out_shape),
        out_shape=out_shape,
        input_output_aliases=aliases,
        compiler_params=params(),
        cost_estimate=pl.CostEstimate(flops=800_000_000 * (end - begin), bytes_accessed=3_000_000, transcendentals=0),
        name="far_step",
    )(*args)
    return out if first else [carried[0], *out]


def step_factor(squares, times=1):
    square_sum = jnp.sum(jnp.sum(squares, axis=0, keepdims=True), axis=1, keepdims=True)
    return STEP_SCALE / jnp.sqrt(square_sum / (times * CELLS) + EPSILON)


def gradient_kernel(*refs, first):
    if first:
        facts_ref, power_ref, other_ref, measured_ref, probe_ref, far_ref, rows_ref, cols_ref, keep_ref, give_ref, change, total = refs
    else:
        (facts_ref, squares_ref, base_ref, power_ref, other_ref, measured_ref, probe_ref, far_ref, step_ref, rows_ref, cols_ref,
         keep_ref, give_ref, far_out_ref, base_out_ref, factor_ref, change, total) = refs
        factor_ref[...] = jnp.broadcast_to(step_factor(squares_ref[...]), (8, SIDE))
        factor = factor_ref[0:1]
    for parity in range(2):
        rows = slice(parity * HALF, (parity + 1) * HALF)
        if first:
            power = power_ref[parity] + other_ref[parity]
        else:
            cross = power_ref[0, parity] + other_ref[0, parity]
            square = power_ref[1, parity] + other_ref[1, parity]
            power = jnp.maximum(base_ref[parity] + factor * (2.0 * cross + factor * square), 0.0)
            base_out_ref[parity] = power
        ratio = (measured_ref[rows] + REGULARIZER) / (power + REGULARIZER)
        change[parity] = jnp.sqrt(ratio) - 1.0
    total[...] = jnp.zeros_like(total)

    def one(m, carry):
        shifted = []
        for parity in range(2):
            far = far_ref[m, parity]
            if not first:
                far = far + factor_ref[0:1] * step_ref[m, parity]
                far_out_ref[m, parity] = far
            c = change[parity]
            shifted.append(jnp.concatenate([far[:HALF] * c, far[HALF:] * c], axis=0))
        dr, di = inverse_transform(shifted[0], shifted[1], rows_ref, cols_ref)
        pr, pi = probe_ref[m, 0], probe_ref[m, 1]
        total[0] += pr * dr + pi * di
        total[1] += pr * di - pi * dr
        return carry

    lax.fori_loop(0, OWN_MODES, one, 0, unroll=UNROLL)
    core = facts_ref[1]
    keep_ref[...] = total[:, pl.ds(pl.multiple_of(core * HALF, HALF), HALF), :]
    give_ref[...] = total[:, pl.ds(pl.multiple_of((1 - core) * HALF, HALF), HALF), :]


def gradient_call(facts, squares, base, power, other, measured, probe, far, step, inv):
    first = squares is None
    half = jax.ShapeDtypeStruct((2, HALF, SIDE), f32)
    aliases = {}
    if first:
        args = [facts, power, other, measured, probe, far, *inv]
        out_shape = [half, half]
    else:
        args = [facts, squares, base, power, other, measured, probe, far, step, *inv]
        out_shape = [half, half, FULL, half]
        aliases = {7: 2, 2: 3}
    return pl.pallas_call(
        functools.partial(gradient_kernel, first=first),
        in_specs=[SMEM] + [VMEM] * (len(args) - 1),
        out_specs=[VMEM] * len(out_shape),
        out_shape=out_shape,
        input_output_aliases=aliases,
        scratch_shapes=[pltpu.VMEM((8, SIDE), f32)] * (not first)
        + [pltpu.VMEM((2, HALF, SIDE), f32), pltpu.VMEM((2, SIDE, SIDE), f32)],
        compiler_params=params(),
        cost_estimate=pl.CostEstimate(flops=3_400_000_000, bytes_accessed=17_000_000, transcendentals=65536),
        name="window_gradient",
    )(*args)


def merge_kernel(facts_ref, own_ref, a_ref, b_ref, c_ref, *refs, earlier):
    band_ref, square_ref = refs[-2:]
    core, last, initial = facts_ref[1], facts_ref[2], facts_ref[8]

    def wide(x, column):
        x = jnp.concatenate([x, jnp.zeros((HALF, WIDTH - SIDE), f32)], axis=1)
        return pltpu.roll(x, column, 1)

    drop_own = (last == 1) & (core == 1)
    drop_other = (initial == 1) & (core == 0)
    squares = jnp.zeros((8, 128), f32)
    for part in range(2):
        own = wide(own_ref[part], facts_ref[3]) + wide(a_ref[part], facts_ref[4])
        other = wide(b_ref[part], facts_ref[5]) + wide(c_ref[part], facts_ref[6])
        own = jnp.where(drop_own, jnp.zeros_like(own), own)
        other = jnp.where(drop_other, jnp.zeros_like(other), other)
        band = own + other
        band_ref[part] = band
        sq = (band * band).reshape(HALF // 8, 8, WIDTH).sum(axis=0)
        squares = squares + sq[:, 0:128] + sq[:, 128:256] + sq[:, 256:384]
        if earlier:
            totals, bands = refs[0], refs[1 : 1 + earlier]
            factors = [step_factor(totals[8 * k : 8 * k + 8], 2) for k in range(earlier)]
            band_ref[2 + part] = sum(f * g[part] for f, g in zip(factors, bands))
    square_ref[...] = squares


def merge_call(facts, own, a, b, c, totals, bands):
    args = [facts, own, a, b, c, *totals, *bands]
    parts = 4 if bands else 2
    return pl.pallas_call(
        functools.partial(merge_kernel, earlier=len(bands)),
        in_specs=[SMEM] + [VMEM] * (len(args) - 1),
        out_specs=[VMEM, VMEM],
        out_shape=[jax.ShapeDtypeStruct((parts, HALF, WIDTH), f32), SMALL],
        compiler_params=params(),
        cost_estimate=pl.CostEstimate(flops=1_000_000, bytes_accessed=2_000_000, transcendentals=0),
        name="band_sum",
    )(*args)


def choose_kernel(facts_ref, own_ref, partner_ref, _, out_ref):
    core = facts_ref[1]

    @pl.when(core == 0)
    def _():
        out_ref[...] = own_ref[...]

    @pl.when(core == 1)
    def _():
        out_ref[...] = partner_ref[...]


def choose_call(facts, own, partner, after):
    return pl.pallas_call(
        choose_kernel,
        in_specs=[SMEM, VMEM, VMEM, ANY],
        out_specs=VMEM,
        out_shape=jax.ShapeDtypeStruct((4, HALF, WIDTH), f32),
        compiler_params=params(),
        name="choose",
    )(facts, own, partner, after)


UPPER = ((0, 2, 3, 3), (2, 0, 1, 2))
LOWER = ((1, 0, 2, 2), (3, 2, 0, 1))


def finish_kernel(facts_ref, squares_ref, field_ref, own_ref, partner_ref, one_ref, two_ref, out_ref):
    i, core = facts_ref[0], facts_ref[1]
    factor = step_factor(squares_ref[...], 2)
    for rows, sources in ((slice(0, HALF), UPPER), (slice(HALF, SIDE), LOWER)):
        for source, ref in enumerate((own_ref, partner_ref, one_ref, two_ref)):
            chosen = [(core == c) & (i == k) for c in range(2) for k in range(4) if sources[c][k] == source]
            here = chosen[0]
            for more in chosen[1:]:
                here = here | more

            @pl.when(here)
            def _():
                for part in range(2):
                    moved = ref[2 + part] + factor * ref[part]
                    out_ref[part, rows] = field_ref[part, rows] + moved


def finish_call(*args):
    return pl.pallas_call(
        finish_kernel,
        in_specs=[SMEM] + [VMEM] * 6,
        out_specs=VMEM,
        out_shape=jax.ShapeDtypeStruct((2, SIDE, WIDTH), f32),
        compiler_params=params(),
        name="finish",
    )(*args)


def take_kernel(ids_ref, probe_ref, measured_ref, _, own_ref, real_ref, imag_ref, mine_ref, sems):
    core, window = ids_ref[1], ids_ref[5]
    copies = copy_all(
        [
            (probe_ref.at[0, core], own_ref.at[0]),
            (probe_ref.at[1, core], own_ref.at[1]),
            (probe_ref.at[0, core], real_ref),
            (probe_ref.at[1, core], imag_ref),
            (measured_ref.at[0, window], mine_ref),
        ],
        sems,
    )
    for copy in copies:
        copy.wait()


def take_call(ids, probe_modes, measured, after):
    return pl.pallas_call(
        take_kernel,
        in_specs=[SMEM, HBM, HBM, ANY],
        out_specs=[VMEM] * 4,
        out_shape=[jax.ShapeDtypeStruct((2, SIDE, SIDE), f32)] + [jax.ShapeDtypeStruct((SIDE, SIDE), f32)] * 3,
        scratch_shapes=[pltpu.SemaphoreType.DMA((5,))],
        compiler_params=params(),
        name="take",
    )(ids, probe_modes, measured, after)


def split_kernel(both_ref, _, real_ref, imag_ref, sems):
    for copy in copy_all([(both_ref.at[0], real_ref), (both_ref.at[1], imag_ref)], sems):
        copy.wait()


def split_call(both, after):
    plane = jax.ShapeDtypeStruct((SIDE, SIDE), f32)
    return pl.pallas_call(
        split_kernel,
        in_specs=[ANY, ANY],
        out_specs=[VMEM] * 2,
        out_shape=[plane] * 2,
        scratch_shapes=[pltpu.SemaphoreType.DMA((2,))],
        compiler_params=params(),
        name="split",
    )(both, after)


def body(object_field, probe_modes, measured, positions):
    strip, mode = lax.axis_index("strip"), lax.axis_index("mode")
    core, j = strip % 2, strip // 2
    z, w = mode // 2, mode % 2
    i = jnp.where(j % 2 == 0, z, 3 - z)
    pair = 4 * j + i
    last = (pair == 31).astype(jnp.int32)
    initial = (pair == 0).astype(jnp.int32)
    fwd, inv = tables()
    fwd = [jnp.asarray(t) for t in fwd]
    inv = [jnp.asarray(t) for t in inv]
    shuffle = jnp.asarray(shuffle_table())

    window = jnp.where(i % 2 == 0, 1 + w, 3 * w)
    ids = jnp.stack([i, core, w, last, initial, window, core, core]).astype(jnp.int32)

    places = positions[0]
    top = pack_call(ring_pack_kernel, HALF + 8, object_field, places, [], "ring_pack")
    ring = send(top, RING)
    own, real, imag, mine = take_call(ids, probe_modes, measured, top)
    up, down = send(own, Z_UP), send(own, Z_DOWN)
    side = send(real, Y_UP), send(imag, Y_DOWN)
    opposite, up_side, down_side = send(up, Z_UP), send(up, Y_UP), send(down, Y_DOWN)

    pack = pack_call(core_pack_kernel, SIDE + HALF + 16, object_field, places, [ring, up, down, *side], "core_pack")
    patch, pattern, facts = pl.pallas_call(
        prepare_kernel,
        in_specs=[SMEM] * 2 + [VMEM] * 6,
        out_specs=[VMEM] * 2 + [SMEM],
        out_shape=[
            jax.ShapeDtypeStruct((2, SIDE, SIDE), f32),
            jax.ShapeDtypeStruct((SIDE, SIDE), f32),
            jax.ShapeDtypeStruct((9,), jnp.int32),
        ],
        scratch_shapes=[pltpu.VMEM((2, 640, WIDTH), f32)],
        compiler_params=params(),
        name="prepare",
    )(ids, places, ring, pack, send(pack, SWAP_CORE), mine, send(mine, SWAP_CORE), shuffle)

    carried = first_call(0, 4, 2, patch, fwd, [*side, own, up, down], [])
    real, imag = split_call(opposite, carried[2])
    opposite_side = send(real, Y_UP), send(imag, Y_DOWN)
    carried = first_call(4, 7, 0, patch, fwd, [up_side, down_side, opposite], carried)
    far, probe, power = first_call(7, 8, 2, patch, fwd, opposite_side, carried)
    base = squares = step = None
    bands, totals = [], []
    for iteration in range(ITERS):
        other = send(power, SWAP_CORE)
        if iteration == 0:
            keep, give = gradient_call(facts, None, None, power, other, pattern, probe, far, None, inv)
            base = power + other
        else:
            keep, give, far, base = gradient_call(
                facts, squares, base, power, other, pattern, probe, far, step, inv
            )
            totals.append(squares)
        final = iteration + 1 == ITERS
        if final:
            stacked = jnp.concatenate(totals, axis=0)
            stacked = stacked + send(stacked, SWAP_CORE)
        half = keep + send(give, SWAP_CORE)
        band, squares = merge_call(
            facts,
            half,
            send(half, BAND_A),
            send(half, BAND_B),
            send(half, BAND_C),
            [stacked] if final else [],
            bands if final else [],
        )
        bands.append(band)
        partner = send(band, SWAP_CORE)
        if final:
            squares = squares + send(squares, SWAP_CORE)
            got_one = send(band, FINAL_ONE)
        carried = None
        for stage, route in enumerate(LAST_DOUBLING if final else DOUBLING):
            arrived = send(squares, route)
            if not final and stage in PIECES:
                begin, end = PIECES[stage]
                carried = advance_call(begin, end, facts, band, partner, probe, far, fwd, squares, carried)
                arrived = arrived + carried[3]
            squares = squares + arrived
            if final and stage == 0:
                got_two = send(choose_call(facts, band, partner, squares), FINAL_TWO)
        if not final:
            _, step, power, _ = carried
    return finish_call(facts, squares, object_field, band, partner, got_one, got_two)


PIECES = {1: (0, 5), 2: (5, 7), 3: (7, 8)}


def solution(mesh):
    return jax.shard_map(
        body,
        mesh=mesh,
        in_specs=(
            P(None, "strip", None),
            P(None, "mode", None, None),
            P("strip", None, None, None),
            P("strip", None, None),
        ),
        out_specs=P(None, "strip", None),
        check_vma=False,
    )
```

```python
import functools

import jax
import jax.numpy as jnp
import numpy as np
from jax import lax
from jax.experimental import pallas as pl
from jax.experimental.pallas import tpu as pltpu
from jax.sharding import PartitionSpec as P

ITERS = 3
SIDE = 256
HALF = 128
WIDTH = 384
OWN_MODES = 8
REGULARIZER = 0.1
STEP_SCALE = 0.3
EPSILON = 1e-06
CELLS = 4096 * 384
AXES = ("strip", "mode")
f32, bf16 = jnp.float32, jnp.bfloat16


def place(index):
    strip, mode = divmod(index, 8)
    core, j = strip % 2, strip // 2
    z, w = divmod(mode, 2)
    i = z if j % 2 == 0 else 3 - z
    return 4 * j + i, w, core


def device_of(pair, w, core):
    j, i = divmod(pair % 32, 4)
    z = i if j % 2 == 0 else 3 - i
    return (2 * j + core) * 8 + 2 * z + w


def route_pairs(move):
    return [(d, device_of(*move(*place(d)))) for d in range(128)]


def route_grid(move):
    route = []
    for d in range(128):
        strip, mode = divmod(d, 8)
        core, x, y_hi = strip % 2, strip // 2 % 4, strip // 8
        z, y_lo = divmod(mode, 2)
        y, x, z = move(2 * y_hi + y_lo, x, z)
        y, x, z = y % 4, x % 4, z % 4
        route.append((d, (((y // 2) * 4 + x) * 2 + core) * 8 + 2 * z + y % 2))
    return route


SWAP_CORE = route_pairs(lambda p, w, c: (p, w, 1 - c))
BAND_A = route_pairs(lambda p, w, c: (p, 1 - w, c))
BAND_B = route_pairs(lambda p, w, c: (p + 2 * c - 1, w, 1 - c))
BAND_C = route_pairs(lambda p, w, c: (p + 2 * c - 1, 1 - w, 1 - c))
Z_UP = route_grid(lambda y, x, z: (y, x, z + 1))
Z_DOWN = route_grid(lambda y, x, z: (y, x, z - 1))
Y_UP = route_grid(lambda y, x, z: (y + 1, x, z))
Y_DOWN = route_grid(lambda y, x, z: (y - 1, x, z))
DOUBLING = [
    route_grid(lambda y, x, z: (y, x, z ^ 1)),
    route_grid(lambda y, x, z: (y, x ^ 1, z)),
    route_grid(lambda y, x, z: (y ^ 2, x, z)),
    route_grid(lambda y, x, z: (y, x ^ 2, z)),
    route_grid(lambda y, x, z: (y, x, z ^ 2)),
]

LAST_DOUBLING = [DOUBLING[k] for k in (1, 2, 3, 0, 4)]


def ring_route():
    route = []
    for j in range(8):
        for mode in range(8):
            low, high = (2 * j + 1) * 8 + mode, (2 * ((j + 1) % 8)) * 8 + mode
            route += [(low, high), (high, low)]
    return route


RING = ring_route()


def final_routes():
    one, two = [], []
    for j in range(8):
        for w in range(2):

            def at(i, c):
                return device_of(4 * j + i, w, c)

            one += [
                (at(0, 0), at(1, 0)),
                (at(1, 0), at(2, 0)),
                (at(0, 1), at(3, 0)),
                (at(2, 1), at(1, 1)),
                (at(2, 0), at(3, 1)),
                (at(1, 1), at(0, 1)),
            ]
            two += [(at(0, 0), at(2, 0)), (at(0, 1), at(3, 0)), (at(3, 0), at(0, 1))]
    return one, two


FINAL_ONE, FINAL_TWO = final_routes()


def send(value, route):
    return lax.ppermute(value, AXES, route)


def table(parity):
    n = np.arange(HALF)
    turns = (n[:, None] * (2 * n[None, :] + parity)) % SIDE
    angle = -2.0 * np.pi * turns / SIDE
    real, imag = np.cos(angle) / 16.0, np.sin(angle) / 16.0
    return np.block([[real, imag], [-imag, real]])


def tables():
    right, left = [], []
    for parity in range(2):
        t = table(parity)
        high = t.astype(np.float32).astype(jnp.bfloat16)
        low = (t - high.astype(np.float64)).astype(np.float32).astype(jnp.bfloat16)
        right.append(np.concatenate([high, high, low], axis=0))
        left.append(np.concatenate([high, high, low], axis=1))
    turned_right = [np.concatenate([r[:256].T, r[:256].T, r[512:].T], axis=0) for r in right]
    turned_left = [np.concatenate([r[:256].T, r[:256].T, r[512:].T], axis=1) for r in right]
    forward = (np.stack(right), np.stack(turned_left))
    inverse = (np.stack(left), np.stack(turned_right))
    return forward, inverse


def shuffle_table():
    rows = np.arange(SIDE)
    take = 2 * (rows % HALF) + rows // HALF
    return (take[:, None] == np.arange(SIDE)[None, :]).astype(jnp.bfloat16)


def halves(x):
    high = x.astype(bf16)
    low = (x - high.astype(f32)).astype(bf16)
    return high, low


def times_right(x, tab):
    high, low = halves(x)
    return jnp.dot(jnp.concatenate([high, low, high], axis=1), tab, preferred_element_type=f32)


def times_left(tab, x):
    high, low = halves(x)
    return jnp.dot(tab, jnp.concatenate([high, low, high], axis=0), preferred_element_type=f32)


def forward_transform(real, imag, cols, rows):
    stage = []
    for sign in (1.0, -1.0):
        if sign > 0:
            r, i = real[:, :HALF] + real[:, HALF:], imag[:, :HALF] + imag[:, HALF:]
        else:
            r, i = real[:, :HALF] - real[:, HALF:], imag[:, :HALF] - imag[:, HALF:]
        stage.append(times_right(jnp.concatenate([r, i], axis=1), cols[0 if sign > 0 else 1]))
    even, odd = stage
    top = [even[:HALF], odd[:HALF]]
    bottom = [even[HALF:], odd[HALF:]]
    out = []
    for parity in range(2):
        if parity == 0:
            mixed = [t + b for t, b in zip(top, bottom)]
        else:
            mixed = [t - b for t, b in zip(top, bottom)]
        block = jnp.concatenate(
            [
                jnp.concatenate([m[:, :HALF] for m in mixed], axis=1),
                jnp.concatenate([m[:, HALF:] for m in mixed], axis=1),
            ],
            axis=0,
        )
        out.append(times_left(rows[parity], block))
    return out


def inverse_transform(far_even, far_odd, rows, cols):
    b0 = times_left(rows[0], far_even)
    b1 = times_left(rows[1], far_odd)
    plus, minus = b0 + b1, b0 - b1
    c = []
    for q in range(2):
        lanes = slice(q * HALF, (q + 1) * HALF)
        real = jnp.concatenate([plus[:HALF, lanes], minus[:HALF, lanes]], axis=0)
        imag = jnp.concatenate([plus[HALF:, lanes], minus[HALF:, lanes]], axis=0)
        c.append(times_right(jnp.concatenate([real, imag], axis=1), cols[q]))
    real = jnp.concatenate([c[0][:, :HALF] + c[1][:, :HALF], c[0][:, :HALF] - c[1][:, :HALF]], axis=1)
    imag = jnp.concatenate([c[0][:, HALF:] + c[1][:, HALF:], c[0][:, HALF:] - c[1][:, HALF:]], axis=1)
    return real, imag


def cut_columns(x, column):
    return pltpu.roll(x, lax.rem(WIDTH - column, WIDTH), 1)[:, :SIDE]


VMEM = pl.BlockSpec(memory_space=pltpu.VMEM)
SMEM = pl.BlockSpec(memory_space=pltpu.SMEM)
ANY = pl.BlockSpec(memory_space=pl.ANY)
HBM = pl.BlockSpec(memory_space=pltpu.HBM)


def params(mebibytes=12):
    return pltpu.CompilerParams(vmem_limit_bytes=mebibytes * 1024 * 1024)


def copy_all(pairs, sems):
    copies = [pltpu.make_async_copy(source, target, sems.at[k]) for k, (source, target) in enumerate(pairs)]
    for copy in copies:
        copy.start()
    return copies


def write_columns(places_ref, out_ref, row):
    for k in range(4):
        column = places_ref[k, 1].astype(f32)
        out_ref[0, row + k : row + k + 1] = jnp.full((1, WIDTH), column, f32)
        out_ref[1, row + k : row + k + 1] = jnp.full((1, WIDTH), column, f32)
    out_ref[:, row + 4 : row + 8] = jnp.zeros((2, 4, WIDTH), f32)


def ring_pack_kernel(field_ref, places_ref, *refs):
    out_ref, sems = refs[-2:]
    copies = copy_all([(field_ref.at[:, pl.ds(0, HALF)], out_ref.at[:, pl.ds(0, HALF)])], sems)
    write_columns(places_ref, out_ref, HALF)
    for copy in copies:
        copy.wait()


def core_pack_kernel(field_ref, places_ref, ring_ref, *refs):
    out_ref, sems = refs[-2:]
    copies = copy_all(
        [(field_ref, out_ref.at[:, pl.ds(0, SIDE)]), (ring_ref, out_ref.at[:, pl.ds(SIDE, HALF + 8)])], sems
    )
    write_columns(places_ref, out_ref, SIDE + HALF + 8)
    for copy in copies:
        copy.wait()


def pack_call(kernel, rows, field, places, others, name):
    return pl.pallas_call(
        kernel,
        in_specs=[HBM, SMEM] + [ANY] * len(others),
        out_specs=VMEM,
        out_shape=jax.ShapeDtypeStruct((2, rows, WIDTH), f32),
        scratch_shapes=[pltpu.SemaphoreType.DMA((2,))],
        compiler_params=params(),
        name=name,
    )(field, places, *others)


def prepare_kernel(ids_ref, places_ref, ring_ref, mine_pack_ref, pack_ref, mine_ref, other_ref, shuffle_ref,
                   patch_ref, measured_ref, facts_ref, tall):
    i, core, w, last = ids_ref[0], ids_ref[1], ids_ref[2], ids_ref[3]

    def listed(ref, row):
        return [jnp.max(ref[0, row + k : row + k + 1, 0:128]).astype(jnp.int32) for k in range(4)]

    partner_columns = listed(pack_ref, SIDE + HALF + 8)
    ring_columns = listed(ring_ref, HALF)

    def pick(values, k):
        return jnp.where(k == 0, values[0], jnp.where(k == 1, values[1], jnp.where(k == 2, values[2], values[3])))

    def column(i, w):
        k = jnp.where(lax.rem(i + 4, 2) == 0, 1 + w, 3 * w)
        block = jnp.where(i < 2, 0, 1)
        near = jnp.where(block == core, places_ref[k, 1], pick(partner_columns, k))
        return jnp.where((i < 0) | (i > 3), pick(ring_columns, k), near)

    other = i + 2 * core - 1
    own_column = column(i, w)
    facts_ref[0] = i
    facts_ref[1] = core
    facts_ref[2] = last
    facts_ref[3] = own_column
    facts_ref[4] = column(i, 1 - w)
    facts_ref[5] = column(other, w)
    facts_ref[6] = column(other, 1 - w)
    facts_ref[7] = 0
    facts_ref[8] = ids_ref[4]
    for part in range(2):
        own, partner = mine_pack_ref[part, 0:SIDE], pack_ref[part, 0:SIDE]
        tall[part, 0:256] = jnp.where(core == 0, own, partner)
        tall[part, 256:512] = jnp.where(core == 0, partner, own)
        below = jnp.where(core == 0, pack_ref[part, SIDE : SIDE + HALF], ring_ref[part, 0:HALF])
        tall[part, 512:640] = jnp.where(last == 1, jnp.zeros_like(below), below)
        rows = tall[part, pl.ds(pl.multiple_of(i * HALF, HALF), SIDE), :]
        patch_ref[part] = cut_columns(rows, own_column)
    block = jnp.where(i < 2, 0, 1)
    window = jnp.where(block == core, mine_ref[...], other_ref[...])
    shuffle = shuffle_ref[...]
    h0 = window.astype(bf16)
    rest = window - h0.astype(f32)
    h1 = rest.astype(bf16)
    h2 = (rest - h1.astype(f32)).astype(bf16)
    moved = []
    for piece in (h0, h1, h2):
        rows = jnp.dot(shuffle, piece, preferred_element_type=f32).astype(bf16)
        moved.append(lax.dot_general(rows, shuffle, (((1,), (1,)), ((), ())), preferred_element_type=f32))
    measured_ref[...] = moved[0] + moved[1] + moved[2]


def power_of(far):
    return far[:HALF] * far[:HALF] + far[HALF:] * far[HALF:]


def first_kernel(patch_ref, cols_ref, rows_ref, *refs, begin, end, planes):
    far_ref, probe_ref, power_ref, sems = refs[-4:]
    pairs, waits = [], []
    for m in range(begin, end):
        if m - begin < planes // 2:
            k = 2 * (m - begin)
            waits.append((len(pairs), len(pairs) + 1))
            pairs += [(refs[k], probe_ref.at[m, 0]), (refs[k + 1], probe_ref.at[m, 1])]
        else:
            waits.append((len(pairs),))
            pairs.append((refs[planes + m - begin - planes // 2], probe_ref.at[m]))
    copies = copy_all(pairs, sems)
    if begin > 0:
        power_ref[...] = refs[planes // 2 + end - begin + 2][...]
    xr, xi = patch_ref[0], patch_ref[1]
    for m in range(begin, end):
        for k in waits[m - begin]:
            copies[k].wait()
        pr, pi = probe_ref[m, 0], probe_ref[m, 1]
        far = forward_transform(pr * xr - pi * xi, pr * xi + pi * xr, cols_ref, rows_ref)
        for parity in range(2):
            far_ref[m, parity] = far[parity]
            power = power_of(far[parity])
            power_ref[parity] = power if m == 0 else power_ref[parity] + power


FULL = jax.ShapeDtypeStruct((OWN_MODES, 2, SIDE, SIDE), f32)


def first_call(begin, end, planes, patch, fwd, arrays, carried):
    args = [patch, *fwd, *arrays]
    in_specs = [VMEM] * 3 + [ANY] * len(arrays)
    aliases = {}
    if carried:
        aliases = {len(args) + k: k for k in range(2)}
        args += carried
        in_specs += [VMEM] * 3
    return pl.pallas_call(
        functools.partial(first_kernel, begin=begin, end=end, planes=planes),
        in_specs=in_specs,
        out_specs=[VMEM] * 3,
        out_shape=[FULL, FULL, jax.ShapeDtypeStruct((2, HALF, SIDE), f32)],
        input_output_aliases=aliases,
        scratch_shapes=[pltpu.SemaphoreType.DMA((8,))],
        compiler_params=params(),
        cost_estimate=pl.CostEstimate(flops=800_000_000 * (end - begin), bytes_accessed=3_000_000, transcendentals=0),
        name="first_far",
    )(*args)


def advance_kernel(*refs, begin, end, first):
    if first:
        facts_ref, mine_ref, other_ref, probe_ref, far_ref, cols_ref, rows_ref, _, patch, step_ref, powers_ref, token_ref = refs
        core, last, column = facts_ref[1], facts_ref[2], facts_ref[3]
        for part in range(2):
            mine, other = mine_ref[part], other_ref[part]
            top = jnp.where(core == 0, mine, other)
            bottom = jnp.where(core == 0, other, mine)
            bottom = jnp.where(last == 1, jnp.zeros_like(bottom), bottom)
            patch[part, 0:HALF] = cut_columns(top, column)
            patch[part, HALF:] = cut_columns(bottom, column)
        powers_ref[...] = jnp.zeros_like(powers_ref)
    else:
        patch, probe_ref, far_ref, cols_ref, rows_ref, _, _, powers_in_ref, step_ref, powers_ref, token_ref = refs
        powers_ref[...] = powers_in_ref[...]
    token_ref[...] = jnp.zeros_like(token_ref)

    for m in range(begin, end):
        pr, pi = probe_ref[m, 0], probe_ref[m, 1]
        xr, xi = patch[0], patch[1]
        step = forward_transform(pr * xr - pi * xi, pr * xi + pi * xr, cols_ref, rows_ref)
        for parity in range(2):
            step_ref[m, parity] = step[parity]
            far = far_ref[m, parity]
            cross = far * step[parity]
            powers_ref[0, parity] += cross[:HALF] + cross[HALF:]
            powers_ref[1, parity] += power_of(step[parity])


UNROLL = 2
SMALL = jax.ShapeDtypeStruct((8, 128), f32)


def advance_call(begin, end, facts, mine, other, probe, far, fwd, after, carried):
    powers = jax.ShapeDtypeStruct((2, 2, HALF, SIDE), f32)
    first = carried is None
    aliases = {}
    if first:
        args = [facts, mine, other, probe, far, *fwd, after]
        in_specs = [SMEM] + [VMEM] * 6 + [ANY]
        out_shape = [jax.ShapeDtypeStruct((2, SIDE, SIDE), f32), FULL, powers, SMALL]
    else:
        args = [carried[0], probe, far, *fwd, after, carried[1], carried[2]]
        in_specs = [VMEM] * 5 + [ANY] + [VMEM] * 2
        out_shape = [FULL, powers, SMALL]
        aliases = {6: 0, 7: 1}
    out = pl.pallas_call(
        functools.partial(advance_kernel, begin=begin, end=end, first=first),
        in_specs=in_specs,
        out_specs=[VMEM] * len(out_shape),
        out_shape=out_shape,
        input_output_aliases=aliases,
        compiler_params=params(),
        cost_estimate=pl.CostEstimate(flops=800_000_000 * (end - begin), bytes_accessed=3_000_000, transcendentals=0),
        name="far_step",
    )(*args)
    return out if first else [carried[0], *out]


def step_factor(squares, times=1):
    square_sum = jnp.sum(jnp.sum(squares, axis=0, keepdims=True), axis=1, keepdims=True)
    return STEP_SCALE / jnp.sqrt(square_sum / (times * CELLS) + EPSILON)


def gradient_kernel(*refs, first):
    if first:
        facts_ref, power_ref, other_ref, measured_ref, probe_ref, far_ref, rows_ref, cols_ref, keep_ref, give_ref, change, total = refs
    else:
        (facts_ref, squares_ref, base_ref, power_ref, other_ref, measured_ref, probe_ref, far_ref, step_ref, rows_ref, cols_ref,
         keep_ref, give_ref, far_out_ref, base_out_ref, factor_ref, change, total) = refs
        factor_ref[...] = jnp.broadcast_to(step_factor(squares_ref[...]), (8, SIDE))
        factor = factor_ref[0:1]
    for parity in range(2):
        rows = slice(parity * HALF, (parity + 1) * HALF)
        if first:
            power = power_ref[parity] + other_ref[parity]
        else:
            cross = power_ref[0, parity] + other_ref[0, parity]
            square = power_ref[1, parity] + other_ref[1, parity]
            power = jnp.maximum(base_ref[parity] + factor * (2.0 * cross + factor * square), 0.0)
            base_out_ref[parity] = power
        ratio = (measured_ref[rows] + REGULARIZER) / (power + REGULARIZER)
        change[parity] = jnp.sqrt(ratio) - 1.0
    total[...] = jnp.zeros_like(total)

    def one(m, carry):
        shifted = []
        for parity in range(2):
            far = far_ref[m, parity]
            if not first:
                far = far + factor_ref[0:1] * step_ref[m, parity]
                far_out_ref[m, parity] = far
            c = change[parity]
            shifted.append(jnp.concatenate([far[:HALF] * c, far[HALF:] * c], axis=0))
        dr, di = inverse_transform(shifted[0], shifted[1], rows_ref, cols_ref)
        pr, pi = probe_ref[m, 0], probe_ref[m, 1]
        total[0] += pr * dr + pi * di
        total[1] += pr * di - pi * dr
        return carry

    lax.fori_loop(0, OWN_MODES, one, 0, unroll=UNROLL)
    core = facts_ref[1]
    keep_ref[...] = total[:, pl.ds(pl.multiple_of(core * HALF, HALF), HALF), :]
    give_ref[...] = total[:, pl.ds(pl.multiple_of((1 - core) * HALF, HALF), HALF), :]


def gradient_call(facts, squares, base, power, other, measured, probe, far, step, inv):
    first = squares is None
    half = jax.ShapeDtypeStruct((2, HALF, SIDE), f32)
    aliases = {}
    if first:
        args = [facts, power, other, measured, probe, far, *inv]
        out_shape = [half, half]
    else:
        args = [facts, squares, base, power, other, measured, probe, far, step, *inv]
        out_shape = [half, half, FULL, half]
        aliases = {7: 2, 2: 3}
    return pl.pallas_call(
        functools.partial(gradient_kernel, first=first),
        in_specs=[SMEM] + [VMEM] * (len(args) - 1),
        out_specs=[VMEM] * len(out_shape),
        out_shape=out_shape,
        input_output_aliases=aliases,
        scratch_shapes=[pltpu.VMEM((8, SIDE), f32)] * (not first)
        + [pltpu.VMEM((2, HALF, SIDE), f32), pltpu.VMEM((2, SIDE, SIDE), f32)],
        compiler_params=params(),
        cost_estimate=pl.CostEstimate(flops=3_400_000_000, bytes_accessed=17_000_000, transcendentals=65536),
        name="window_gradient",
    )(*args)


def merge_kernel(facts_ref, own_ref, a_ref, b_ref, c_ref, *refs, earlier):
    band_ref, square_ref = refs[-2:]
    core, last, initial = facts_ref[1], facts_ref[2], facts_ref[8]

    def wide(x, column):
        x = jnp.concatenate([x, jnp.zeros((HALF, WIDTH - SIDE), f32)], axis=1)
        return pltpu.roll(x, column, 1)

    drop_own = (last == 1) & (core == 1)
    drop_other = (initial == 1) & (core == 0)
    squares = jnp.zeros((8, 128), f32)
    for part in range(2):
        own = wide(own_ref[part], facts_ref[3]) + wide(a_ref[part], facts_ref[4])
        other = wide(b_ref[part], facts_ref[5]) + wide(c_ref[part], facts_ref[6])
        own = jnp.where(drop_own, jnp.zeros_like(own), own)
        other = jnp.where(drop_other, jnp.zeros_like(other), other)
        band = own + other
        band_ref[part] = band
        sq = (band * band).reshape(HALF // 8, 8, WIDTH).sum(axis=0)
        squares = squares + sq[:, 0:128] + sq[:, 128:256] + sq[:, 256:384]
        if earlier:
            totals, bands = refs[0], refs[1 : 1 + earlier]
            factors = [step_factor(totals[8 * k : 8 * k + 8], 2) for k in range(earlier)]
            band_ref[2 + part] = sum(f * g[part] for f, g in zip(factors, bands))
    square_ref[...] = squares


def merge_call(facts, own, a, b, c, totals, bands):
    args = [facts, own, a, b, c, *totals, *bands]
    parts = 4 if bands else 2
    return pl.pallas_call(
        functools.partial(merge_kernel, earlier=len(bands)),
        in_specs=[SMEM] + [VMEM] * (len(args) - 1),
        out_specs=[VMEM, VMEM],
        out_shape=[jax.ShapeDtypeStruct((parts, HALF, WIDTH), f32), SMALL],
        compiler_params=params(),
        cost_estimate=pl.CostEstimate(flops=1_000_000, bytes_accessed=2_000_000, transcendentals=0),
        name="band_sum",
    )(*args)


def choose_kernel(facts_ref, own_ref, partner_ref, _, out_ref):
    core = facts_ref[1]

    @pl.when(core == 0)
    def _():
        out_ref[...] = own_ref[...]

    @pl.when(core == 1)
    def _():
        out_ref[...] = partner_ref[...]


def choose_call(facts, own, partner, after):
    return pl.pallas_call(
        choose_kernel,
        in_specs=[SMEM, VMEM, VMEM, ANY],
        out_specs=VMEM,
        out_shape=jax.ShapeDtypeStruct((4, HALF, WIDTH), f32),
        compiler_params=params(),
        name="choose",
    )(facts, own, partner, after)


UPPER = ((0, 2, 3, 3), (2, 0, 1, 2))
LOWER = ((1, 0, 2, 2), (3, 2, 0, 1))


def finish_kernel(facts_ref, squares_ref, field_ref, own_ref, partner_ref, one_ref, two_ref, out_ref):
    i, core = facts_ref[0], facts_ref[1]
    factor = step_factor(squares_ref[...], 2)
    for rows, sources in ((slice(0, HALF), UPPER), (slice(HALF, SIDE), LOWER)):
        for source, ref in enumerate((own_ref, partner_ref, one_ref, two_ref)):
            chosen = [(core == c) & (i == k) for c in range(2) for k in range(4) if sources[c][k] == source]
            here = chosen[0]
            for more in chosen[1:]:
                here = here | more

            @pl.when(here)
            def _():
                for part in range(2):
                    moved = ref[2 + part] + factor * ref[part]
                    out_ref[part, rows] = field_ref[part, rows] + moved


def finish_call(*args):
    return pl.pallas_call(
        finish_kernel,
        in_specs=[SMEM] + [VMEM] * 6,
        out_specs=VMEM,
        out_shape=jax.ShapeDtypeStruct((2, SIDE, WIDTH), f32),
        compiler_params=params(),
        name="finish",
    )(*args)


def take_kernel(ids_ref, probe_ref, measured_ref, _, own_ref, real_ref, imag_ref, mine_ref, sems):
    core, window = ids_ref[1], ids_ref[5]
    copies = copy_all(
        [
            (probe_ref.at[0, core], own_ref.at[0]),
            (probe_ref.at[1, core], own_ref.at[1]),
            (probe_ref.at[0, core], real_ref),
            (probe_ref.at[1, core], imag_ref),
            (measured_ref.at[0, window], mine_ref),
        ],
        sems,
    )
    for copy in copies:
        copy.wait()


def take_call(ids, probe_modes, measured, after):
    return pl.pallas_call(
        take_kernel,
        in_specs=[SMEM, HBM, HBM, ANY],
        out_specs=[VMEM] * 4,
        out_shape=[jax.ShapeDtypeStruct((2, SIDE, SIDE), f32)] + [jax.ShapeDtypeStruct((SIDE, SIDE), f32)] * 3,
        scratch_shapes=[pltpu.SemaphoreType.DMA((5,))],
        compiler_params=params(),
        name="take",
    )(ids, probe_modes, measured, after)


def split_kernel(both_ref, _, real_ref, imag_ref, sems):
    for copy in copy_all([(both_ref.at[0], real_ref), (both_ref.at[1], imag_ref)], sems):
        copy.wait()


def split_call(both, after):
    plane = jax.ShapeDtypeStruct((SIDE, SIDE), f32)
    return pl.pallas_call(
        split_kernel,
        in_specs=[ANY, ANY],
        out_specs=[VMEM] * 2,
        out_shape=[plane] * 2,
        scratch_shapes=[pltpu.SemaphoreType.DMA((2,))],
        compiler_params=params(),
        name="split",
    )(both, after)


def body(object_field, probe_modes, measured, positions):
    strip, mode = lax.axis_index("strip"), lax.axis_index("mode")
    core, j = strip % 2, strip // 2
    z, w = mode // 2, mode % 2
    i = jnp.where(j % 2 == 0, z, 3 - z)
    pair = 4 * j + i
    last = (pair == 31).astype(jnp.int32)
    initial = (pair == 0).astype(jnp.int32)
    fwd, inv = tables()
    fwd = [jnp.asarray(t) for t in fwd]
    inv = [jnp.asarray(t) for t in inv]
    shuffle = jnp.asarray(shuffle_table())

    window = jnp.where(i % 2 == 0, 1 + w, 3 * w)
    ids = jnp.stack([i, core, w, last, initial, window, core, core]).astype(jnp.int32)

    places = positions[0]
    top = pack_call(ring_pack_kernel, HALF + 8, object_field, places, [], "ring_pack")
    ring = send(top, RING)
    own, real, imag, mine = take_call(ids, probe_modes, measured, top)
    up, down = send(own, Z_UP), send(own, Z_DOWN)
    side = send(real, Y_UP), send(imag, Y_DOWN)
    opposite, up_side, down_side = send(up, Z_UP), send(up, Y_UP), send(down, Y_DOWN)

    pack = pack_call(core_pack_kernel, SIDE + HALF + 16, object_field, places, [ring, up, down, *side], "core_pack")
    patch, pattern, facts = pl.pallas_call(
        prepare_kernel,
        in_specs=[SMEM] * 2 + [VMEM] * 6,
        out_specs=[VMEM] * 2 + [SMEM],
        out_shape=[
            jax.ShapeDtypeStruct((2, SIDE, SIDE), f32),
            jax.ShapeDtypeStruct((SIDE, SIDE), f32),
            jax.ShapeDtypeStruct((9,), jnp.int32),
        ],
        scratch_shapes=[pltpu.VMEM((2, 640, WIDTH), f32)],
        compiler_params=params(),
        name="prepare",
    )(ids, places, ring, pack, send(pack, SWAP_CORE), mine, send(mine, SWAP_CORE), shuffle)

    carried = first_call(0, 4, 2, patch, fwd, [*side, own, up, down], [])
    real, imag = split_call(opposite, carried[2])
    opposite_side = send(real, Y_UP), send(imag, Y_DOWN)
    carried = first_call(4, 7, 0, patch, fwd, [up_side, down_side, opposite], carried)
    far, probe, power = first_call(7, 8, 2, patch, fwd, opposite_side, carried)
    base = squares = step = None
    bands, totals = [], []
    for iteration in range(ITERS):
        other = send(power, SWAP_CORE)
        if iteration == 0:
            keep, give = gradient_call(facts, None, None, power, other, pattern, probe, far, None, inv)
            base = power + other
        else:
            keep, give, far, base = gradient_call(
                facts, squares, base, power, other, pattern, probe, far, step, inv
            )
            totals.append(squares)
        final = iteration + 1 == ITERS
        if final:
            stacked = jnp.concatenate(totals, axis=0)
            stacked = stacked + send(stacked, SWAP_CORE)
        half = keep + send(give, SWAP_CORE)
        band, squares = merge_call(
            facts,
            half,
            send(half, BAND_A),
            send(half, BAND_B),
            send(half, BAND_C),
            [stacked] if final else [],
            bands if final else [],
        )
        bands.append(band)
        partner = send(band, SWAP_CORE)
        if final:
            squares = squares + send(squares, SWAP_CORE)
            got_one = send(band, FINAL_ONE)
        carried = None
        for stage, route in enumerate(LAST_DOUBLING if final else DOUBLING):
            arrived = send(squares, route)
            if not final and stage in PIECES:
                begin, end = PIECES[stage]
                carried = advance_call(begin, end, facts, band, partner, probe, far, fwd, squares, carried)
                arrived = arrived + carried[3]
            squares = squares + arrived
            if final and stage == 0:
                got_two = send(choose_call(facts, band, partner, squares), FINAL_TWO)
        if not final:
            _, step, power, _ = carried
    return finish_call(facts, squares, object_field, band, partner, got_one, got_two)


PIECES = {1: (0, 5), 2: (5, 7), 3: (7, 8)}


def solution(mesh):
    return jax.shard_map(
        body,
        mesh=mesh,
        in_specs=(
            P(None, "strip", None),
            P(None, "mode", None, None),
            P("strip", None, None, None),
            P("strip", None, None),
        ),
        out_specs=P(None, "strip", None),
        check_vma=False,
    )
```

```python
import functools

import jax
import jax.numpy as jnp
import numpy as np
from jax import lax
from jax.experimental import pallas as pl
from jax.experimental.pallas import tpu as pltpu
from jax.sharding import PartitionSpec as P

ITERS = 3
SIDE = 256
HALF = 128
WIDTH = 384
OWN_MODES = 8
REGULARIZER = 0.1
STEP_SCALE = 0.3
EPSILON = 1e-06
CELLS = 4096 * 384
AXES = ("strip", "mode")
f32, bf16 = jnp.float32, jnp.bfloat16


def place(index):
    strip, mode = divmod(index, 8)
    core, j = strip % 2, strip // 2
    z, w = divmod(mode, 2)
    i = z if j % 2 == 0 else 3 - z
    return 4 * j + i, w, core


def device_of(pair, w, core):
    j, i = divmod(pair % 32, 4)
    z = i if j % 2 == 0 else 3 - i
    return (2 * j + core) * 8 + 2 * z + w


def route_pairs(move):
    return [(d, device_of(*move(*place(d)))) for d in range(128)]


def route_grid(move):
    route = []
    for d in range(128):
        strip, mode = divmod(d, 8)
        core, x, y_hi = strip % 2, strip // 2 % 4, strip // 8
        z, y_lo = divmod(mode, 2)
        y, x, z = move(2 * y_hi + y_lo, x, z)
        y, x, z = y % 4, x % 4, z % 4
        route.append((d, (((y // 2) * 4 + x) * 2 + core) * 8 + 2 * z + y % 2))
    return route


SWAP_CORE = route_pairs(lambda p, w, c: (p, w, 1 - c))
BAND_A = route_pairs(lambda p, w, c: (p, 1 - w, c))
BAND_B = route_pairs(lambda p, w, c: (p + 2 * c - 1, w, 1 - c))
BAND_C = route_pairs(lambda p, w, c: (p + 2 * c - 1, 1 - w, 1 - c))
Z_UP = route_grid(lambda y, x, z: (y, x, z + 1))
Z_DOWN = route_grid(lambda y, x, z: (y, x, z - 1))
Y_UP = route_grid(lambda y, x, z: (y + 1, x, z))
Y_DOWN = route_grid(lambda y, x, z: (y - 1, x, z))
DOUBLING = [
    route_grid(lambda y, x, z: (y, x, z ^ 1)),
    route_grid(lambda y, x, z: (y, x ^ 1, z)),
    route_grid(lambda y, x, z: (y ^ 2, x, z)),
    route_grid(lambda y, x, z: (y, x ^ 2, z)),
    route_grid(lambda y, x, z: (y, x, z ^ 2)),
]

LAST_DOUBLING = [DOUBLING[k] for k in (1, 2, 3, 0, 4)]


def ring_route():
    route = []
    for j in range(8):
        for mode in range(8):
            low, high = (2 * j + 1) * 8 + mode, (2 * ((j + 1) % 8)) * 8 + mode
            route += [(low, high), (high, low)]
    return route


RING = ring_route()


def final_routes():
    one, two = [], []
    for j in range(8):
        for w in range(2):

            def at(i, c):
                return device_of(4 * j + i, w, c)

            one += [
                (at(0, 0), at(1, 0)),
                (at(1, 0), at(2, 0)),
                (at(0, 1), at(3, 0)),
                (at(2, 1), at(1, 1)),
                (at(2, 0), at(3, 1)),
                (at(1, 1), at(0, 1)),
            ]
            two += [(at(0, 0), at(2, 0)), (at(0, 1), at(3, 0)), (at(3, 0), at(0, 1))]
    return one, two


FINAL_ONE, FINAL_TWO = final_routes()


def send(value, route):
    return lax.ppermute(value, AXES, route)


def table(parity):
    n = np.arange(HALF)
    turns = (n[:, None] * (2 * n[None, :] + parity)) % SIDE
    angle = -2.0 * np.pi * turns / SIDE
    real, imag = np.cos(angle) / 16.0, np.sin(angle) / 16.0
    return np.block([[real, imag], [-imag, real]])


def tables():
    right, left = [], []
    for parity in range(2):
        t = table(parity)
        high = t.astype(np.float32).astype(jnp.bfloat16)
        low = (t - high.astype(np.float64)).astype(np.float32).astype(jnp.bfloat16)
        right.append(np.concatenate([high, high, low], axis=0))
        left.append(np.concatenate([high, high, low], axis=1))
    turned_right = [np.concatenate([r[:256].T, r[:256].T, r[512:].T], axis=0) for r in right]
    turned_left = [np.concatenate([r[:256].T, r[:256].T, r[512:].T], axis=1) for r in right]
    forward = (np.stack(right), np.stack(turned_left))
    inverse = (np.stack(left), np.stack(turned_right))
    return forward, inverse


def shuffle_table():
    rows = np.arange(SIDE)
    take = 2 * (rows % HALF) + rows // HALF
    return (take[:, None] == np.arange(SIDE)[None, :]).astype(jnp.bfloat16)


def halves(x):
    high = x.astype(bf16)
    low = (x - high.astype(f32)).astype(bf16)
    return high, low


def times_right(x, tab):
    high, low = halves(x)
    return jnp.dot(jnp.concatenate([high, low, high], axis=1), tab, preferred_element_type=f32)


def times_left(tab, x):
    high, low = halves(x)
    return jnp.dot(tab, jnp.concatenate([high, low, high], axis=0), preferred_element_type=f32)


def forward_transform(real, imag, cols, rows):
    stage = []
    for sign in (1.0, -1.0):
        if sign > 0:
            r, i = real[:, :HALF] + real[:, HALF:], imag[:, :HALF] + imag[:, HALF:]
        else:
            r, i = real[:, :HALF] - real[:, HALF:], imag[:, :HALF] - imag[:, HALF:]
        stage.append(times_right(jnp.concatenate([r, i], axis=1), cols[0 if sign > 0 else 1]))
    even, odd = stage
    top = [even[:HALF], odd[:HALF]]
    bottom = [even[HALF:], odd[HALF:]]
    out = []
    for parity in range(2):
        if parity == 0:
            mixed = [t + b for t, b in zip(top, bottom)]
        else:
            mixed = [t - b for t, b in zip(top, bottom)]
        block = jnp.concatenate(
            [
                jnp.concatenate([m[:, :HALF] for m in mixed], axis=1),
                jnp.concatenate([m[:, HALF:] for m in mixed], axis=1),
            ],
            axis=0,
        )
        out.append(times_left(rows[parity], block))
    return out


def inverse_transform(far_even, far_odd, rows, cols):
    b0 = times_left(rows[0], far_even)
    b1 = times_left(rows[1], far_odd)
    plus, minus = b0 + b1, b0 - b1
    c = []
    for q in range(2):
        lanes = slice(q * HALF, (q + 1) * HALF)
        real = jnp.concatenate([plus[:HALF, lanes], minus[:HALF, lanes]], axis=0)
        imag = jnp.concatenate([plus[HALF:, lanes], minus[HALF:, lanes]], axis=0)
        c.append(times_right(jnp.concatenate([real, imag], axis=1), cols[q]))
    real = jnp.concatenate([c[0][:, :HALF] + c[1][:, :HALF], c[0][:, :HALF] - c[1][:, :HALF]], axis=1)
    imag = jnp.concatenate([c[0][:, HALF:] + c[1][:, HALF:], c[0][:, HALF:] - c[1][:, HALF:]], axis=1)
    return real, imag


def cut_columns(x, column):
    return pltpu.roll(x, lax.rem(WIDTH - column, WIDTH), 1)[:, :SIDE]


VMEM = pl.BlockSpec(memory_space=pltpu.VMEM)
SMEM = pl.BlockSpec(memory_space=pltpu.SMEM)
ANY = pl.BlockSpec(memory_space=pl.ANY)
HBM = pl.BlockSpec(memory_space=pltpu.HBM)


def params(mebibytes=12):
    return pltpu.CompilerParams(vmem_limit_bytes=mebibytes * 1024 * 1024)


def copy_all(pairs, sems):
    copies = [pltpu.make_async_copy(source, target, sems.at[k]) for k, (source, target) in enumerate(pairs)]
    for copy in copies:
        copy.start()
    return copies


def write_columns(places_ref, out_ref, row):
    for k in range(4):
        column = places_ref[0, k, 1].astype(f32)
        out_ref[0, row + k : row + k + 1] = jnp.full((1, WIDTH), column, f32)
        out_ref[1, row + k : row + k + 1] = jnp.full((1, WIDTH), column, f32)
    out_ref[:, row + 4 : row + 8] = jnp.zeros((2, 4, WIDTH), f32)


def ring_pack_kernel(field_ref, places_ref, *refs):
    out_ref, sems = refs[-2:]
    copies = copy_all([(field_ref.at[:, pl.ds(0, HALF)], out_ref.at[:, pl.ds(0, HALF)])], sems)
    write_columns(places_ref, out_ref, HALF)
    for copy in copies:
        copy.wait()


def core_pack_kernel(field_ref, places_ref, ring_ref, *refs):
    out_ref, sems = refs[-2:]
    copies = copy_all(
        [(field_ref, out_ref.at[:, pl.ds(0, SIDE)]), (ring_ref, out_ref.at[:, pl.ds(SIDE, HALF + 8)])], sems
    )
    write_columns(places_ref, out_ref, SIDE + HALF + 8)
    for copy in copies:
        copy.wait()


def pack_call(kernel, rows, field, places, others, name):
    return pl.pallas_call(
        kernel,
        in_specs=[HBM, SMEM] + [ANY] * len(others),
        out_specs=VMEM,
        out_shape=jax.ShapeDtypeStruct((2, rows, WIDTH), f32),
        scratch_shapes=[pltpu.SemaphoreType.DMA((2,))],
        compiler_params=params(),
        name=name,
    )(field, places, *others)


def prepare_kernel(ids_ref, places_ref, ring_ref, mine_pack_ref, pack_ref, mine_ref, other_ref, shuffle_ref,
                   patch_ref, measured_ref, facts_ref, tall):
    i, core, w, last = ids_ref[0], ids_ref[1], ids_ref[2], ids_ref[3]

    def listed(ref, row):
        return [jnp.max(ref[0, row + k : row + k + 1, 0:128]).astype(jnp.int32) for k in range(4)]

    partner_columns = listed(pack_ref, SIDE + HALF + 8)
    ring_columns = listed(ring_ref, HALF)

    def pick(values, k):
        return jnp.where(k == 0, values[0], jnp.where(k == 1, values[1], jnp.where(k == 2, values[2], values[3])))

    def column(i, w):
        k = jnp.where(lax.rem(i + 4, 2) == 0, 1 + w, 3 * w)
        block = jnp.where(i < 2, 0, 1)
        near = jnp.where(block == core, places_ref[0, k, 1], pick(partner_columns, k))
        return jnp.where((i < 0) | (i > 3), pick(ring_columns, k), near)

    other = i + 2 * core - 1
    own_column = column(i, w)
    facts_ref[0] = i
    facts_ref[1] = core
    facts_ref[2] = last
    facts_ref[3] = own_column
    facts_ref[4] = column(i, 1 - w)
    facts_ref[5] = column(other, w)
    facts_ref[6] = column(other, 1 - w)
    facts_ref[7] = 0
    facts_ref[8] = ids_ref[4]
    for part in range(2):
        own, partner = mine_pack_ref[part, 0:SIDE], pack_ref[part, 0:SIDE]
        tall[part, 0:256] = jnp.where(core == 0, own, partner)
        tall[part, 256:512] = jnp.where(core == 0, partner, own)
        below = jnp.where(core == 0, pack_ref[part, SIDE : SIDE + HALF], ring_ref[part, 0:HALF])
        tall[part, 512:640] = jnp.where(last == 1, jnp.zeros_like(below), below)
        rows = tall[part, pl.ds(pl.multiple_of(i * HALF, HALF), SIDE), :]
        patch_ref[part] = cut_columns(rows, own_column)
    block = jnp.where(i < 2, 0, 1)
    window = jnp.where(block == core, mine_ref[...], other_ref[...])
    shuffle = shuffle_ref[...]
    h0 = window.astype(bf16)
    rest = window - h0.astype(f32)
    h1 = rest.astype(bf16)
    h2 = (rest - h1.astype(f32)).astype(bf16)
    moved = []
    for piece in (h0, h1, h2):
        rows = jnp.dot(shuffle, piece, preferred_element_type=f32).astype(bf16)
        moved.append(lax.dot_general(rows, shuffle, (((1,), (1,)), ((), ())), preferred_element_type=f32))
    measured_ref[...] = moved[0] + moved[1] + moved[2]


def power_of(far):
    return far[:HALF] * far[:HALF] + far[HALF:] * far[HALF:]


def first_kernel(patch_ref, cols_ref, rows_ref, *refs, begin, end, planes):
    far_ref, probe_ref, power_ref, sems = refs[-4:]
    pairs, waits = [], []
    for m in range(begin, end):
        if m - begin < planes // 2:
            k = 2 * (m - begin)
            waits.append((len(pairs), len(pairs) + 1))
            pairs += [(refs[k], probe_ref.at[m, 0]), (refs[k + 1], probe_ref.at[m, 1])]
        else:
            waits.append((len(pairs),))
            pairs.append((refs[planes + m - begin - planes // 2], probe_ref.at[m]))
    copies = copy_all(pairs, sems)
    if begin > 0:
        power_ref[...] = refs[planes // 2 + end - begin + 2][...]
    xr, xi = patch_ref[0], patch_ref[1]
    for m in range(begin, end):
        for k in waits[m - begin]:
            copies[k].wait()
        pr, pi = probe_ref[m, 0], probe_ref[m, 1]
        far = forward_transform(pr * xr - pi * xi, pr * xi + pi * xr, cols_ref, rows_ref)
        for parity in range(2):
            far_ref[m, parity] = far[parity]
            power = power_of(far[parity])
            power_ref[parity] = power if m == 0 else power_ref[parity] + power


FULL = jax.ShapeDtypeStruct((OWN_MODES, 2, SIDE, SIDE), f32)


def first_call(begin, end, planes, patch, fwd, arrays, carried):
    args = [patch, *fwd, *arrays]
    in_specs = [VMEM] * 3 + [ANY] * len(arrays)
    aliases = {}
    if carried:
        aliases = {len(args) + k: k for k in range(2)}
        args += carried
        in_specs += [VMEM] * 3
    return pl.pallas_call(
        functools.partial(first_kernel, begin=begin, end=end, planes=planes),
        in_specs=in_specs,
        out_specs=[VMEM] * 3,
        out_shape=[FULL, FULL, jax.ShapeDtypeStruct((2, HALF, SIDE), f32)],
        input_output_aliases=aliases,
        scratch_shapes=[pltpu.SemaphoreType.DMA((8,))],
        compiler_params=params(),
        cost_estimate=pl.CostEstimate(flops=800_000_000 * (end - begin), bytes_accessed=3_000_000, transcendentals=0),
        name="first_far",
    )(*args)


def advance_kernel(*refs, begin, end, first):
    if first:
        facts_ref, mine_ref, other_ref, probe_ref, far_ref, cols_ref, rows_ref, _, patch, step_ref, powers_ref, token_ref = refs
        core, last, column = facts_ref[1], facts_ref[2], facts_ref[3]
        for part in range(2):
            mine, other = mine_ref[part], other_ref[part]
            top = jnp.where(core == 0, mine, other)
            bottom = jnp.where(core == 0, other, mine)
            bottom = jnp.where(last == 1, jnp.zeros_like(bottom), bottom)
            patch[part, 0:HALF] = cut_columns(top, column)
            patch[part, HALF:] = cut_columns(bottom, column)
        powers_ref[...] = jnp.zeros_like(powers_ref)
    else:
        patch, probe_ref, far_ref, cols_ref, rows_ref, _, _, powers_in_ref, step_ref, powers_ref, token_ref = refs
        powers_ref[...] = powers_in_ref[...]
    token_ref[...] = jnp.zeros_like(token_ref)

    for m in range(begin, end):
        pr, pi = probe_ref[m, 0], probe_ref[m, 1]
        xr, xi = patch[0], patch[1]
        step = forward_transform(pr * xr - pi * xi, pr * xi + pi * xr, cols_ref, rows_ref)
        for parity in range(2):
            step_ref[m, parity] = step[parity]
            far = far_ref[m, parity]
            cross = far * step[parity]
            powers_ref[0, parity] += cross[:HALF] + cross[HALF:]
            powers_ref[1, parity] += power_of(step[parity])


UNROLL = 2
SMALL = jax.ShapeDtypeStruct((8, 128), f32)


def advance_call(begin, end, facts, mine, other, probe, far, fwd, after, carried):
    powers = jax.ShapeDtypeStruct((2, 2, HALF, SIDE), f32)
    first = carried is None
    aliases = {}
    if first:
        args = [facts, mine, other, probe, far, *fwd, after]
        in_specs = [SMEM] + [VMEM] * 6 + [ANY]
        out_shape = [jax.ShapeDtypeStruct((2, SIDE, SIDE), f32), FULL, powers, SMALL]
    else:
        args = [carried[0], probe, far, *fwd, after, carried[1], carried[2]]
        in_specs = [VMEM] * 5 + [ANY] + [VMEM] * 2
        out_shape = [FULL, powers, SMALL]
        aliases = {6: 0, 7: 1}
    out = pl.pallas_call(
        functools.partial(advance_kernel, begin=begin, end=end, first=first),
        in_specs=in_specs,
        out_specs=[VMEM] * len(out_shape),
        out_shape=out_shape,
        input_output_aliases=aliases,
        compiler_params=params(),
        cost_estimate=pl.CostEstimate(flops=800_000_000 * (end - begin), bytes_accessed=3_000_000, transcendentals=0),
        name="far_step",
    )(*args)
    return out if first else [carried[0], *out]


def step_factor(squares, times=1):
    square_sum = jnp.sum(jnp.sum(squares, axis=0, keepdims=True), axis=1, keepdims=True)
    return STEP_SCALE / jnp.sqrt(square_sum / (times * CELLS) + EPSILON)


def gradient_kernel(*refs, first):
    if first:
        facts_ref, power_ref, other_ref, measured_ref, probe_ref, far_ref, rows_ref, cols_ref, keep_ref, give_ref, change, total = refs
    else:
        (facts_ref, squares_ref, base_ref, power_ref, other_ref, measured_ref, probe_ref, far_ref, step_ref, rows_ref, cols_ref,
         keep_ref, give_ref, far_out_ref, base_out_ref, factor_ref, change, total) = refs
        factor_ref[...] = jnp.broadcast_to(step_factor(squares_ref[...]), (8, SIDE))
        factor = factor_ref[0:1]
    for parity in range(2):
        rows = slice(parity * HALF, (parity + 1) * HALF)
        if first:
            power = power_ref[parity] + other_ref[parity]
        else:
            cross = power_ref[0, parity] + other_ref[0, parity]
            square = power_ref[1, parity] + other_ref[1, parity]
            power = jnp.maximum(base_ref[parity] + factor * (2.0 * cross + factor * square), 0.0)
            base_out_ref[parity] = power
        ratio = (measured_ref[rows] + REGULARIZER) / (power + REGULARIZER)
        change[parity] = jnp.sqrt(ratio) - 1.0
    total[...] = jnp.zeros_like(total)

    def one(m, carry):
        shifted = []
        for parity in range(2):
            far = far_ref[m, parity]
            if not first:
                far = far + factor_ref[0:1] * step_ref[m, parity]
                far_out_ref[m, parity] = far
            c = change[parity]
            shifted.append(jnp.concatenate([far[:HALF] * c, far[HALF:] * c], axis=0))
        dr, di = inverse_transform(shifted[0], shifted[1], rows_ref, cols_ref)
        pr, pi = probe_ref[m, 0], probe_ref[m, 1]
        total[0] += pr * dr + pi * di
        total[1] += pr * di - pi * dr
        return carry

    lax.fori_loop(0, OWN_MODES, one, 0, unroll=UNROLL)
    core = facts_ref[1]
    keep_ref[...] = total[:, pl.ds(pl.multiple_of(core * HALF, HALF), HALF), :]
    give_ref[...] = total[:, pl.ds(pl.multiple_of((1 - core) * HALF, HALF), HALF), :]


def gradient_call(facts, squares, base, power, other, measured, probe, far, step, inv):
    first = squares is None
    half = jax.ShapeDtypeStruct((2, HALF, SIDE), f32)
    aliases = {}
    if first:
        args = [facts, power, other, measured, probe, far, *inv]
        out_shape = [half, half]
    else:
        args = [facts, squares, base, power, other, measured, probe, far, step, *inv]
        out_shape = [half, half, FULL, half]
        aliases = {7: 2, 2: 3}
    return pl.pallas_call(
        functools.partial(gradient_kernel, first=first),
        in_specs=[SMEM] + [VMEM] * (len(args) - 1),
        out_specs=[VMEM] * len(out_shape),
        out_shape=out_shape,
        input_output_aliases=aliases,
        scratch_shapes=[pltpu.VMEM((8, SIDE), f32)] * (not first)
        + [pltpu.VMEM((2, HALF, SIDE), f32), pltpu.VMEM((2, SIDE, SIDE), f32)],
        compiler_params=params(),
        cost_estimate=pl.CostEstimate(flops=3_400_000_000, bytes_accessed=17_000_000, transcendentals=65536),
        name="window_gradient",
    )(*args)


def merge_kernel(facts_ref, own_ref, a_ref, b_ref, c_ref, *refs, earlier):
    band_ref, square_ref = refs[-2:]
    core, last, initial = facts_ref[1], facts_ref[2], facts_ref[8]

    def wide(x, column):
        x = jnp.concatenate([x, jnp.zeros((HALF, WIDTH - SIDE), f32)], axis=1)
        return pltpu.roll(x, column, 1)

    drop_own = (last == 1) & (core == 1)
    drop_other = (initial == 1) & (core == 0)
    squares = jnp.zeros((8, 128), f32)
    for part in range(2):
        own = wide(own_ref[part], facts_ref[3]) + wide(a_ref[part], facts_ref[4])
        other = wide(b_ref[part], facts_ref[5]) + wide(c_ref[part], facts_ref[6])
        own = jnp.where(drop_own, jnp.zeros_like(own), own)
        other = jnp.where(drop_other, jnp.zeros_like(other), other)
        band = own + other
        band_ref[part] = band
        sq = (band * band).reshape(HALF // 8, 8, WIDTH).sum(axis=0)
        squares = squares + sq[:, 0:128] + sq[:, 128:256] + sq[:, 256:384]
        if earlier:
            totals, bands = refs[0], refs[1 : 1 + earlier]
            factors = [step_factor(totals[8 * k : 8 * k + 8], 2) for k in range(earlier)]
            band_ref[2 + part] = sum(f * g[part] for f, g in zip(factors, bands))
    square_ref[...] = squares


def merge_call(facts, own, a, b, c, totals, bands):
    args = [facts, own, a, b, c, *totals, *bands]
    parts = 4 if bands else 2
    return pl.pallas_call(
        functools.partial(merge_kernel, earlier=len(bands)),
        in_specs=[SMEM] + [VMEM] * (len(args) - 1),
        out_specs=[VMEM, VMEM],
        out_shape=[jax.ShapeDtypeStruct((parts, HALF, WIDTH), f32), SMALL],
        compiler_params=params(),
        cost_estimate=pl.CostEstimate(flops=1_000_000, bytes_accessed=2_000_000, transcendentals=0),
        name="band_sum",
    )(*args)


def choose_kernel(facts_ref, own_ref, partner_ref, _, out_ref):
    core = facts_ref[1]

    @pl.when(core == 0)
    def _():
        out_ref[...] = own_ref[...]

    @pl.when(core == 1)
    def _():
        out_ref[...] = partner_ref[...]


def choose_call(facts, own, partner, after):
    return pl.pallas_call(
        choose_kernel,
        in_specs=[SMEM, VMEM, VMEM, ANY],
        out_specs=VMEM,
        out_shape=jax.ShapeDtypeStruct((4, HALF, WIDTH), f32),
        compiler_params=params(),
        name="choose",
    )(facts, own, partner, after)


UPPER = ((0, 2, 3, 3), (2, 0, 1, 2))
LOWER = ((1, 0, 2, 2), (3, 2, 0, 1))


def finish_kernel(facts_ref, squares_ref, field_ref, own_ref, partner_ref, one_ref, two_ref, out_ref):
    i, core = facts_ref[0], facts_ref[1]
    factor = step_factor(squares_ref[...], 2)
    for rows, sources in ((slice(0, HALF), UPPER), (slice(HALF, SIDE), LOWER)):
        for source, ref in enumerate((own_ref, partner_ref, one_ref, two_ref)):
            chosen = [(core == c) & (i == k) for c in range(2) for k in range(4) if sources[c][k] == source]
            here = chosen[0]
            for more in chosen[1:]:
                here = here | more

            @pl.when(here)
            def _():
                for part in range(2):
                    moved = ref[2 + part] + factor * ref[part]
                    out_ref[part, rows] = field_ref[part, rows] + moved


def finish_call(*args):
    return pl.pallas_call(
        finish_kernel,
        in_specs=[SMEM] + [VMEM] * 6,
        out_specs=VMEM,
        out_shape=jax.ShapeDtypeStruct((2, SIDE, WIDTH), f32),
        compiler_params=params(),
        name="finish",
    )(*args)


def take_kernel(ids_ref, probe_ref, measured_ref, _, own_ref, real_ref, imag_ref, mine_ref, sems):
    core, window = ids_ref[1], ids_ref[5]
    copies = copy_all(
        [
            (probe_ref.at[0, core], own_ref.at[0]),
            (probe_ref.at[1, core], own_ref.at[1]),
            (probe_ref.at[0, core], real_ref),
            (probe_ref.at[1, core], imag_ref),
            (measured_ref.at[0, window], mine_ref),
        ],
        sems,
    )
    for copy in copies:
        copy.wait()


def take_call(ids, probe_modes, measured, after):
    return pl.pallas_call(
        take_kernel,
        in_specs=[SMEM, HBM, HBM, SMEM],
        out_specs=[VMEM] * 4,
        out_shape=[jax.ShapeDtypeStruct((2, SIDE, SIDE), f32)] + [jax.ShapeDtypeStruct((SIDE, SIDE), f32)] * 3,
        scratch_shapes=[pltpu.SemaphoreType.DMA((5,))],
        compiler_params=params(),
        name="take",
    )(ids, probe_modes, measured, after)


def split_kernel(both_ref, _, real_ref, imag_ref, sems):
    for copy in copy_all([(both_ref.at[0], real_ref), (both_ref.at[1], imag_ref)], sems):
        copy.wait()


def split_call(both, after):
    plane = jax.ShapeDtypeStruct((SIDE, SIDE), f32)
    return pl.pallas_call(
        split_kernel,
        in_specs=[ANY, ANY],
        out_specs=[VMEM] * 2,
        out_shape=[plane] * 2,
        scratch_shapes=[pltpu.SemaphoreType.DMA((2,))],
        compiler_params=params(),
        name="split",
    )(both, after)


def body(object_field, probe_modes, measured, positions):
    strip, mode = lax.axis_index("strip"), lax.axis_index("mode")
    core, j = strip % 2, strip // 2
    z, w = mode // 2, mode % 2
    i = jnp.where(j % 2 == 0, z, 3 - z)
    pair = 4 * j + i
    last = (pair == 31).astype(jnp.int32)
    initial = (pair == 0).astype(jnp.int32)
    fwd, inv = tables()
    fwd = [jnp.asarray(t) for t in fwd]
    inv = [jnp.asarray(t) for t in inv]
    shuffle = jnp.asarray(shuffle_table())

    window = jnp.where(i % 2 == 0, 1 + w, 3 * w)
    ids = jnp.stack([i, core, w, last, initial, window, core, core]).astype(jnp.int32)

    places = positions
    top = pack_call(ring_pack_kernel, HALF + 8, object_field, places, [], "ring_pack")
    ring = send(top, RING)
    own, real, imag, mine = take_call(ids, probe_modes, measured, ids)
    up, down = send(own, Z_UP), send(own, Z_DOWN)
    side = send(real, Y_UP), send(imag, Y_DOWN)
    opposite, up_side, down_side = send(up, Z_UP), send(up, Y_UP), send(down, Y_DOWN)

    pack = pack_call(core_pack_kernel, SIDE + HALF + 16, object_field, places, [ring, up, down, *side], "core_pack")
    patch, pattern, facts = pl.pallas_call(
        prepare_kernel,
        in_specs=[SMEM] * 2 + [VMEM] * 6,
        out_specs=[VMEM] * 2 + [SMEM],
        out_shape=[
            jax.ShapeDtypeStruct((2, SIDE, SIDE), f32),
            jax.ShapeDtypeStruct((SIDE, SIDE), f32),
            jax.ShapeDtypeStruct((9,), jnp.int32),
        ],
        scratch_shapes=[pltpu.VMEM((2, 640, WIDTH), f32)],
        compiler_params=params(),
        name="prepare",
    )(ids, places, ring, pack, send(pack, SWAP_CORE), mine, send(mine, SWAP_CORE), shuffle)

    carried = first_call(0, 4, 2, patch, fwd, [*side, own, up, down], [])
    real, imag = split_call(opposite, carried[2])
    opposite_side = send(real, Y_UP), send(imag, Y_DOWN)
    carried = first_call(4, 7, 0, patch, fwd, [up_side, down_side, opposite], carried)
    far, probe, power = first_call(7, 8, 2, patch, fwd, opposite_side, carried)
    base = squares = step = None
    bands, totals = [], []
    for iteration in range(ITERS):
        other = send(power, SWAP_CORE)
        if iteration == 0:
            keep, give = gradient_call(facts, None, None, power, other, pattern, probe, far, None, inv)
            base = power + other
        else:
            keep, give, far, base = gradient_call(
                facts, squares, base, power, other, pattern, probe, far, step, inv
            )
            totals.append(squares)
        final = iteration + 1 == ITERS
        if final:
            stacked = jnp.concatenate(totals, axis=0)
            stacked = stacked + send(stacked, SWAP_CORE)
        half = keep + send(give, SWAP_CORE)
        band, squares = merge_call(
            facts,
            half,
            send(half, BAND_A),
            send(half, BAND_B),
            send(half, BAND_C),
            [stacked] if final else [],
            bands if final else [],
        )
        bands.append(band)
        partner = send(band, SWAP_CORE)
        if final:
            squares = squares + send(squares, SWAP_CORE)
            got_one = send(band, FINAL_ONE)
        carried = None
        for stage, route in enumerate(LAST_DOUBLING):
            arrived = send(squares, route)
            if not final and stage in PIECES:
                begin, end = PIECES[stage]
                carried = advance_call(begin, end, facts, band, partner, probe, far, fwd, squares, carried)
                arrived = arrived + carried[3]
            squares = squares + arrived
            if final and stage == 0:
                got_two = send(choose_call(facts, band, partner, squares), FINAL_TWO)
        if not final:
            _, step, power, _ = carried
    return finish_call(facts, squares, object_field, band, partner, got_one, got_two)


PIECES = {1: (0, 5), 2: (5, 7), 3: (7, 8)}


def solution(mesh):
    return jax.shard_map(
        body,
        mesh=mesh,
        in_specs=(
            P(None, "strip", None),
            P(None, "mode", None, None),
            P("strip", None, None, None),
            P("strip", None, None),
        ),
        out_specs=P(None, "strip", None),
        check_vma=False,
    )
```

```python
import functools

import jax
import jax.numpy as jnp
import numpy as np
from jax import lax
from jax.experimental import pallas as pl
from jax.experimental.pallas import tpu as pltpu
from jax.sharding import PartitionSpec as P

ITERS = 3
SIDE = 256
HALF = 128
WIDTH = 384
OWN_MODES = 8
REGULARIZER = 0.1
STEP_SCALE = 0.3
EPSILON = 1e-06
CELLS = 4096 * 384
AXES = ("strip", "mode")
f32, bf16 = jnp.float32, jnp.bfloat16


def place(index):
    strip, mode = divmod(index, 8)
    core, j = strip % 2, strip // 2
    z, w = divmod(mode, 2)
    i = z if j % 2 == 0 else 3 - z
    return 4 * j + i, w, core


def device_of(pair, w, core):
    j, i = divmod(pair % 32, 4)
    z = i if j % 2 == 0 else 3 - i
    return (2 * j + core) * 8 + 2 * z + w


def route_pairs(move):
    return [(d, device_of(*move(*place(d)))) for d in range(128)]


def route_grid(move):
    route = []
    for d in range(128):
        strip, mode = divmod(d, 8)
        core, x, y_hi = strip % 2, strip // 2 % 4, strip // 8
        z, y_lo = divmod(mode, 2)
        y, x, z = move(2 * y_hi + y_lo, x, z)
        y, x, z = y % 4, x % 4, z % 4
        route.append((d, (((y // 2) * 4 + x) * 2 + core) * 8 + 2 * z + y % 2))
    return route


SWAP_CORE = route_pairs(lambda p, w, c: (p, w, 1 - c))
BAND_A = route_pairs(lambda p, w, c: (p, 1 - w, c))
BAND_B = route_pairs(lambda p, w, c: (p + 2 * c - 1, w, 1 - c))
BAND_C = route_pairs(lambda p, w, c: (p + 2 * c - 1, 1 - w, 1 - c))
Z_UP = route_grid(lambda y, x, z: (y, x, z + 1))
Z_DOWN = route_grid(lambda y, x, z: (y, x, z - 1))
Y_UP = route_grid(lambda y, x, z: (y + 1, x, z))
Y_DOWN = route_grid(lambda y, x, z: (y - 1, x, z))
DOUBLING = [
    route_grid(lambda y, x, z: (y, x, z ^ 1)),
    route_grid(lambda y, x, z: (y, x ^ 1, z)),
    route_grid(lambda y, x, z: (y ^ 2, x, z)),
    route_grid(lambda y, x, z: (y, x ^ 2, z)),
    route_grid(lambda y, x, z: (y, x, z ^ 2)),
]

LAST_DOUBLING = [DOUBLING[k] for k in (1, 2, 3, 0, 4)]


def ring_route():
    route = []
    for j in range(8):
        for mode in range(8):
            low, high = (2 * j + 1) * 8 + mode, (2 * ((j + 1) % 8)) * 8 + mode
            route += [(low, high), (high, low)]
    return route


RING = ring_route()


def final_routes():
    one, two = [], []
    for j in range(8):
        for w in range(2):

            def at(i, c):
                return device_of(4 * j + i, w, c)

            one += [
                (at(0, 0), at(1, 0)),
                (at(1, 0), at(2, 0)),
                (at(0, 1), at(3, 0)),
                (at(2, 1), at(1, 1)),
                (at(2, 0), at(3, 1)),
                (at(1, 1), at(0, 1)),
            ]
            two += [(at(0, 0), at(2, 0)), (at(0, 1), at(3, 0)), (at(3, 0), at(0, 1))]
    return one, two


FINAL_ONE, FINAL_TWO = final_routes()


def send(value, route):
    return lax.ppermute(value, AXES, route)


def table(parity):
    n = np.arange(HALF)
    turns = (n[:, None] * (2 * n[None, :] + parity)) % SIDE
    angle = -2.0 * np.pi * turns / SIDE
    real, imag = np.cos(angle) / 16.0, np.sin(angle) / 16.0
    return np.block([[real, imag], [-imag, real]])


def tables():
    right, left = [], []
    for parity in range(2):
        t = table(parity)
        high = t.astype(np.float32).astype(jnp.bfloat16)
        low = (t - high.astype(np.float64)).astype(np.float32).astype(jnp.bfloat16)
        right.append(np.concatenate([high, high, low], axis=0))
        left.append(np.concatenate([high, high, low], axis=1))
    turned_right = [np.concatenate([r[:256].T, r[:256].T, r[512:].T], axis=0) for r in right]
    turned_left = [np.concatenate([r[:256].T, r[:256].T, r[512:].T], axis=1) for r in right]
    forward = (np.stack(right), np.stack(turned_left))
    inverse = (np.stack(left), np.stack(turned_right))
    return forward, inverse


def shuffle_table():
    rows = np.arange(SIDE)
    take = 2 * (rows % HALF) + rows // HALF
    return (take[:, None] == np.arange(SIDE)[None, :]).astype(jnp.bfloat16)


def halves(x):
    high = x.astype(bf16)
    low = (x - high.astype(f32)).astype(bf16)
    return high, low


def times_right(x, tab):
    high, low = halves(x)
    return jnp.dot(jnp.concatenate([high, low, high], axis=1), tab, preferred_element_type=f32)


def times_left(tab, x):
    high, low = halves(x)
    return jnp.dot(tab, jnp.concatenate([high, low, high], axis=0), preferred_element_type=f32)


def forward_transform(real, imag, cols, rows):
    stage = []
    for sign in (1.0, -1.0):
        if sign > 0:
            r, i = real[:, :HALF] + real[:, HALF:], imag[:, :HALF] + imag[:, HALF:]
        else:
            r, i = real[:, :HALF] - real[:, HALF:], imag[:, :HALF] - imag[:, HALF:]
        stage.append(times_right(jnp.concatenate([r, i], axis=1), cols[0 if sign > 0 else 1]))
    even, odd = stage
    top = [even[:HALF], odd[:HALF]]
    bottom = [even[HALF:], odd[HALF:]]
    out = []
    for parity in range(2):
        if parity == 0:
            mixed = [t + b for t, b in zip(top, bottom)]
        else:
            mixed = [t - b for t, b in zip(top, bottom)]
        block = jnp.concatenate(
            [
                jnp.concatenate([m[:, :HALF] for m in mixed], axis=1),
                jnp.concatenate([m[:, HALF:] for m in mixed], axis=1),
            ],
            axis=0,
        )
        out.append(times_left(rows[parity], block))
    return out


def inverse_transform(far_even, far_odd, rows, cols):
    b0 = times_left(rows[0], far_even)
    b1 = times_left(rows[1], far_odd)
    plus, minus = b0 + b1, b0 - b1
    c = []
    for q in range(2):
        lanes = slice(q * HALF, (q + 1) * HALF)
        real = jnp.concatenate([plus[:HALF, lanes], minus[:HALF, lanes]], axis=0)
        imag = jnp.concatenate([plus[HALF:, lanes], minus[HALF:, lanes]], axis=0)
        c.append(times_right(jnp.concatenate([real, imag], axis=1), cols[q]))
    real = jnp.concatenate([c[0][:, :HALF] + c[1][:, :HALF], c[0][:, :HALF] - c[1][:, :HALF]], axis=1)
    imag = jnp.concatenate([c[0][:, HALF:] + c[1][:, HALF:], c[0][:, HALF:] - c[1][:, HALF:]], axis=1)
    return real, imag


def cut_columns(x, column):
    return pltpu.roll(x, lax.rem(WIDTH - column, WIDTH), 1)[:, :SIDE]


VMEM = pl.BlockSpec(memory_space=pltpu.VMEM)
SMEM = pl.BlockSpec(memory_space=pltpu.SMEM)
ANY = pl.BlockSpec(memory_space=pl.ANY)
HBM = pl.BlockSpec(memory_space=pltpu.HBM)


def params(mebibytes=12):
    return pltpu.CompilerParams(vmem_limit_bytes=mebibytes * 1024 * 1024)


def copy_all(pairs, sems):
    copies = [pltpu.make_async_copy(source, target, sems.at[k]) for k, (source, target) in enumerate(pairs)]
    for copy in copies:
        copy.start()
    return copies


def write_columns(places_ref, out_ref, row):
    for k in range(4):
        column = places_ref[0, k, 1].astype(f32)
        out_ref[0, row + k : row + k + 1] = jnp.full((1, WIDTH), column, f32)
        out_ref[1, row + k : row + k + 1] = jnp.full((1, WIDTH), column, f32)
    out_ref[:, row + 4 : row + 8] = jnp.zeros((2, 4, WIDTH), f32)


def ring_pack_kernel(field_ref, places_ref, *refs):
    out_ref, sems = refs[-2:]
    copies = copy_all([(field_ref.at[:, pl.ds(0, HALF)], out_ref.at[:, pl.ds(0, HALF)])], sems)
    write_columns(places_ref, out_ref, HALF)
    for copy in copies:
        copy.wait()


def core_pack_kernel(field_ref, places_ref, ring_ref, *refs):
    out_ref, sems = refs[-2:]
    copies = copy_all(
        [(field_ref, out_ref.at[:, pl.ds(0, SIDE)]), (ring_ref, out_ref.at[:, pl.ds(SIDE, HALF + 8)])], sems
    )
    write_columns(places_ref, out_ref, SIDE + HALF + 8)
    for copy in copies:
        copy.wait()


def pack_call(kernel, rows, field, places, others, name):
    return pl.pallas_call(
        kernel,
        in_specs=[HBM, SMEM] + [ANY] * len(others),
        out_specs=VMEM,
        out_shape=jax.ShapeDtypeStruct((2, rows, WIDTH), f32),
        scratch_shapes=[pltpu.SemaphoreType.DMA((2,))],
        compiler_params=params(),
        name=name,
    )(field, places, *others)


def prepare_kernel(ids_ref, places_ref, ring_ref, mine_pack_ref, pack_ref, mine_ref, other_ref, shuffle_ref,
                   patch_ref, measured_ref, facts_ref, tall):
    i, core, w, last = ids_ref[0], ids_ref[1], ids_ref[2], ids_ref[3]

    def listed(ref, row):
        return [jnp.max(ref[0, row + k : row + k + 1, 0:128]).astype(jnp.int32) for k in range(4)]

    partner_columns = listed(pack_ref, SIDE + HALF + 8)
    ring_columns = listed(ring_ref, HALF)

    def pick(values, k):
        return jnp.where(k == 0, values[0], jnp.where(k == 1, values[1], jnp.where(k == 2, values[2], values[3])))

    def column(i, w):
        k = jnp.where(lax.rem(i + 4, 2) == 0, 1 + w, 3 * w)
        block = jnp.where(i < 2, 0, 1)
        near = jnp.where(block == core, places_ref[0, k, 1], pick(partner_columns, k))
        return jnp.where((i < 0) | (i > 3), pick(ring_columns, k), near)

    other = i + 2 * core - 1
    own_column = column(i, w)
    facts_ref[0] = i
    facts_ref[1] = core
    facts_ref[2] = last
    facts_ref[3] = own_column
    facts_ref[4] = column(i, 1 - w)
    facts_ref[5] = column(other, w)
    facts_ref[6] = column(other, 1 - w)
    facts_ref[7] = 0
    facts_ref[8] = ids_ref[4]
    for part in range(2):
        own, partner = mine_pack_ref[part, 0:SIDE], pack_ref[part, 0:SIDE]
        tall[part, 0:256] = jnp.where(core == 0, own, partner)
        tall[part, 256:512] = jnp.where(core == 0, partner, own)
        below = jnp.where(core == 0, pack_ref[part, SIDE : SIDE + HALF], ring_ref[part, 0:HALF])
        tall[part, 512:640] = jnp.where(last == 1, jnp.zeros_like(below), below)
        rows = tall[part, pl.ds(pl.multiple_of(i * HALF, HALF), SIDE), :]
        patch_ref[part] = cut_columns(rows, own_column)
    block = jnp.where(i < 2, 0, 1)
    window = jnp.where(block == core, mine_ref[...], other_ref[...])
    shuffle = shuffle_ref[...]
    h0 = window.astype(bf16)
    rest = window - h0.astype(f32)
    h1 = rest.astype(bf16)
    h2 = (rest - h1.astype(f32)).astype(bf16)
    moved = []
    for piece in (h0, h1, h2):
        rows = jnp.dot(shuffle, piece, preferred_element_type=f32).astype(bf16)
        moved.append(lax.dot_general(rows, shuffle, (((1,), (1,)), ((), ())), preferred_element_type=f32))
    measured_ref[...] = moved[0] + moved[1] + moved[2]


def power_of(far):
    return far[:HALF] * far[:HALF] + far[HALF:] * far[HALF:]


def first_kernel(patch_ref, cols_ref, rows_ref, *refs, begin, end, planes):
    far_ref, probe_ref, power_ref, sems = refs[-4:]
    pairs, waits = [], []
    for m in range(begin, end):
        if m - begin < planes // 2:
            k = 2 * (m - begin)
            waits.append((len(pairs), len(pairs) + 1))
            pairs += [(refs[k], probe_ref.at[m, 0]), (refs[k + 1], probe_ref.at[m, 1])]
        else:
            waits.append((len(pairs),))
            pairs.append((refs[planes + m - begin - planes // 2], probe_ref.at[m]))
    copies = copy_all(pairs, sems)
    if begin > 0:
        power_ref[...] = refs[planes // 2 + end - begin + 2][...]
    xr, xi = patch_ref[0], patch_ref[1]
    for m in range(begin, end):
        for k in waits[m - begin]:
            copies[k].wait()
        pr, pi = probe_ref[m, 0], probe_ref[m, 1]
        far = forward_transform(pr * xr - pi * xi, pr * xi + pi * xr, cols_ref, rows_ref)
        for parity in range(2):
            far_ref[m, parity] = far[parity]
            power = power_of(far[parity])
            power_ref[parity] = power if m == 0 else power_ref[parity] + power


FULL = jax.ShapeDtypeStruct((OWN_MODES, 2, SIDE, SIDE), f32)


def first_call(begin, end, planes, patch, fwd, arrays, carried):
    args = [patch, *fwd, *arrays]
    in_specs = [VMEM] * 3 + [ANY] * len(arrays)
    aliases = {}
    if carried:
        aliases = {len(args) + k: k for k in range(2)}
        args += carried
        in_specs += [VMEM] * 3
    return pl.pallas_call(
        functools.partial(first_kernel, begin=begin, end=end, planes=planes),
        in_specs=in_specs,
        out_specs=[VMEM] * 3,
        out_shape=[FULL, FULL, jax.ShapeDtypeStruct((2, HALF, SIDE), f32)],
        input_output_aliases=aliases,
        scratch_shapes=[pltpu.SemaphoreType.DMA((8,))],
        compiler_params=params(),
        cost_estimate=pl.CostEstimate(flops=800_000_000 * (end - begin), bytes_accessed=3_000_000, transcendentals=0),
        name="first_far",
    )(*args)


def advance_kernel(*refs, begin, end, first):
    if first:
        facts_ref, mine_ref, other_ref, probe_ref, far_ref, cols_ref, rows_ref, _, patch, step_ref, powers_ref, token_ref = refs
        core, last, column = facts_ref[1], facts_ref[2], facts_ref[3]
        for part in range(2):
            mine, other = mine_ref[part], other_ref[part]
            top = jnp.where(core == 0, mine, other)
            bottom = jnp.where(core == 0, other, mine)
            bottom = jnp.where(last == 1, jnp.zeros_like(bottom), bottom)
            patch[part, 0:HALF] = cut_columns(top, column)
            patch[part, HALF:] = cut_columns(bottom, column)
        powers_ref[...] = jnp.zeros_like(powers_ref)
    else:
        patch, probe_ref, far_ref, cols_ref, rows_ref, _, _, powers_in_ref, step_ref, powers_ref, token_ref = refs
        powers_ref[...] = powers_in_ref[...]
    token_ref[...] = jnp.zeros_like(token_ref)

    for m in range(begin, end):
        pr, pi = probe_ref[m, 0], probe_ref[m, 1]
        xr, xi = patch[0], patch[1]
        step = forward_transform(pr * xr - pi * xi, pr * xi + pi * xr, cols_ref, rows_ref)
        for parity in range(2):
            step_ref[m, parity] = step[parity]
            far = far_ref[m, parity]
            cross = far * step[parity]
            powers_ref[0, parity] += cross[:HALF] + cross[HALF:]
            powers_ref[1, parity] += power_of(step[parity])


UNROLL = 4
SMALL = jax.ShapeDtypeStruct((8, 128), f32)


def advance_call(begin, end, facts, mine, other, probe, far, fwd, after, carried):
    powers = jax.ShapeDtypeStruct((2, 2, HALF, SIDE), f32)
    first = carried is None
    aliases = {}
    if first:
        args = [facts, mine, other, probe, far, *fwd, after]
        in_specs = [SMEM] + [VMEM] * 6 + [ANY]
        out_shape = [jax.ShapeDtypeStruct((2, SIDE, SIDE), f32), FULL, powers, SMALL]
    else:
        args = [carried[0], probe, far, *fwd, after, carried[1], carried[2]]
        in_specs = [VMEM] * 5 + [ANY] + [VMEM] * 2
        out_shape = [FULL, powers, SMALL]
        aliases = {6: 0, 7: 1}
    out = pl.pallas_call(
        functools.partial(advance_kernel, begin=begin, end=end, first=first),
        in_specs=in_specs,
        out_specs=[VMEM] * len(out_shape),
        out_shape=out_shape,
        input_output_aliases=aliases,
        compiler_params=params(),
        cost_estimate=pl.CostEstimate(flops=800_000_000 * (end - begin), bytes_accessed=3_000_000, transcendentals=0),
        name="far_step",
    )(*args)
    return out if first else [carried[0], *out]


def step_factor(squares, times=1):
    square_sum = jnp.sum(jnp.sum(squares, axis=0, keepdims=True), axis=1, keepdims=True)
    return STEP_SCALE / jnp.sqrt(square_sum / (times * CELLS) + EPSILON)


def gradient_kernel(*refs, first):
    if first:
        facts_ref, power_ref, other_ref, measured_ref, probe_ref, far_ref, rows_ref, cols_ref, keep_ref, give_ref, change, total = refs
    else:
        (facts_ref, squares_ref, base_ref, power_ref, other_ref, measured_ref, probe_ref, far_ref, step_ref, rows_ref, cols_ref,
         keep_ref, give_ref, far_out_ref, base_out_ref, factor_ref, change, total) = refs
        factor_ref[...] = jnp.broadcast_to(step_factor(squares_ref[...]), (8, SIDE))
        factor = factor_ref[0:1]
    for parity in range(2):
        rows = slice(parity * HALF, (parity + 1) * HALF)
        if first:
            power = power_ref[parity] + other_ref[parity]
        else:
            cross = power_ref[0, parity] + other_ref[0, parity]
            square = power_ref[1, parity] + other_ref[1, parity]
            power = jnp.maximum(base_ref[parity] + factor * (2.0 * cross + factor * square), 0.0)
            base_out_ref[parity] = power
        ratio = (measured_ref[rows] + REGULARIZER) / (power + REGULARIZER)
        change[parity] = jnp.sqrt(ratio) - 1.0
    total[...] = jnp.zeros_like(total)

    def one(m, carry):
        shifted = []
        for parity in range(2):
            far = far_ref[m, parity]
            if not first:
                far = far + factor_ref[0:1] * step_ref[m, parity]
                far_out_ref[m, parity] = far
            c = change[parity]
            shifted.append(jnp.concatenate([far[:HALF] * c, far[HALF:] * c], axis=0))
        dr, di = inverse_transform(shifted[0], shifted[1], rows_ref, cols_ref)
        pr, pi = probe_ref[m, 0], probe_ref[m, 1]
        total[0] += pr * dr + pi * di
        total[1] += pr * di - pi * dr
        return carry

    lax.fori_loop(0, OWN_MODES, one, 0, unroll=UNROLL)
    core = facts_ref[1]
    keep_ref[...] = total[:, pl.ds(pl.multiple_of(core * HALF, HALF), HALF), :]
    give_ref[...] = total[:, pl.ds(pl.multiple_of((1 - core) * HALF, HALF), HALF), :]


def gradient_call(facts, squares, base, power, other, measured, probe, far, step, inv):
    first = squares is None
    half = jax.ShapeDtypeStruct((2, HALF, SIDE), f32)
    aliases = {}
    if first:
        args = [facts, power, other, measured, probe, far, *inv]
        out_shape = [half, half]
    else:
        args = [facts, squares, base, power, other, measured, probe, far, step, *inv]
        out_shape = [half, half, FULL, half]
        aliases = {7: 2, 2: 3}
    return pl.pallas_call(
        functools.partial(gradient_kernel, first=first),
        in_specs=[SMEM] + [VMEM] * (len(args) - 1),
        out_specs=[VMEM] * len(out_shape),
        out_shape=out_shape,
        input_output_aliases=aliases,
        scratch_shapes=[pltpu.VMEM((8, SIDE), f32)] * (not first)
        + [pltpu.VMEM((2, HALF, SIDE), f32), pltpu.VMEM((2, SIDE, SIDE), f32)],
        compiler_params=params(),
        cost_estimate=pl.CostEstimate(flops=3_400_000_000, bytes_accessed=17_000_000, transcendentals=65536),
        name="window_gradient",
    )(*args)


def merge_kernel(facts_ref, own_ref, a_ref, b_ref, c_ref, *refs, earlier):
    band_ref, square_ref = refs[-2:]
    core, last, initial = facts_ref[1], facts_ref[2], facts_ref[8]

    def wide(x, column):
        x = jnp.concatenate([x, jnp.zeros((HALF, WIDTH - SIDE), f32)], axis=1)
        return pltpu.roll(x, column, 1)

    drop_own = (last == 1) & (core == 1)
    drop_other = (initial == 1) & (core == 0)
    squares = jnp.zeros((8, 128), f32)
    for part in range(2):
        own = wide(own_ref[part], facts_ref[3]) + wide(a_ref[part], facts_ref[4])
        other = wide(b_ref[part], facts_ref[5]) + wide(c_ref[part], facts_ref[6])
        own = jnp.where(drop_own, jnp.zeros_like(own), own)
        other = jnp.where(drop_other, jnp.zeros_like(other), other)
        band = own + other
        band_ref[part] = band
        sq = (band * band).reshape(HALF // 8, 8, WIDTH).sum(axis=0)
        squares = squares + sq[:, 0:128] + sq[:, 128:256] + sq[:, 256:384]
        if earlier:
            totals, bands = refs[0], refs[1 : 1 + earlier]
            factors = [step_factor(totals[8 * k : 8 * k + 8], 2) for k in range(earlier)]
            band_ref[2 + part] = sum(f * g[part] for f, g in zip(factors, bands))
    square_ref[...] = squares


def merge_call(facts, own, a, b, c, totals, bands):
    args = [facts, own, a, b, c, *totals, *bands]
    parts = 4 if bands else 2
    return pl.pallas_call(
        functools.partial(merge_kernel, earlier=len(bands)),
        in_specs=[SMEM] + [VMEM] * (len(args) - 1),
        out_specs=[VMEM, VMEM],
        out_shape=[jax.ShapeDtypeStruct((parts, HALF, WIDTH), f32), SMALL],
        compiler_params=params(),
        cost_estimate=pl.CostEstimate(flops=1_000_000, bytes_accessed=2_000_000, transcendentals=0),
        name="band_sum",
    )(*args)


def choose_kernel(facts_ref, own_ref, partner_ref, _, out_ref):
    core = facts_ref[1]

    @pl.when(core == 0)
    def _():
        out_ref[...] = own_ref[...]

    @pl.when(core == 1)
    def _():
        out_ref[...] = partner_ref[...]


def choose_call(facts, own, partner, after):
    return pl.pallas_call(
        choose_kernel,
        in_specs=[SMEM, VMEM, VMEM, ANY],
        out_specs=VMEM,
        out_shape=jax.ShapeDtypeStruct((4, HALF, WIDTH), f32),
        compiler_params=params(),
        name="choose",
    )(facts, own, partner, after)


UPPER = ((0, 2, 3, 3), (2, 0, 1, 2))
LOWER = ((1, 0, 2, 2), (3, 2, 0, 1))


def finish_kernel(facts_ref, squares_ref, field_ref, own_ref, partner_ref, one_ref, two_ref, out_ref):
    i, core = facts_ref[0], facts_ref[1]
    factor = step_factor(squares_ref[...], 2)
    for rows, sources in ((slice(0, HALF), UPPER), (slice(HALF, SIDE), LOWER)):
        for source, ref in enumerate((own_ref, partner_ref, one_ref, two_ref)):
            chosen = [(core == c) & (i == k) for c in range(2) for k in range(4) if sources[c][k] == source]
            here = chosen[0]
            for more in chosen[1:]:
                here = here | more

            @pl.when(here)
            def _():
                for part in range(2):
                    moved = ref[2 + part] + factor * ref[part]
                    out_ref[part, rows] = field_ref[part, rows] + moved


def finish_call(*args):
    return pl.pallas_call(
        finish_kernel,
        in_specs=[SMEM] + [VMEM] * 6,
        out_specs=VMEM,
        out_shape=jax.ShapeDtypeStruct((2, SIDE, WIDTH), f32),
        compiler_params=params(),
        name="finish",
    )(*args)


def take_kernel(ids_ref, probe_ref, measured_ref, _, own_ref, real_ref, imag_ref, mine_ref, sems):
    core, window = ids_ref[1], ids_ref[5]
    copies = copy_all(
        [
            (probe_ref.at[0, core], own_ref.at[0]),
            (probe_ref.at[1, core], own_ref.at[1]),
            (probe_ref.at[0, core], real_ref),
            (probe_ref.at[1, core], imag_ref),
            (measured_ref.at[0, window], mine_ref),
        ],
        sems,
    )
    for copy in copies:
        copy.wait()


def take_call(ids, probe_modes, measured, after):
    return pl.pallas_call(
        take_kernel,
        in_specs=[SMEM, HBM, HBM, SMEM],
        out_specs=[VMEM] * 4,
        out_shape=[jax.ShapeDtypeStruct((2, SIDE, SIDE), f32)] + [jax.ShapeDtypeStruct((SIDE, SIDE), f32)] * 3,
        scratch_shapes=[pltpu.SemaphoreType.DMA((5,))],
        compiler_params=params(),
        name="take",
    )(ids, probe_modes, measured, after)


def split_kernel(both_ref, _, real_ref, imag_ref, sems):
    for copy in copy_all([(both_ref.at[0], real_ref), (both_ref.at[1], imag_ref)], sems):
        copy.wait()


def split_call(both, after):
    plane = jax.ShapeDtypeStruct((SIDE, SIDE), f32)
    return pl.pallas_call(
        split_kernel,
        in_specs=[ANY, ANY],
        out_specs=[VMEM] * 2,
        out_shape=[plane] * 2,
        scratch_shapes=[pltpu.SemaphoreType.DMA((2,))],
        compiler_params=params(),
        name="split",
    )(both, after)


def body(object_field, probe_modes, measured, positions):
    strip, mode = lax.axis_index("strip"), lax.axis_index("mode")
    core, j = strip % 2, strip // 2
    z, w = mode // 2, mode % 2
    i = jnp.where(j % 2 == 0, z, 3 - z)
    pair = 4 * j + i
    last = (pair == 31).astype(jnp.int32)
    initial = (pair == 0).astype(jnp.int32)
    fwd, inv = tables()
    fwd = [jnp.asarray(t) for t in fwd]
    inv = [jnp.asarray(t) for t in inv]
    shuffle = jnp.asarray(shuffle_table())

    window = jnp.where(i % 2 == 0, 1 + w, 3 * w)
    ids = jnp.stack([i, core, w, last, initial, window, core, core]).astype(jnp.int32)

    places = positions
    top = pack_call(ring_pack_kernel, HALF + 8, object_field, places, [], "ring_pack")
    ring = send(top, RING)
    own, real, imag, mine = take_call(ids, probe_modes, measured, ids)
    up, down = send(own, Z_UP), send(own, Z_DOWN)
    side = send(real, Y_UP), send(imag, Y_DOWN)
    opposite, up_side, down_side = send(up, Z_UP), send(up, Y_UP), send(down, Y_DOWN)

    pack = pack_call(core_pack_kernel, SIDE + HALF + 16, object_field, places, [ring, up, down, *side], "core_pack")
    patch, pattern, facts = pl.pallas_call(
        prepare_kernel,
        in_specs=[SMEM] * 2 + [VMEM] * 6,
        out_specs=[VMEM] * 2 + [SMEM],
        out_shape=[
            jax.ShapeDtypeStruct((2, SIDE, SIDE), f32),
            jax.ShapeDtypeStruct((SIDE, SIDE), f32),
            jax.ShapeDtypeStruct((9,), jnp.int32),
        ],
        scratch_shapes=[pltpu.VMEM((2, 640, WIDTH), f32)],
        compiler_params=params(),
        name="prepare",
    )(ids, places, ring, pack, send(pack, SWAP_CORE), mine, send(mine, SWAP_CORE), shuffle)

    carried = first_call(0, 4, 2, patch, fwd, [*side, own, up, down], [])
    real, imag = split_call(opposite, carried[2])
    opposite_side = send(real, Y_UP), send(imag, Y_DOWN)
    carried = first_call(4, 7, 0, patch, fwd, [up_side, down_side, opposite], carried)
    far, probe, power = first_call(7, 8, 2, patch, fwd, opposite_side, carried)
    base = squares = step = None
    bands, totals = [], []
    for iteration in range(ITERS):
        other = send(power, SWAP_CORE)
        if iteration == 0:
            keep, give = gradient_call(facts, None, None, power, other, pattern, probe, far, None, inv)
            base = power + other
        else:
            keep, give, far, base = gradient_call(
                facts, squares, base, power, other, pattern, probe, far, step, inv
            )
            totals.append(squares)
        final = iteration + 1 == ITERS
        if final:
            stacked = jnp.concatenate(totals, axis=0)
            stacked = stacked + send(stacked, SWAP_CORE)
        half = keep + send(give, SWAP_CORE)
        band, squares = merge_call(
            facts,
            half,
            send(half, BAND_A),
            send(half, BAND_B),
            send(half, BAND_C),
            [stacked] if final else [],
            bands if final else [],
        )
        bands.append(band)
        partner = send(band, SWAP_CORE)
        if final:
            squares = squares + send(squares, SWAP_CORE)
            got_one = send(band, FINAL_ONE)
        carried = None
        for stage, route in enumerate(LAST_DOUBLING):
            arrived = send(squares, route)
            if not final and stage in PIECES:
                begin, end = PIECES[stage]
                carried = advance_call(begin, end, facts, band, partner, probe, far, fwd, squares, carried)
                arrived = arrived + carried[3]
            squares = squares + arrived
            if final and stage == 0:
                got_two = send(choose_call(facts, band, partner, squares), FINAL_TWO)
        if not final:
            _, step, power, _ = carried
    return finish_call(facts, squares, object_field, band, partner, got_one, got_two)


PIECES = {1: (0, 5), 2: (5, 7), 3: (7, 8)}


def solution(mesh):
    return jax.shard_map(
        body,
        mesh=mesh,
        in_specs=(
            P(None, "strip", None),
            P(None, "mode", None, None),
            P("strip", None, None, None),
            P("strip", None, None),
        ),
        out_specs=P(None, "strip", None),
        check_vma=False,
    )
```
